768 devices in a mesh: mesh: 48 (over z, y_lo, core), state: 16 (over x, y_hi).
Axes of the slice: x: 4, y: 8 (y_hi: 4, y_lo: 2; y = y_hi * 2 + y_lo), z: 12, core: 2. Of those that a mesh axis runs over, the one named last changes fastest.
Arguments:
- states: bfloat16 [49152, 3072], P('mesh', 'state'), may hold values from -6 to 6
- cell_ham: bfloat16 [96, 512, 512], P('mesh'), may hold values from -0.25 to 0.25
- projectors: bfloat16 [96, 72, 512], P('mesh'), may hold values from -0.15625 to 0.15625
- slot_atom: int32 [96, 4], P('mesh'), may hold values from 0 to 47, as said below
- coupling: float32 [48, 18], replicated, may hold values from 0.3 to 0.5
- occupancy: float32 [3072], P('state'), may hold values from 0.2 to 2
Outputs:
- filtered: bfloat16 [49152, 3072], P('mesh', 'state')
- density: float32 [49152], P(('mesh', 'state'))
The draws below stay inside these ranges and needn't reach their ends.
Inputs may be any that keep to these rules, and one draw needn't show every extreme that they name: `slot_atom`: atom a is owned by partition a; cells k * 2 to (k + 1) * 2 - 1 form partition k. Slot 0 of every cell names an atom of the cell's own partition; other slots may name an atom of any partition.
All inputs are finite; a program needn't handle non-finite values.
Results may differ from the reference program's by a relative error of at most 0.006.
Values may be sent and summed in bfloat16 or wider, within the bound.
No kernel may reach another device: no remote copies, remote signals or barrier semaphores. Data moves between devices by JAX's collectives and lax.ppermute only.
A program may use at most 32 MiB of HBM per device.

```python
import math
import jax
import jax.numpy as jnp
from jax import lax

NODES = 512
FACE = 64
CELLS_DEV = 2
STATE_DEV = 192
NPROJ = 18
SLOTS = 4
ATOMS_DEV = 1
DEGREE = 4
CELLS = 96
NODES_ALL = 49152
NSTATE = 3072
ATOMS = 48
N_STATE = 16


def draw_slot_atom(key, part):
    partitions = CELLS // CELLS_DEV
    key_step, key_inner = jax.random.split(jax.random.fold_in(key, 17))
    cell_ids = jnp.arange(CELLS, dtype=jnp.int32)[:, None]
    slot_ids = jnp.arange(SLOTS, dtype=jnp.int32)[None, :]
    owner = cell_ids // CELLS_DEV
    target = jax.random.randint(key_step, (CELLS, SLOTS), 0, partitions, dtype=jnp.int32)
    far = (owner + partitions // 2) % partitions
    first_cell = cell_ids % CELLS_DEV == 0
    target = jnp.where(first_cell & (slot_ids == 1), far, target)
    target = jnp.where(slot_ids == 0, owner, target)
    inner = jax.random.randint(key_inner, (CELLS, SLOTS), 0, ATOMS_DEV, dtype=jnp.int32)
    first = cell_ids % CELLS_DEV % ATOMS_DEV
    inner = jnp.where(slot_ids == 0, first, inner)
    return (target * ATOMS_DEV + inner).astype(jnp.int32)


def shard_levels(key, extent, pieces, low, top_value):
    def one(dim, blocks):
        steps = jax.random.uniform(jax.random.fold_in(jax.random.fold_in(key, 6), dim), (blocks,), jnp.float32, low / len(pieces), top_value / len(pieces))
        return jnp.repeat(jnp.exp(steps), extent[dim] // blocks).reshape((-1,) + (1,) * (len(extent) - dim - 1))

    gain = one(*pieces[0])
    for cut in pieces[1:]:
        gain = gain * one(*cut)
    return gain


def noise(rng, dims, scale, limit, pieces=(), kind=jnp.bfloat16):
    entries = jax.random.normal(rng, dims, jnp.float32) * scale
    if len(pieces) > 0:
        entries = shard_levels(rng, dims, pieces, -0.22, 0.18) * entries
    return jnp.clip(entries, min=-limit, max=limit).astype(kind)


def setup_inputs(seed: int = 0) -> dict:
    seeds = jax.random.split(jax.random.key(seed), 7)
    return {
        "states": noise(seeds[0], (NODES_ALL, NSTATE), 1.0, 6.0, ((0, 48), (1, 16))),
        "cell_ham": noise(seeds[1], (CELLS, NODES, NODES), NODES ** -0.5, 0.25, ((0, 48),)),
        "projectors": noise(seeds[2], (CELLS, SLOTS * NPROJ, NODES), (NODES * CELLS_DEV * SLOTS // (3 * ATOMS_DEV)) ** -0.5, 0.15625, ((0, 48),)),
        "slot_atom": draw_slot_atom(jax.random.fold_in(seeds[6], 71), 0),
        "coupling": jnp.clip(jnp.exp(jax.random.uniform(seeds[4], (ATOMS, NPROJ), jnp.float32, math.log(0.3), math.log(0.5))), 0.3, 0.5),
        "occupancy": jnp.clip(jnp.exp(math.log(2.0) - 2.3025851 * jax.random.uniform(seeds[5], (NSTATE,), jnp.float32) ** shard_levels(seeds[5], (NSTATE,), ((0, 16),), -0.2, 0.2)), 0.2, 2.0),
    }


def apply_operator(block, ham, proj, slot_atom, coupling):
    width = block.shape[1]
    cellwise = block.astype(jnp.float32).reshape(CELLS, NODES, width)
    local = jnp.einsum("cij,cjs->cis", ham, cellwise)
    coef = jnp.einsum("ckn,cns->cks", proj, cellwise)
    coef = coef.reshape(CELLS * SLOTS, NPROJ * width)
    table = jax.ops.segment_sum(coef, slot_atom.reshape(-1), num_segments=ATOMS)
    scaled = (table.reshape(ATOMS, NPROJ, width) * coupling[:, :, None]).astype(jnp.bfloat16)
    per_slot = scaled[slot_atom.reshape(-1)].reshape(CELLS, SLOTS * NPROJ, width).astype(jnp.float32)
    local = local + jnp.einsum("ckn,cks->cns", proj, per_slot)
    lower = local[:, :FACE]
    upper = local[:, NODES - FACE:]
    zero_face = jnp.zeros((1, FACE, width), jnp.float32)
    from_below = jnp.concatenate([zero_face, upper[:CELLS - 1]], axis=0)
    from_above = jnp.concatenate([lower[1:], zero_face], axis=0)
    middle = local[:, FACE:NODES - FACE]
    total = jnp.concatenate([lower + from_below, middle, upper + from_above], axis=1)
    return total.reshape(CELLS * NODES, width)


def filter_block(block, ham, proj, slot_atom, coupling):
    half_width = 1.5
    center = 0.5
    low_edge = -1.2
    sigma = half_width / (low_edge - center)
    gamma = 2.0 / sigma
    previous = block
    image = apply_operator(block, ham, proj, slot_atom, coupling)
    current = ((image - center * block.astype(jnp.float32)) * (sigma / half_width)).astype(jnp.bfloat16)
    for degree in range(1, DEGREE):
        sigma_new = 1.0 / (gamma - sigma)
        image = apply_operator(current, ham, proj, slot_atom, coupling)
        following = (image - center * current.astype(jnp.float32)) * (2.0 * sigma_new / half_width)
        following = following - (sigma * sigma_new) * previous.astype(jnp.float32)
        previous = current
        current = following.astype(jnp.bfloat16)
        sigma = sigma_new
    return current


def reference(states, cell_ham, projectors, slot_atom, coupling, occupancy):
    ham = cell_ham.astype(jnp.float32)
    proj = projectors.astype(jnp.float32)
    blocks = states.reshape(NODES_ALL, N_STATE, STATE_DEV).transpose(1, 0, 2)
    weights = occupancy.reshape(N_STATE, STATE_DEV)

    def run(pair):
        block, weight = pair
        result = filter_block(block, ham, proj, slot_atom, coupling)
        values = result.astype(jnp.float32)
        partial_density = jnp.dot(values * values, weight, precision=lax.Precision.HIGHEST)
        return result, partial_density

    results, partials = lax.map(run, (blocks, weights))
    filtered = results.transpose(1, 0, 2).reshape(NODES_ALL, NSTATE)
    density = jnp.sum(partials, axis=0) / NSTATE
    return filtered, density
```

```python
import functools

import jax
import jax.numpy as jnp
from jax import lax
from jax.experimental import pallas as pl
from jax.experimental.pallas import tpu as pltpu
from jax.sharding import Mesh, PartitionSpec as P

FACE = 64
DEGREE = 4
LANES = 128
NODES = 512
NPROJ = 18
SLOTS = 4
ROWS = SLOTS * NPROJ
PACK = NODES + 80
GROUP = 4
PART = 2 * NODES
CENTER = 0.5
HALF_WIDTH = 1.5
LOW_EDGE = -1.2

BF16 = jnp.bfloat16
F32 = jnp.float32
NT = (((1,), (1,)), ((), ()))


def chebyshev_factors():
    sigma = HALF_WIDTH / (LOW_EDGE - CENTER)
    gamma = 2.0 / sigma
    factors = [(sigma / HALF_WIDTH, 0.0)]
    for _ in range(1, DEGREE):
        sigma_new = 1.0 / (gamma - sigma)
        factors.append((2.0 * sigma_new / HALF_WIDTH, sigma * sigma_new))
        sigma = sigma_new
    return factors


def iota(shape, dim):
    return lax.broadcasted_iota(jnp.int32, shape, dim)


def dot(a, b):
    return jnp.dot(a, b, preferred_element_type=F32)


def dot_nt(a, b):
    return lax.dot_general(a, b, NT, preferred_element_type=F32)


def placers():
    row = iota((LANES, ROWS), 0)
    col = iota((LANES, ROWS), 1)
    first = row == col
    second = ((row < NPROJ) & (row == col)) | ((row >= ROWS) & (row == col + ROWS - NPROJ))
    second = second & (row < 2 * ROWS - NPROJ)
    return first.astype(F32).astype(BF16), second.astype(F32).astype(BF16)


def low_lanes(rows):
    return iota((rows, LANES), 1) < FACE


def pick(rows, at):
    return jnp.sum(jnp.where(iota(rows.shape, 0) == at, rows, 0.0), axis=0, keepdims=True)


def open_kernel(atom_ref, v_ref, ham_ref, proj_ref, out_ref):
    width = v_ref.shape[0]
    piece = width // GROUP
    place0, place1 = placers()
    p0 = dot(place0, proj_ref[0]).astype(BF16)
    p1 = dot(place1, proj_ref[1]).astype(BF16)
    v0 = v_ref[:, :NODES]
    v1 = v_ref[:, NODES:]
    coef = dot_nt(v0, p0) + dot_nt(v1, p1)
    low = dot_nt(v0, ham_ref[0, :LANES, :])
    high = dot_nt(v1, ham_ref[1, NODES - LANES :, :])
    face = jnp.where(low_lanes(width), low, high)
    edge = jnp.where(
        low_lanes(ROWS),
        proj_ref[0, :, :LANES].astype(F32),
        proj_ref[1, :, NODES - LANES :].astype(F32),
    ).astype(BF16)
    lane = iota((16, LANES), 1)
    atoms = jnp.full((16, LANES), -1, jnp.int32)
    for block in range(2 * SLOTS - 1):
        cell, slot = (0, block) if block < SLOTS else (1, block - SLOTS + 1)
        inside = (lane >= block * NPROJ) & (lane < (block + 1) * NPROJ)
        atoms = jnp.where(inside, atom_ref[cell, slot], atoms)
    atoms = atoms.astype(F32).astype(BF16)
    tail = jnp.concatenate(
        [edge[piece:], jnp.zeros((2 * piece - 16 - ROWS, LANES), BF16)], axis=0
    )
    for to in range(GROUP):
        rows = slice(to * piece, (to + 1) * piece)
        out_ref[to, :, :PART] = v_ref[rows, :]
        out_ref[to, :, PART : PART + LANES] = coef[rows].astype(BF16)
        out_ref[to, :, PART + LANES : PART + 2 * LANES] = face[rows].astype(BF16)
        out_ref[to, :, PART + 2 * LANES : PART + 3 * LANES] = edge[:piece]
        out_ref[to, : piece - 16, PART + 3 * LANES :] = tail
        out_ref[to, piece - 16 :, PART + 3 * LANES :] = atoms


def pack_kernel(in_ref, out_ref):
    last = GROUP - 1
    piece = in_ref.shape[1]
    low = low_lanes(piece)
    for part in range(GROUP):
        out_ref[:, part * LANES : (part + 1) * LANES] = in_ref[part, :, :LANES]
    at = GROUP * LANES
    for k in (1, 2, 3):
        lanes = slice(k * LANES, (k + 1) * LANES)
        tile = jnp.where(low, in_ref[0, :, lanes].astype(F32), in_ref[last, :, lanes].astype(F32))
        if k == 3:
            row = iota((piece, LANES), 0)
            first = piece - 16
            for part in range(GROUP):
                atoms = in_ref[part, first:, lanes].astype(F32)
                tile = jnp.where(row == first + part, atoms[:1], tile)
        out_ref[:, at : at + LANES] = tile.astype(BF16)
        at += LANES


def step_kernel(degree, factors, *refs):
    first = degree == 0
    last = degree == DEGREE - 1
    refs = list(refs)
    take = lambda: refs.pop(0)
    place_ref, coup_ref, got_ref, v_ref = take(), take(), take(), take()
    old_ref = None if first else take()
    if first:
        packs = [take() for _ in range(GROUP)]
    else:
        packs = [take() for _ in range(GROUP)]
        proj_ref, near_ref, atoms_ref = take(), take(), take()
    occ_ref = take() if last else None
    next_ref = take()
    if first:
        proj_ref, near_ref, atoms_ref = None, None, None
    if last:
        density_ref = take()
    else:
        message_ref = take()
    if first:
        proj_ref, near_ref, atoms_ref = take(), take(), take()
    local_ref = take()

    groups = got_ref.shape[0]
    piece = v_ref.shape[1]
    me = place_ref[0]
    z = place_ref[1]
    below = jnp.maximum(z - 1, 0)
    above = jnp.minimum(z + 1, groups - 1)
    has_below = (z > 0).astype(F32)
    has_above = (z < groups - 1).astype(F32)
    wide = GROUP * LANES

    for r in range(GROUP):
        part = jnp.bitwise_xor(me, r)
        for cell in range(2):
            ham = packs[r][cell, :NODES, :]
            lanes = slice(cell * NODES, (cell + 1) * NODES)
            local_ref[part, :, lanes] = dot_nt(v_ref[part, :, lanes], ham)

    if first:
        place0, place1 = placers()
        for r in range(GROUP):
            part = jnp.bitwise_xor(me, r)
            for cell, place in ((0, place0), (1, place1)):
                raw = packs[r][cell, NODES : NODES + ROWS, :]
                lanes = slice(cell * NODES, (cell + 1) * NODES)
                proj_ref[part, :, lanes] = dot(place, raw).astype(BF16)
        edge_at = wide + LANES
        for k, group, place in ((0, below, place1), (1, above, place0)):
            tail = got_ref[group, : ROWS - piece, edge_at + LANES :]
            raw = jnp.concatenate([got_ref[group, :, edge_at : edge_at + LANES], tail], axis=0)
            near_ref[k] = dot(place, raw).astype(BF16)
        atoms_ref[...] = jnp.full(atoms_ref.shape, -1.0, F32)
        for group in range(groups):
            rows = got_ref[group, piece - 16 :, edge_at + LANES :].astype(F32)
            for part in range(GROUP):
                atoms_ref[group : group + 1, part * LANES : (part + 1) * LANES] = rows[part : part + 1]

    atoms = atoms_ref[...]
    which = lax.rem(iota(atoms.shape, 1) % LANES, NPROJ).astype(F32)
    codes = jnp.where(atoms < 0, -1.0, atoms * NPROJ + which)
    mine = jnp.concatenate(
        [
            pick(atoms[:16], z),
            pick(atoms[:16, wide - LANES :], below),
            pick(atoms[:16, :LANES], above),
        ],
        axis=1,
    )
    mine_which = lax.rem(iota(mine.shape, 1) % LANES, NPROJ).astype(F32)
    wanted = jnp.where(mine < 0, -2.0, mine * NPROJ + mine_which)
    spread = jnp.transpose(codes)
    total = jnp.zeros((piece, wide + 2 * LANES), F32)
    for group in range(groups):
        match = spread[:, group : group + 1] == wanted
        chosen = jnp.where(match, 1.0, 0.0).astype(BF16)
        total = total + dot(got_ref[group, :, :wide], chosen)
    count = coup_ref.shape[0]
    row = iota((count, LANES), 0).astype(F32)
    scaled = []
    for k in range(GROUP + 2):
        lanes = slice(k * LANES, (k + 1) * LANES)
        factor = jnp.sum(
            jnp.where(row == mine[:, lanes], coup_ref[...], 0.0), axis=0, keepdims=True
        )
        scaled.append((total[:, lanes] * factor).astype(BF16))

    for part in range(GROUP):
        local_ref[part] = local_ref[part] + dot(scaled[part], proj_ref[part])

    low = low_lanes(piece)
    face = slice(wide, wide + LANES)
    from_below = (got_ref[below, :, face].astype(F32) + dot(scaled[GROUP], near_ref[0])) * has_below
    from_above = (
        got_ref[above, :, face].astype(F32) + dot(scaled[GROUP + 1], near_ref[1])
    ) * has_above
    cells = [(part, cell * NODES) for part in range(GROUP) for cell in range(2)]
    heads = [local_ref[part, :, a : a + LANES] for part, a in cells]
    tails = [local_ref[part, :, a + NODES - LANES : a + NODES] for part, a in cells]
    for k, (part, a) in enumerate(cells):
        under = tails[k - 1] if k > 0 else from_below
        over = heads[k + 1] if k + 1 < len(cells) else from_above
        local_ref[part, :, a : a + LANES] = heads[k] + jnp.where(
            low, pltpu.roll(under, FACE, 1), 0.0
        )
        local_ref[part, :, a + NODES - LANES : a + NODES] = tails[k] + jnp.where(
            low, 0.0, pltpu.roll(over, FACE, 1)
        )

    gain, back = factors[degree]
    for part in range(GROUP):
        now = v_ref[part].astype(F32)
        new = (local_ref[part] - CENTER * now) * gain
        if not first:
            new = new - back * old_ref[part].astype(F32)
        new = new.astype(BF16)
        next_ref[part] = new
        if last:
            values = new.astype(F32)
            weight = jnp.broadcast_to(pick(occ_ref[...], me), (8, piece))
            density_ref[part : part + 1, :] = jnp.dot(
                weight, values * values, precision=lax.Precision.HIGHEST, preferred_element_type=F32
            )[:1]
        else:
            message_ref[:, part * LANES : (part + 1) * LANES] = dot_nt(new, proj_ref[part]).astype(
                BF16
            )
    if not last:
        for r in range(GROUP):
            part = jnp.bitwise_xor(me, r)

            @pl.when(part == 0)
            def _():
                tile = dot_nt(next_ref[0, :, :NODES], packs[r][0, :LANES, :])
                local_ref[0, :, :LANES] = tile

            @pl.when(part == GROUP - 1)
            def _():
                tile = dot_nt(
                    next_ref[GROUP - 1, :, NODES:], packs[r][1, NODES - LANES : NODES, :]
                )
                local_ref[0, :, LANES : 2 * LANES] = tile

        message_ref[:, wide:] = jnp.where(
            low, local_ref[0, :, :LANES], local_ref[0, :, LANES : 2 * LANES]
        ).astype(BF16)


def vmem():
    return pl.BlockSpec(memory_space=pltpu.VMEM)


def smem():
    return pl.BlockSpec(memory_space=pltpu.SMEM)


def shape(dims, dtype=BF16):
    return jax.ShapeDtypeStruct(dims, dtype)


def shards(interpret, states, cell_ham, projectors, slot_atom, coupling, occupancy):
    width = states.shape[1]
    piece = width // GROUP
    groups = lax.axis_size("z")
    y_hi = lax.axis_size("yh")
    params = pltpu.CompilerParams(vmem_limit_bytes=32 * 1024 * 1024)
    call = functools.partial(pl.pallas_call, compiler_params=params, interpret=interpret)
    me = 2 * lax.axis_index("yl") + lax.axis_index("c")
    place = jnp.stack([me, lax.axis_index("z")]).astype(jnp.int32)
    coup = jnp.tile(coupling, (1, LANES // NPROJ + 1))[:, :LANES]
    occ = occupancy.reshape(GROUP, piece)

    pack = jnp.concatenate(
        [cell_ham, jnp.pad(projectors, ((0, 0), (0, PACK - NODES - ROWS), (0, 0)))], axis=1
    )
    swap = [(0, 1), (1, 0)]
    ring = 2 * y_hi
    spot = lambda y: (y % 2) * y_hi + y // 2
    up = [(spot(y), spot((y + 1) % ring)) for y in range(ring)]
    down = [(b, a) for a, b in up]
    side = jnp.stack(
        [lax.ppermute(pack[0], ("yl", "yh"), up), lax.ppermute(pack[1], ("yl", "yh"), down)]
    )
    packs = [pack, lax.ppermute(pack, "c", swap), side, lax.ppermute(side, "c", swap)]

    v_t = states.T
    opened = call(
        open_kernel,
        out_shape=shape((GROUP, piece, PART + 4 * LANES)),
        in_specs=[smem(), vmem(), vmem(), vmem()],
        out_specs=vmem(),
    )(slot_atom, v_t, cell_ham, projectors)
    opened = lax.all_to_all(opened, ("yl", "c"), 0, 0)
    v = opened[:, :, :PART]
    message = call(
        pack_kernel,
        out_shape=shape((piece, 7 * LANES)),
        in_specs=[vmem()],
        out_specs=vmem(),
    )(opened[:, :, PART:])

    factors = chebyshev_factors()
    state_shape = shape((GROUP, piece, PART))
    message_shape = shape((piece, 5 * LANES))
    old = None
    kept = []
    for degree in range(DEGREE):
        got = lax.all_gather(message, "z")
        first, last = degree == 0, degree == DEGREE - 1
        ins = [place, coup, got, v] + ([] if first else [old]) + packs + kept
        ins += [occ] if last else []
        outs = [state_shape, shape((GROUP, PART), F32) if last else message_shape]
        if first:
            outs += [
                shape((GROUP, LANES, PART)),
                shape((2, LANES, LANES)),
                shape((LANES, GROUP * LANES), F32),
            ]
        result = call(
            functools.partial(step_kernel, degree, factors),
            out_shape=outs,
            in_specs=[smem()] + [vmem()] * (len(ins) - 1),
            out_specs=[vmem()] * len(outs),
            scratch_shapes=[pltpu.VMEM((GROUP, piece, PART), F32)],
        )(*ins)
        if first:
            kept = list(result[2:])
        old, v, message = v, result[0], result[1]

    filtered = lax.all_to_all(v, ("yl", "c"), 0, 0).reshape(width, PART).T
    parts = GROUP * lax.axis_size("x") * y_hi
    terms = lax.all_to_all(
        message.reshape(parts, GROUP * PART // parts), ("yl", "c", "x", "yh"), 0, 0, tiled=True
    )
    density = jnp.sum(terms, axis=0) / (width * lax.axis_size("x") * y_hi)
    return filtered, density


def build(mesh, interpret=False):
    part = ("z", "yl", "c")
    group = ("x", "yh")
    return jax.shard_map(
        functools.partial(shards, interpret),
        mesh=mesh,
        in_specs=(
            P(part, group),
            P(part, None, None),
            P(part, None, None),
            P(part, None),
            P(),
            P(group),
        ),
        out_specs=(P(part, group), P(part + group)),
        check_vma=False,
    )


def solution(mesh):
    count, groups = mesh.shape["mesh"], mesh.shape["state"]
    devices = mesh.devices.reshape(count // GROUP, 2, 2, groups // 4, 4)
    return build(Mesh(devices, ("z", "yl", "c", "x", "yh")))
```

```python
import functools

import jax
import jax.numpy as jnp
from jax import lax
from jax.experimental import pallas as pl
from jax.experimental.pallas import tpu as pltpu
from jax.sharding import Mesh, PartitionSpec as P

FACE = 64
DEGREE = 4
LANES = 128
NODES = 512
NPROJ = 18
SLOTS = 4
ROWS = SLOTS * NPROJ
SHARE = 208
GROUP = 4
PART = 2 * NODES
CENTER = 0.5
HALF_WIDTH = 1.5
LOW_EDGE = -1.2

BF16 = jnp.bfloat16
F32 = jnp.float32
NT = (((1,), (1,)), ((), ()))


def chebyshev_factors():
    sigma = HALF_WIDTH / (LOW_EDGE - CENTER)
    gamma = 2.0 / sigma
    factors = [(sigma / HALF_WIDTH, 0.0)]
    for _ in range(1, DEGREE):
        sigma_new = 1.0 / (gamma - sigma)
        factors.append((2.0 * sigma_new / HALF_WIDTH, sigma * sigma_new))
        sigma = sigma_new
    return factors


def iota(shape, dim):
    return lax.broadcasted_iota(jnp.int32, shape, dim)


def dot(a, b):
    return jnp.dot(a, b, preferred_element_type=F32)


def dot_nt(a, b):
    return lax.dot_general(a, b, NT, preferred_element_type=F32)


def placers():
    row = iota((LANES, ROWS), 0)
    col = iota((LANES, ROWS), 1)
    first = row == col
    second = ((row < NPROJ) & (row == col)) | ((row >= ROWS) & (row == col + ROWS - NPROJ))
    second = second & (row < 2 * ROWS - NPROJ)
    return first.astype(F32).astype(BF16), second.astype(F32).astype(BF16)


def low_lanes(rows):
    return iota((rows, LANES), 1) < FACE


def pick(rows, at):
    return jnp.sum(jnp.where(iota(rows.shape, 0) == at, rows, 0.0), axis=0, keepdims=True)


def open_kernel(atom_ref, v_ref, ham_ref, proj_ref, out_ref):
    width = v_ref.shape[0]
    piece = width // GROUP
    place0, place1 = placers()
    p0 = dot(place0, proj_ref[0]).astype(BF16)
    p1 = dot(place1, proj_ref[1]).astype(BF16)
    v0 = v_ref[:, :NODES]
    v1 = v_ref[:, NODES:]
    coef = dot_nt(v0, p0) + dot_nt(v1, p1)
    low = dot_nt(v0, ham_ref[0, :LANES, :])
    high = dot_nt(v1, ham_ref[1, NODES - LANES :, :])
    face = jnp.where(low_lanes(width), low, high)
    edge = jnp.where(
        low_lanes(ROWS),
        proj_ref[0, :, :LANES].astype(F32),
        proj_ref[1, :, NODES - LANES :].astype(F32),
    ).astype(BF16)
    lane = iota((16, LANES), 1)
    atoms = jnp.full((16, LANES), -1, jnp.int32)
    for block in range(2 * SLOTS - 1):
        cell, slot = (0, block) if block < SLOTS else (1, block - SLOTS + 1)
        inside = (lane >= block * NPROJ) & (lane < (block + 1) * NPROJ)
        atoms = jnp.where(inside, atom_ref[cell, slot], atoms)
    atoms = atoms.astype(F32).astype(BF16)
    tail = jnp.concatenate(
        [edge[piece:], jnp.zeros((2 * piece - 16 - ROWS, LANES), BF16)], axis=0
    )
    for to in range(GROUP):
        rows = slice(to * piece, (to + 1) * piece)
        out_ref[to, :, :LANES] = coef[rows].astype(BF16)
        out_ref[to, :, LANES : 2 * LANES] = face[rows].astype(BF16)
        out_ref[to, :, 2 * LANES : 3 * LANES] = edge[:piece]
        out_ref[to, : piece - 16, 3 * LANES :] = tail
        out_ref[to, piece - 16 :, 3 * LANES :] = atoms


def share_kernel(place_ref, v_ref, ham_ref, proj_ref, *out_refs):
    me = place_ref[0]
    piece = v_ref.shape[0] // GROUP
    local = [dot_nt(v_ref[:, :NODES], ham_ref[0]), dot_nt(v_ref[:, NODES:], ham_ref[1])]
    local = jnp.concatenate(local, axis=1).astype(BF16)
    first = me == 0
    half = FACE // 2
    at = 2 * piece
    for to in range(GROUP):
        rows = slice(to * piece, (to + 1) * piece)
        for r, out_ref in enumerate(out_refs):

            @pl.when(jnp.bitwise_xor(me, r) == to)
            def _():
                out_ref[:piece, :] = v_ref[rows, :]
                out_ref[piece:at, :] = local[rows]

    for out_ref in out_refs:
        for k in range(2):
            lanes = slice(k * NODES, (k + 1) * NODES)

            @pl.when(first)
            def _():
                out_ref[at : at + half, lanes] = ham_ref[0, k * half : (k + 1) * half, :]

            @pl.when(jnp.logical_not(first))
            def _():
                start = NODES - FACE + k * half
                out_ref[at : at + half, lanes] = ham_ref[1, start : start + half, :]

            out_ref[at + half :, lanes] = jnp.concatenate(
                [proj_ref[k], jnp.zeros((SHARE - at - half - ROWS, NODES), BF16)], axis=0
            )


def pack_kernel(in_ref, out_ref):
    last = GROUP - 1
    piece = in_ref.shape[1]
    low = low_lanes(piece)
    for part in range(GROUP):
        out_ref[:, part * LANES : (part + 1) * LANES] = in_ref[part, :, :LANES]
    at = GROUP * LANES
    for k in (1, 2, 3):
        lanes = slice(k * LANES, (k + 1) * LANES)
        tile = jnp.where(low, in_ref[0, :, lanes].astype(F32), in_ref[last, :, lanes].astype(F32))
        if k == 3:
            row = iota((piece, LANES), 0)
            first = piece - 16
            for part in range(GROUP):
                atoms = in_ref[part, first:, lanes].astype(F32)
                tile = jnp.where(row == first + part, atoms[:1], tile)
        out_ref[:, at : at + LANES] = tile.astype(BF16)
        at += LANES


def sum_coefs(place_ref, coup_ref, got_ref, atoms_ref):
    groups = got_ref.shape[0]
    piece = got_ref.shape[1]
    wide = GROUP * LANES
    z = place_ref[1]
    below = jnp.maximum(z - 1, 0)
    above = jnp.minimum(z + 1, groups - 1)
    atoms = atoms_ref[:16, :]
    mine = jnp.concatenate(
        [pick(atoms, z), pick(atoms[:, wide - LANES :], below), pick(atoms[:, :LANES], above)], axis=1
    )
    wanted = jnp.where(mine < 0, -2.0, mine).astype(BF16)
    spread = jnp.transpose(atoms_ref[...]).astype(BF16)
    same = lax.rem(iota((LANES, LANES), 0), NPROJ) == lax.rem(iota((LANES, LANES), 1), NPROJ)
    same = same.astype(F32).astype(BF16)
    same = jnp.concatenate([same] * (GROUP + 2), axis=1)
    same = jnp.concatenate([same] * GROUP, axis=0)
    none = jnp.zeros((), BF16)
    total = jnp.zeros((piece, wide + 2 * LANES), F32)
    for group in range(groups):
        chosen = jnp.where(spread[:, group : group + 1] == wanted, same, none)
        total = total + dot(got_ref[group, :, :wide], chosen)
    row = iota((coup_ref.shape[0], LANES), 0).astype(F32)
    scaled = []
    for k in range(GROUP + 2):
        lanes = slice(k * LANES, (k + 1) * LANES)
        factor = jnp.where(row == mine[:, lanes], coup_ref[...], 0.0)
        factor = jnp.sum(factor, axis=0, keepdims=True)
        scaled.append((total[:, lanes] * factor).astype(BF16))
    return scaled


def add_faces(place_ref, got_ref, near_ref, scaled, local_ref):
    groups = got_ref.shape[0]
    piece = got_ref.shape[1]
    z = place_ref[1]
    below = jnp.maximum(z - 1, 0)
    above = jnp.minimum(z + 1, groups - 1)
    low = low_lanes(piece)
    face = slice(GROUP * LANES, (GROUP + 1) * LANES)
    from_below = got_ref[below, :, face].astype(F32) + dot(scaled[GROUP], near_ref[0])
    from_above = got_ref[above, :, face].astype(F32) + dot(scaled[GROUP + 1], near_ref[1])
    from_below = from_below * (z > 0).astype(F32)
    from_above = from_above * (z < groups - 1).astype(F32)
    cells = [(part, cell * NODES) for part in range(GROUP) for cell in range(2)]
    heads = [local_ref[part, :, a : a + LANES] for part, a in cells]
    tails = [local_ref[part, :, a + NODES - LANES : a + NODES] for part, a in cells]
    for k, (part, a) in enumerate(cells):
        under = tails[k - 1] if k > 0 else from_below
        over = heads[k + 1] if k + 1 < len(cells) else from_above
        local_ref[part, :, a : a + LANES] = heads[k] + jnp.where(
            low, pltpu.roll(under, FACE, 1), 0.0
        )
        local_ref[part, :, a + NODES - LANES : a + NODES] = tails[k] + jnp.where(
            low, 0.0, pltpu.roll(over, FACE, 1)
        )


def write_message(new, proj_ref, edge_ref, message_ref):
    for part in range(GROUP):
        lanes = slice(part * LANES, (part + 1) * LANES)
        message_ref[:, lanes] = dot_nt(new[part], proj_ref[part]).astype(BF16)
    ends = jnp.concatenate([new[0][:, :NODES], new[GROUP - 1][:, NODES:]], axis=1)
    message_ref[:, GROUP * LANES :] = dot_nt(ends, edge_ref[...]).astype(BF16)


def first_kernel(factors, place_ref, coup_ref, got_ref, *refs):
    shares = refs[:GROUP]
    next_ref, message_ref, v_ref, proj_ref, near_ref, edge_ref, atoms_ref, local_ref = refs[GROUP:]
    groups = got_ref.shape[0]
    piece = v_ref.shape[1]
    me = place_ref[0]
    z = place_ref[1]
    below = jnp.maximum(z - 1, 0)
    above = jnp.minimum(z + 1, groups - 1)
    wide = GROUP * LANES
    half = FACE // 2
    at = 2 * piece

    place0, place1 = placers()
    edge_ref[...] = jnp.zeros(edge_ref.shape, BF16)
    for r, share in enumerate(shares):
        part = jnp.bitwise_xor(me, r)
        v_ref[part] = share[:piece, :]
        local_ref[part] = share[piece:at, :].astype(F32)
        for cell, place in ((0, place0), (1, place1)):
            lanes = slice(cell * NODES, (cell + 1) * NODES)
            raw = share[at + half : at + half + ROWS, lanes]
            proj_ref[part, :, lanes] = dot(place, raw).astype(BF16)
        for k, end in ((0, 0), (1, GROUP - 1)):

            @pl.when(part == end)
            def _():
                lanes = slice(k * NODES, (k + 1) * NODES)
                row = k * FACE
                edge_ref[row : row + half, lanes] = share[at : at + half, :NODES]
                edge_ref[row + half : row + FACE, lanes] = share[at : at + half, NODES:]

    edge_at = wide + LANES
    for k, group, place in ((0, below, place1), (1, above, place0)):
        tail = got_ref[group, : ROWS - piece, edge_at + LANES :]
        raw = jnp.concatenate([got_ref[group, :, edge_at : edge_at + LANES], tail], axis=0)
        near_ref[k] = dot(place, raw).astype(BF16)
    atoms_ref[...] = jnp.full(atoms_ref.shape, -1.0, F32)
    for group in range(groups):
        rows = got_ref[group, piece - 16 :, edge_at + LANES :].astype(F32)
        for part in range(GROUP):
            lanes = slice(part * LANES, (part + 1) * LANES)
            atoms_ref[group : group + 1, lanes] = rows[part : part + 1]

    scaled = sum_coefs(place_ref, coup_ref, got_ref, atoms_ref)
    for part in range(GROUP):
        local_ref[part] = local_ref[part] + dot(scaled[part], proj_ref[part])
    add_faces(place_ref, got_ref, near_ref, scaled, local_ref)
    gain, _ = factors[0]
    new = []
    for part in range(GROUP):
        new.append(((local_ref[part] - CENTER * v_ref[part].astype(F32)) * gain).astype(BF16))
        next_ref[part] = new[part]
    write_message(new, proj_ref, edge_ref, message_ref)


def step_kernel(degree, factors, place_ref, coup_ref, got_ref, v_ref, old_ref, ham_ref, *refs):
    last = degree == DEGREE - 1
    proj_ref, near_ref, edge_ref, atoms_ref = refs[:4]
    refs = refs[4:]
    if last:
        occ_ref, next_ref, local_ref, held_ref, sems = refs
    else:
        next_ref, message_ref, local_ref, held_ref, sems = refs
    piece = v_ref.shape[1]
    copies = [
        pltpu.make_async_copy(ham_ref.at[k // 2, k % 2], held_ref.at[k], sems.at[k])
        for k in range(2 * GROUP)
    ]
    for copy in copies:
        copy.start()
    scaled = sum_coefs(place_ref, coup_ref, got_ref, atoms_ref)
    for copy in copies:
        copy.wait()
    for part in range(GROUP):
        for cell in range(2):
            lanes = slice(cell * NODES, (cell + 1) * NODES)
            local = dot_nt(v_ref[part, :, lanes], held_ref[2 * part + cell])
            local_ref[part, :, lanes] = local + dot(scaled[part], proj_ref[part, :, lanes])
    add_faces(place_ref, got_ref, near_ref, scaled, local_ref)

    gain, back = factors[degree]
    new = []
    for part in range(GROUP):
        now = v_ref[part].astype(F32)
        image = (local_ref[part] - CENTER * now) * gain - back * old_ref[part].astype(F32)
        new.append(image.astype(BF16))
        next_ref[part, :piece, :] = new[part]
    if not last:
        write_message(new, proj_ref, edge_ref, message_ref)
        return
    weight = jnp.broadcast_to(pick(occ_ref[...], place_ref[0]), (8, piece))
    row = iota((16, PART), 0)
    for part in range(GROUP):
        values = new[part].astype(F32)
        sums = jnp.dot(
            weight, values * values, precision=lax.Precision.HIGHEST, preferred_element_type=F32
        )[:1]
        high = sums.astype(BF16).astype(F32)
        both = jnp.where(row == 0, high, jnp.where(row == 1, sums - high, 0.0))
        next_ref[part, piece:, :] = both.astype(BF16)


def density_kernel(in_ref, out_ref):
    total = jnp.zeros((2, PART), F32)
    for part in range(GROUP):
        total = total + in_ref[part, :2, :].astype(F32)
    total = total[:1] + total[1:]
    for k in range(PART // LANES):
        tile = total[:, k * LANES : (k + 1) * LANES]
        out_ref[2 * k : 2 * k + 1, :] = tile[:, :FACE]
        out_ref[2 * k + 1 : 2 * k + 2, :] = tile[:, FACE:]


def vmem():
    return pl.BlockSpec(memory_space=pltpu.VMEM)


def smem():
    return pl.BlockSpec(memory_space=pltpu.SMEM)


def shape(dims, dtype=BF16):
    return jax.ShapeDtypeStruct(dims, dtype)


def shards(interpret, states, cell_ham, projectors, slot_atom, coupling, occupancy):
    width = states.shape[1]
    piece = width // GROUP
    y_hi = lax.axis_size("yh")
    spread = lax.axis_size("x") * y_hi
    params = pltpu.CompilerParams(vmem_limit_bytes=32 * 1024 * 1024)
    call = functools.partial(pl.pallas_call, compiler_params=params, interpret=interpret)
    me = 2 * lax.axis_index("yl") + lax.axis_index("c")
    place = jnp.stack([me, lax.axis_index("z")]).astype(jnp.int32)
    coup = jnp.tile(coupling, (1, LANES // NPROJ + 1))[:, :LANES]
    occ = occupancy.reshape(GROUP, piece)
    near = ("yl", "c")

    ham = lax.all_gather(cell_ham, near)
    v_t = states.T
    opened = call(
        open_kernel,
        out_shape=shape((GROUP, piece, 4 * LANES)),
        in_specs=[smem(), vmem(), vmem(), vmem()],
        out_specs=vmem(),
    )(slot_atom, v_t, cell_ham, projectors)
    opened = lax.all_to_all(opened, near, 0, 0)
    shares = call(
        share_kernel,
        out_shape=[shape((SHARE, PART))] * GROUP,
        in_specs=[smem(), vmem(), vmem(), vmem()],
        out_specs=[vmem()] * GROUP,
    )(place, v_t, cell_ham, projectors)
    shares = [shares[0]] + [
        lax.ppermute(shares[r], near, [(k, k ^ r) for k in range(GROUP)]) for r in (1, 2, 3)
    ]
    message = call(
        pack_kernel,
        out_shape=shape((piece, 7 * LANES)),
        in_specs=[vmem()],
        out_specs=vmem(),
    )(opened)

    factors = chebyshev_factors()
    state_shape = shape((GROUP, piece, PART))
    message_shape = shape((piece, 5 * LANES))
    scratch = pltpu.VMEM((GROUP, piece, PART), F32)
    got = lax.all_gather(message, "z")
    v, message, old, *kept = call(
        functools.partial(first_kernel, factors),
        out_shape=[
            state_shape,
            message_shape,
            state_shape,
            shape((GROUP, LANES, PART)),
            shape((2, LANES, LANES)),
            shape((LANES, PART)),
            shape((LANES, GROUP * LANES), F32),
        ],
        in_specs=[smem()] + [vmem()] * (2 + GROUP),
        out_specs=[vmem()] * 7,
        scratch_shapes=[scratch],
    )(place, coup, got, *shares)
    for degree in range(1, DEGREE):
        got = lax.all_gather(message, "z")
        last = degree == DEGREE - 1
        outs = [shape((GROUP, piece + 16, PART))] if last else [state_shape, message_shape]
        ends = [occ] if last else []
        result = call(
            functools.partial(step_kernel, degree, factors),
            out_shape=outs,
            in_specs=[smem()]
            + [vmem()] * 4
            + [pl.BlockSpec(memory_space=pl.ANY)]
            + [vmem()] * (4 + len(ends)),
            out_specs=[vmem()] * len(outs),
            scratch_shapes=[
                scratch,
                pltpu.VMEM((2 * GROUP, NODES, NODES), BF16),
                pltpu.SemaphoreType.DMA((2 * GROUP,)),
            ],
        )(place, coup, got, v, old, ham, *kept, *ends)
        old, v, message = v, result[0], result[-1]

    final = lax.all_to_all(message, near, 0, 0)
    filtered = final[:, :piece, :].reshape(width, PART).T
    terms = call(
        density_kernel,
        out_shape=shape((PART // FACE, FACE), F32),
        grid=(1,),
        in_specs=[pl.BlockSpec((GROUP, 16, PART), lambda i: (0, piece // 16, 0))],
        out_specs=pl.BlockSpec((PART // FACE, FACE), lambda i: (0, 0)),
    )(final)
    terms = lax.all_to_all(
        terms.reshape(spread, PART // spread), ("x", "yh"), 0, 0, tiled=True
    )
    density = jnp.sum(terms, axis=0) / (width * spread)
    return filtered, density


def build(mesh, interpret=False):
    part = ("z", "yl", "c")
    group = ("x", "yh")
    return jax.shard_map(
        functools.partial(shards, interpret),
        mesh=mesh,
        in_specs=(
            P(part, group),
            P(part, None, None),
            P(part, None, None),
            P(part, None),
            P(),
            P(group),
        ),
        out_specs=(P(part, group), P(part + group)),
        check_vma=False,
    )


def solution(mesh):
    count, groups = mesh.shape["mesh"], mesh.shape["state"]
    devices = mesh.devices.reshape(count // GROUP, 2, 2, groups // 4, 4)
    return build(Mesh(devices, ("z", "yl", "c", "x", "yh")))
```

```python
import functools

import jax
import jax.numpy as jnp
from jax import lax
from jax.experimental import pallas as pl
from jax.experimental.pallas import tpu as pltpu
from jax.sharding import Mesh, PartitionSpec as P

FACE = 64
DEGREE = 4
LANES = 128
NODES = 512
NPROJ = 18
SLOTS = 4
ROWS = SLOTS * NPROJ
SHARE = 128
GROUP = 4
PART = 2 * NODES
CENTER = 0.5
HALF_WIDTH = 1.5
LOW_EDGE = -1.2

BF16 = jnp.bfloat16
F32 = jnp.float32
NT = (((1,), (1,)), ((), ()))


def chebyshev_factors():
    sigma = HALF_WIDTH / (LOW_EDGE - CENTER)
    gamma = 2.0 / sigma
    factors = [(sigma / HALF_WIDTH, 0.0)]
    for _ in range(1, DEGREE):
        sigma_new = 1.0 / (gamma - sigma)
        factors.append((2.0 * sigma_new / HALF_WIDTH, sigma * sigma_new))
        sigma = sigma_new
    return factors


def iota(shape, dim):
    return lax.broadcasted_iota(jnp.int32, shape, dim)


def dot(a, b):
    return jnp.dot(a, b, preferred_element_type=F32)


def dot_nt(a, b):
    return lax.dot_general(a, b, NT, preferred_element_type=F32)


def placers():
    row = iota((LANES, ROWS), 0)
    col = iota((LANES, ROWS), 1)
    first = row == col
    second = ((row < NPROJ) & (row == col)) | ((row >= ROWS) & (row == col + ROWS - NPROJ))
    second = second & (row < 2 * ROWS - NPROJ)
    return first.astype(F32).astype(BF16), second.astype(F32).astype(BF16)


def low_lanes(rows):
    return iota((rows, LANES), 1) < FACE


def pick(rows, at):
    return jnp.sum(jnp.where(iota(rows.shape, 0) == at, rows, 0.0), axis=0, keepdims=True)


def open_kernel(atom_ref, v_hbm, ham_hbm, proj_hbm, out_ref, v_ref, ham_ref, proj_ref, sems):
    copies = [
        pltpu.make_async_copy(v_hbm, v_ref, sems.at[0]),
        pltpu.make_async_copy(proj_hbm, proj_ref, sems.at[1]),
        pltpu.make_async_copy(ham_hbm.at[0, :LANES, :], ham_ref.at[0], sems.at[2]),
        pltpu.make_async_copy(ham_hbm.at[1, NODES - LANES :, :], ham_ref.at[1], sems.at[3]),
    ]
    for copy in copies:
        copy.start()
    for copy in copies:
        copy.wait()
    width = v_ref.shape[0]
    piece = width // GROUP
    place0, place1 = placers()
    p0 = dot(place0, proj_ref[0]).astype(BF16)
    p1 = dot(place1, proj_ref[1]).astype(BF16)
    v0 = v_ref[:, :NODES]
    v1 = v_ref[:, NODES:]
    coef = dot_nt(v0, p0) + dot_nt(v1, p1)
    low = dot_nt(v0, ham_ref[0])
    high = dot_nt(v1, ham_ref[1])
    face = jnp.where(low_lanes(width), low, high)
    edge = jnp.where(
        low_lanes(ROWS),
        proj_ref[0, :, :LANES].astype(F32),
        proj_ref[1, :, NODES - LANES :].astype(F32),
    ).astype(BF16)
    lane = iota((16, LANES), 1)
    atoms = jnp.full((16, LANES), -1, jnp.int32)
    for block in range(2 * SLOTS - 1):
        cell, slot = (0, block) if block < SLOTS else (1, block - SLOTS + 1)
        inside = (lane >= block * NPROJ) & (lane < (block + 1) * NPROJ)
        atoms = jnp.where(inside, atom_ref[cell, slot], atoms)
    atoms = atoms.astype(F32).astype(BF16)
    tail = jnp.concatenate(
        [edge[piece:], jnp.zeros((2 * piece - 16 - ROWS, LANES), BF16)], axis=0
    )
    for to in range(GROUP):
        rows = slice(to * piece, (to + 1) * piece)
        out_ref[to, :, :LANES] = coef[rows].astype(BF16)
        out_ref[to, :, LANES : 2 * LANES] = face[rows].astype(BF16)
        out_ref[to, :, 2 * LANES : 3 * LANES] = edge[:piece]
        out_ref[to, : piece - 16, 3 * LANES :] = tail
        out_ref[to, piece - 16 :, 3 * LANES :] = atoms


def share_kernel(v_hbm, proj_hbm, out_ref, proj_ref, sems):
    piece = v_hbm.shape[0] // GROUP
    copies = [pltpu.make_async_copy(proj_hbm, proj_ref, sems.at[GROUP])]
    for to in range(GROUP):
        rows = pl.ds(to * piece, piece)
        copies.append(
            pltpu.make_async_copy(v_hbm.at[rows, :], out_ref.at[to, pl.ds(0, piece), :], sems.at[to])
        )
    for copy in copies:
        copy.start()
    copies[0].wait()
    pad = jnp.zeros((SHARE - piece - ROWS, NODES), BF16)
    for k in range(2):
        rows = jnp.concatenate([proj_ref[k], pad], axis=0)
        for to in range(GROUP):
            out_ref[to, piece:, k * NODES : (k + 1) * NODES] = rows
    for copy in copies[1:]:
        copy.wait()


def pack_kernel(in_ref, out_ref):
    last = GROUP - 1
    piece = in_ref.shape[1]
    low = low_lanes(piece)
    for part in range(GROUP):
        out_ref[:, part * LANES : (part + 1) * LANES] = in_ref[part, :, :LANES]
    at = GROUP * LANES
    for k in (1, 2, 3):
        lanes = slice(k * LANES, (k + 1) * LANES)
        tile = jnp.where(low, in_ref[0, :, lanes].astype(F32), in_ref[last, :, lanes].astype(F32))
        if k == 3:
            row = iota((piece, LANES), 0)
            first = piece - 16
            for part in range(GROUP):
                atoms = in_ref[part, first:, lanes].astype(F32)
                tile = jnp.where(row == first + part, atoms[:1], tile)
        out_ref[:, at : at + LANES] = tile.astype(BF16)
        at += LANES


def sum_coefs(place_ref, coup_ref, got_ref, atoms_ref):
    groups = got_ref.shape[0]
    piece = got_ref.shape[1]
    wide = GROUP * LANES
    z = place_ref[1]
    below = jnp.maximum(z - 1, 0)
    above = jnp.minimum(z + 1, groups - 1)
    atoms = atoms_ref[:16, :]
    mine = jnp.concatenate(
        [pick(atoms, z), pick(atoms[:, wide - LANES :], below), pick(atoms[:, :LANES], above)], axis=1
    )
    wanted = jnp.where(mine < 0, -2.0, mine).astype(BF16)
    spread = jnp.transpose(atoms_ref[...]).astype(BF16)
    same = lax.rem(iota((LANES, LANES), 0), NPROJ) == lax.rem(iota((LANES, LANES), 1), NPROJ)
    same = same.astype(F32).astype(BF16)
    same = jnp.concatenate([same] * (GROUP + 2), axis=1)
    same = jnp.concatenate([same] * GROUP, axis=0)
    none = jnp.zeros((), BF16)
    total = jnp.zeros((piece, wide + 2 * LANES), F32)
    for group in range(groups):
        chosen = jnp.where(spread[:, group : group + 1] == wanted, same, none)
        total = total + dot(got_ref[group, :, :wide], chosen)
    row = iota((coup_ref.shape[0], LANES), 0).astype(F32)
    scaled = []
    for k in range(GROUP + 2):
        lanes = slice(k * LANES, (k + 1) * LANES)
        factor = jnp.where(row == mine[:, lanes], coup_ref[...], 0.0)
        factor = jnp.sum(factor, axis=0, keepdims=True)
        scaled.append((total[:, lanes] * factor).astype(BF16))
    return scaled


def add_faces(place_ref, got_ref, near_ref, scaled, local_ref):
    groups = got_ref.shape[0]
    piece = got_ref.shape[1]
    z = place_ref[1]
    below = jnp.maximum(z - 1, 0)
    above = jnp.minimum(z + 1, groups - 1)
    low = low_lanes(piece)
    face = slice(GROUP * LANES, (GROUP + 1) * LANES)
    from_below = got_ref[below, :, face].astype(F32) + dot(scaled[GROUP], near_ref[0])
    from_above = got_ref[above, :, face].astype(F32) + dot(scaled[GROUP + 1], near_ref[1])
    from_below = from_below * (z > 0).astype(F32)
    from_above = from_above * (z < groups - 1).astype(F32)
    cells = [(part, cell * NODES) for part in range(GROUP) for cell in range(2)]
    heads = [local_ref[part, :, a : a + LANES] for part, a in cells]
    tails = [local_ref[part, :, a + NODES - LANES : a + NODES] for part, a in cells]
    for k, (part, a) in enumerate(cells):
        under = tails[k - 1] if k > 0 else from_below
        over = heads[k + 1] if k + 1 < len(cells) else from_above
        local_ref[part, :, a : a + LANES] = heads[k] + jnp.where(
            low, pltpu.roll(under, FACE, 1), 0.0
        )
        local_ref[part, :, a + NODES - LANES : a + NODES] = tails[k] + jnp.where(
            low, 0.0, pltpu.roll(over, FACE, 1)
        )


def fetch_hams(ham_refs, held_ref, sems):
    copies = [
        pltpu.make_async_copy(ham_refs[k // 2].at[k % 2], held_ref.at[k], sems.at[k])
        for k in range(2 * GROUP)
    ]
    for copy in copies:
        copy.start()
    return copies


def add_local(me, v_ref, held_ref, local_ref):
    for r in range(GROUP):
        part = jnp.bitwise_xor(me, r)
        for cell in range(2):
            lanes = slice(cell * NODES, (cell + 1) * NODES)
            local_ref[part, :, lanes] += dot_nt(v_ref[part, :, lanes], held_ref[2 * r + cell])


def write_message(me, new, held_ref, proj_ref, edge_ref, message_ref):
    for part in range(GROUP):
        lanes = slice(part * LANES, (part + 1) * LANES)
        message_ref[:, lanes] = dot_nt(new[part], proj_ref[part]).astype(BF16)
    ends = jnp.concatenate([new[0][:, :NODES], new[GROUP - 1][:, NODES:]], axis=1)
    for r in range(GROUP):
        part = jnp.bitwise_xor(me, r)

        @pl.when(part == 0)
        def _():
            edge_ref[:FACE, :NODES] = held_ref[2 * r, :FACE, :]
            edge_ref[:FACE, NODES:] = jnp.zeros((FACE, NODES), BF16)

        @pl.when(part == GROUP - 1)
        def _():
            edge_ref[FACE:, :NODES] = jnp.zeros((FACE, NODES), BF16)
            edge_ref[FACE:, NODES:] = held_ref[2 * r + 1, NODES - FACE :, :]

    message_ref[:, GROUP * LANES :] = dot_nt(ends, edge_ref[...]).astype(BF16)


def first_kernel(factors, place_ref, coup_ref, got_ref, *refs):
    hams, refs = refs[:GROUP], refs[GROUP:]
    share_hbm, next_ref, message_ref, v_ref, proj_ref, near_ref, atoms_ref = refs[:7]
    local_ref, held_ref, edge_ref, share_ref, sems = refs[7:]
    groups = got_ref.shape[0]
    piece = v_ref.shape[1]
    me = place_ref[0]
    z = place_ref[1]
    below = jnp.maximum(z - 1, 0)
    above = jnp.minimum(z + 1, groups - 1)
    wide = GROUP * LANES
    shared = [
        pltpu.make_async_copy(
            share_hbm.at[part, pl.ds(piece, SHARE - piece), :], share_ref.at[part], sems.at[8 + part]
        )
        for part in range(GROUP)
    ] + [
        pltpu.make_async_copy(
            share_hbm.at[part, pl.ds(0, piece), :], v_ref.at[part], sems.at[8 + GROUP + part]
        )
        for part in range(GROUP)
    ]
    for copy in shared:
        copy.start()
    copies = fetch_hams(hams, held_ref, sems)

    place0, place1 = placers()
    edge_at = wide + LANES
    for k, group, place in ((0, below, place1), (1, above, place0)):
        tail = got_ref[group, : ROWS - piece, edge_at + LANES :]
        raw = jnp.concatenate([got_ref[group, :, edge_at : edge_at + LANES], tail], axis=0)
        near_ref[k] = dot(place, raw).astype(BF16)
    atoms_ref[...] = jnp.full(atoms_ref.shape, -1.0, F32)
    for group in range(groups):
        rows = got_ref[group, piece - 16 :, edge_at + LANES :].astype(F32)
        for part in range(GROUP):
            lanes = slice(part * LANES, (part + 1) * LANES)
            atoms_ref[group : group + 1, lanes] = rows[part : part + 1]
    scaled = sum_coefs(place_ref, coup_ref, got_ref, atoms_ref)

    for copy in shared:
        copy.wait()
    for part in range(GROUP):
        for cell, place in ((0, place0), (1, place1)):
            lanes = slice(cell * NODES, (cell + 1) * NODES)
            proj_ref[part, :, lanes] = dot(place, share_ref[part, :ROWS, lanes]).astype(BF16)
        local_ref[part] = dot(scaled[part], proj_ref[part])
    for copy in copies:
        copy.wait()
    add_local(me, v_ref, held_ref, local_ref)
    add_faces(place_ref, got_ref, near_ref, scaled, local_ref)
    gain, _ = factors[0]
    new = []
    for part in range(GROUP):
        new.append(((local_ref[part] - CENTER * v_ref[part].astype(F32)) * gain).astype(BF16))
        next_ref[part] = new[part]
    write_message(me, new, held_ref, proj_ref, edge_ref, message_ref)


def step_kernel(degree, factors, place_ref, coup_ref, got_ref, *refs):
    last = degree == DEGREE - 1
    hams, refs = refs[:GROUP], refs[GROUP:]
    v_ref, old_ref, proj_ref, near_ref, atoms_ref = refs[:5]
    refs = refs[5:]
    if last:
        occ_ref, density_ref, *next_refs = refs[: 2 + GROUP]
        refs = refs[2 + GROUP :]
    else:
        next_ref, message_ref = refs[:2]
        refs = refs[2:]
    local_ref, held_ref, edge_ref, sems = refs
    piece = v_ref.shape[1]
    me = place_ref[0]
    copies = fetch_hams(hams, held_ref, sems)
    scaled = sum_coefs(place_ref, coup_ref, got_ref, atoms_ref)
    for part in range(GROUP):
        local_ref[part] = dot(scaled[part], proj_ref[part])
    for copy in copies:
        copy.wait()
    add_local(me, v_ref, held_ref, local_ref)
    add_faces(place_ref, got_ref, near_ref, scaled, local_ref)

    gain, back = factors[degree]
    if not last:
        new = []
        for part in range(GROUP):
            now = v_ref[part].astype(F32)
            image = (local_ref[part] - CENTER * now) * gain - back * old_ref[part].astype(F32)
            new.append(image.astype(BF16))
            next_ref[part] = new[part]
        write_message(me, new, held_ref, proj_ref, edge_ref, message_ref)
        return
    weight = jnp.broadcast_to(pick(occ_ref[...], me), (8, piece))
    for r in range(GROUP):
        part = jnp.bitwise_xor(me, r)
        now = v_ref[part].astype(F32)
        image = (local_ref[part] - CENTER * now) * gain - back * old_ref[part].astype(F32)
        image = image.astype(BF16)
        next_refs[r][...] = image
        values = image.astype(F32)
        sums = jnp.dot(
            weight, values * values, precision=lax.Precision.HIGHEST, preferred_element_type=F32
        )[:1]
        for k in range(PART // LANES):
            tile = sums[:, k * LANES : (k + 1) * LANES]
            density_ref[part, 2 * k : 2 * k + 1, :] = tile[:, :FACE]
            density_ref[part, 2 * k + 1 : 2 * k + 2, :] = tile[:, FACE:]


def join_kernel(place_ref, *refs):
    ins, (out_ref, sems) = refs[:GROUP], refs[GROUP:]
    piece = ins[0].shape[0]
    copies = []
    for r in range(GROUP):
        start = pl.multiple_of(jnp.bitwise_xor(place_ref[0], r) * piece, 16)
        copies.append(
            pltpu.make_async_copy(ins[r], out_ref.at[pl.ds(start, piece), :], sems.at[r])
        )
    for copy in copies:
        copy.start()
    for copy in copies:
        copy.wait()


def vmem():
    return pl.BlockSpec(memory_space=pltpu.VMEM)


def hbm():
    return pl.BlockSpec(memory_space=pltpu.HBM)


def smem():
    return pl.BlockSpec(memory_space=pltpu.SMEM)


def shape(dims, dtype=BF16):
    return jax.ShapeDtypeStruct(dims, dtype)


def shards(interpret, states, cell_ham, projectors, slot_atom, coupling, occupancy):
    width = states.shape[1]
    piece = width // GROUP
    y_hi = lax.axis_size("yh")
    spread = lax.axis_size("x") * y_hi

    def call(kernel, megabytes=32, **kw):
        params = pltpu.CompilerParams(vmem_limit_bytes=megabytes * 1024 * 1024)
        return pl.pallas_call(kernel, compiler_params=params, interpret=interpret, **kw)

    me = 2 * lax.axis_index("yl") + lax.axis_index("c")
    place = jnp.stack([me, lax.axis_index("z")]).astype(jnp.int32)
    coup = jnp.tile(coupling, (1, LANES // NPROJ + 1))[:, :LANES]
    occ = occupancy.reshape(GROUP, piece)
    near = ("yl", "c")

    dma = pltpu.SemaphoreType.DMA

    swap = [(0, 1), (1, 0)]
    ring = 2 * y_hi
    spot = lambda y, core: ((y % 2) * 2 + core) * y_hi + y // 2
    across = [(spot(y, c), spot((y + 1 - 2 * c) % ring, c)) for y in range(ring) for c in (0, 1)]
    ham_y = lax.ppermute(cell_ham, ("yl", "c", "yh"), across)
    hams = [cell_ham, lax.ppermute(cell_ham, "c", swap), ham_y, lax.ppermute(ham_y, "c", swap)]

    v_t = states.T
    opened = call(
        open_kernel,
        megabytes=60,
        out_shape=shape((GROUP, piece, 4 * LANES)),
        in_specs=[smem()] + [hbm()] * 3,
        out_specs=vmem(),
        scratch_shapes=[
            pltpu.VMEM((width, PART), BF16),
            pltpu.VMEM((2, LANES, NODES), BF16),
            pltpu.VMEM((2, ROWS, NODES), BF16),
            dma((4,)),
        ],
    )(slot_atom, v_t, cell_ham, projectors)
    opened = lax.all_to_all(opened, near, 0, 0)
    shares = call(
        share_kernel,
        megabytes=60,
        out_shape=shape((GROUP, SHARE, PART)),
        in_specs=[hbm(), hbm()],
        out_specs=vmem(),
        scratch_shapes=[pltpu.VMEM((2, ROWS, NODES), BF16), dma((GROUP + 1,))],
    )(v_t, projectors)
    message = call(
        pack_kernel,
        out_shape=shape((piece, 7 * LANES)),
        in_specs=[vmem()],
        out_specs=vmem(),
    )(opened)
    shares = lax.all_to_all(shares, near, 0, 0)

    factors = chebyshev_factors()
    state_shape = shape((GROUP, piece, PART))
    message_shape = shape((piece, 5 * LANES))
    scratch = [
        pltpu.VMEM((GROUP, piece, PART), F32),
        pltpu.VMEM((2 * GROUP, NODES, NODES), BF16),
        pltpu.VMEM((LANES, PART), BF16),
    ]
    got = lax.all_gather(message, "z")
    v, message, old, *kept = call(
        functools.partial(first_kernel, factors),
        out_shape=[
            state_shape,
            message_shape,
            state_shape,
            shape((GROUP, LANES, PART)),
            shape((2, LANES, LANES)),
            shape((LANES, GROUP * LANES), F32),
        ],
        in_specs=[smem()] + [vmem()] * 2 + [hbm()] * (GROUP + 1),
        out_specs=[vmem()] * 6,
        scratch_shapes=scratch
        + [pltpu.VMEM((GROUP, SHARE - piece, PART), BF16), dma((4 * GROUP,))],
    )(place, coup, got, *hams, shares)
    for degree in range(1, DEGREE):
        got = lax.all_gather(message, "z")
        last = degree == DEGREE - 1
        outs = [state_shape, message_shape]
        if last:
            outs = [shape((GROUP, PART // FACE, FACE), F32)] + [shape((piece, PART))] * GROUP
        ends = [occ] if last else []
        result = call(
            functools.partial(step_kernel, degree, factors),
            out_shape=outs,
            in_specs=[smem()] + [vmem()] * 2 + [hbm()] * GROUP + [vmem()] * (5 + len(ends)),
            out_specs=[vmem()] * len(outs),
            scratch_shapes=scratch + [dma((2 * GROUP,))],
        )(place, coup, got, *hams, v, old, *kept, *ends)
        old, v, message = v, result[0], result[1]

    density, *pieces = result
    pieces = [pieces[0]] + [
        lax.ppermute(pieces[r], near, [(k, k ^ r) for k in range(GROUP)]) for r in (1, 2, 3)
    ]
    filtered = call(
        join_kernel,
        out_shape=shape((width, PART)),
        in_specs=[smem()] + [hbm()] * GROUP,
        out_specs=hbm(),
        scratch_shapes=[dma((GROUP,))],
    )(place, *pieces)
    parts = GROUP * spread
    terms = lax.all_to_all(
        density.reshape(parts, GROUP * PART // parts), near + ("x", "yh"), 0, 0, tiled=True
    )
    density = jnp.sum(terms, axis=0) / (width * spread)
    return filtered.T, density


def build(mesh, interpret=False):
    part = ("z", "yl", "c")
    group = ("x", "yh")
    return jax.shard_map(
        functools.partial(shards, interpret),
        mesh=mesh,
        in_specs=(
            P(part, group),
            P(part, None, None),
            P(part, None, None),
            P(part, None),
            P(),
            P(group),
        ),
        out_specs=(P(part, group), P(part + group)),
        check_vma=False,
    )


def solution(mesh):
    count, groups = mesh.shape["mesh"], mesh.shape["state"]
    devices = mesh.devices.reshape(count // GROUP, 2, 2, groups // 4, 4)
    return build(Mesh(devices, ("z", "yl", "c", "x", "yh")))
```

```python
import functools

import jax
import jax.numpy as jnp
from jax import lax
from jax.experimental import pallas as pl
from jax.experimental.pallas import tpu as pltpu
from jax.sharding import Mesh, PartitionSpec as P

FACE = 64
DEGREE = 4
LANES = 128
NODES = 512
NPROJ = 18
SLOTS = 4
ROWS = SLOTS * NPROJ
GROUP = 4
PART = 2 * NODES
PIECE = 48
BLOCKS = 8
PROJ = NPROJ * BLOCKS
SPAN = NPROJ * PIECE
WIDE = 7 * LANES
BODY = GROUP * BLOCKS
PADDED = 80
PACK = PART + 2 * PADDED
HEAD = 32
CENTER = 0.5
HALF_WIDTH = 1.5
LOW_EDGE = -1.2

BF16 = jnp.bfloat16
F32 = jnp.float32
NT = (((1,), (1,)), ((), ()))
TN = (((0,), (0,)), ((), ()))


def chebyshev_factors():
    sigma = HALF_WIDTH / (LOW_EDGE - CENTER)
    gamma = 2.0 / sigma
    factors = [(sigma / HALF_WIDTH, 0.0)]
    for _ in range(1, DEGREE):
        sigma_new = 1.0 / (gamma - sigma)
        factors.append((2.0 * sigma_new / HALF_WIDTH, sigma * sigma_new))
        sigma = sigma_new
    return factors


def iota(shape, dim):
    return lax.broadcasted_iota(jnp.int32, shape, dim)


def dot(a, b):
    return jnp.dot(a, b, preferred_element_type=F32)


def dot_nt(a, b):
    return lax.dot_general(a, b, NT, preferred_element_type=F32)


def dot_tn(a, b):
    return lax.dot_general(a, b, TN, preferred_element_type=F32)


def exact(a, b):
    return jnp.dot(a, b, precision=lax.Precision.HIGHEST, preferred_element_type=F32)


def placers():
    row = iota((PROJ, ROWS), 0)
    col = iota((PROJ, ROWS), 1)
    which = row // BLOCKS
    block = row % BLOCKS
    first = (block < SLOTS) & (col == block * NPROJ + which)
    slot = block - SLOTS + 1
    second = ((block == 0) & (col == which)) | (
        (block >= SLOTS) & (block < 2 * SLOTS - 1) & (col == slot * NPROJ + which)
    )
    return first.astype(F32).astype(BF16), second.astype(F32).astype(BF16)


def low_lanes(rows):
    return iota((rows, LANES), 1) < FACE


def pick(rows, at):
    return jnp.sum(jnp.where(iota(rows.shape, 0) == at, rows, 0.0), axis=0, keepdims=True)


def run(copies):
    for copy in copies:
        copy.start()
    return copies


def finish(copies):
    for copy in copies:
        copy.wait()


def tile(k):
    return slice(k * LANES, (k + 1) * LANES)


def eight(k):
    return slice(k * 8, (k + 1) * 8)


def open_kernel(atom_ref, v_hbm, ham_hbm, proj_hbm, out_ref, v_ref, ham_ref, proj_ref, wide_ref, sems):
    copies = run(
        [
            pltpu.make_async_copy(v_hbm, v_ref, sems.at[0]),
            pltpu.make_async_copy(proj_hbm, proj_ref, sems.at[1]),
            pltpu.make_async_copy(ham_hbm.at[0, :LANES, :], ham_ref.at[0], sems.at[2]),
            pltpu.make_async_copy(ham_hbm.at[1, NODES - LANES :, :], ham_ref.at[1], sems.at[3]),
        ]
    )
    place0, place1 = placers()
    wide_ref[...] = jnp.zeros(wide_ref.shape, F32)
    lane = iota((8, LANES), 1)
    atoms = jnp.full((8, LANES), -1, jnp.int32)
    for block in range(2 * SLOTS - 1):
        cell, slot = (0, block) if block < SLOTS else (1, block - SLOTS + 1)
        atoms = jnp.where(lane == block, atom_ref[cell, slot], atoms)
    atoms = atoms.astype(F32)
    finish(copies)
    width = v_ref.shape[0]
    p0 = dot(place0, proj_ref[0]).astype(BF16)
    p1 = dot(place1, proj_ref[1]).astype(BF16)
    v0 = v_ref[:, :NODES]
    v1 = v_ref[:, NODES:]
    coef = dot_nt(p0, v0) + dot_nt(p1, v1)
    face = jnp.where(low_lanes(width), dot_nt(v0, ham_ref[0]), dot_nt(v1, ham_ref[1]))
    edge = jnp.where(
        low_lanes(ROWS),
        proj_ref[0, :, :LANES].astype(F32),
        proj_ref[1, :, NODES - LANES :].astype(F32),
    )
    for to in range(GROUP):
        for i in range(NPROJ):
            wide_ref[to, :8, i * PIECE : (i + 1) * PIECE] = coef[
                eight(i), to * PIECE : (to + 1) * PIECE
            ]
        for k in range(PIECE // 8):
            wide_ref[to, 8:16, tile(k)] = face[eight(to * (PIECE // 8) + k)]
        wide_ref[to, 8:16, tile(6)] = atoms
        for k in range(8):
            wide_ref[to, 16:24, tile(k)] = edge[eight(k)]
        wide_ref[to, 24:32, :LANES] = edge[eight(8)]
        out_ref[to, :HEAD, :] = wide_ref[to].astype(BF16)
        out_ref[to, HEAD:, :] = v_ref[to * PIECE : (to + 1) * PIECE, :]


def share_kernel(ham_hbm, proj_hbm, out, proj_ref, pad_ref, sems):
    hams = run(
        [
            pltpu.make_async_copy(ham_hbm.at[k], out.at[pl.ds(k * NODES, NODES), :], sems.at[k])
            for k in range(2)
        ]
    )
    proj_in = run([pltpu.make_async_copy(proj_hbm, proj_ref, sems.at[2])])
    finish(proj_in)
    pad = jnp.zeros((PADDED - ROWS, NODES), BF16)
    for k in range(2):
        pad_ref[k * PADDED : (k + 1) * PADDED, :] = jnp.concatenate([proj_ref[k], pad], axis=0)
    projs = run([pltpu.make_async_copy(pad_ref, out.at[pl.ds(PART, 2 * PADDED), :], sems.at[3])])
    finish(hams + projs)


def place_face(face, wide_ref):
    wide_ref[:BODY, WIDE:] = face[:BODY]
    for k in range(PIECE - BODY):
        row = (k % GROUP) * BLOCKS + BLOCKS - 1
        wide_ref[row : row + 1, tile(k // GROUP)] = face[BODY + k : BODY + k + 1]


def read_face(got_ref, group):
    body = got_ref[group, :BODY, :].astype(F32)
    rows = [body[:, WIDE:]]
    for k in range(PIECE - BODY):
        row = (k % GROUP) * BLOCKS + BLOCKS - 1
        rows.append(body[row : row + 1, tile(k // GROUP)])
    return jnp.concatenate(rows, axis=0)


def pack_kernel(in_ref, out_ref, wide_ref):
    last = GROUP - 1
    low = low_lanes(8)
    wide_ref[...] = jnp.zeros(wide_ref.shape, F32)
    pieces = [in_ref[part, :HEAD, :].astype(F32) for part in range(GROUP)]
    both = lambda rows, k: jnp.where(low, pieces[0][rows, tile(k)], pieces[last][rows, tile(k)])
    lane = iota((8, LANES), 1)
    atoms = jnp.full((8, LANES), -1.0, F32)
    for part in range(GROUP):
        wide_ref[eight(part), :WIDE] = pieces[part][:8, :WIDE]
        own = pieces[part][8:16, tile(6)]
        if part:
            own = pltpu.roll(own, part * BLOCKS, 1)
        atoms = jnp.where(lane // BLOCKS == part, own, atoms)
    face = jnp.concatenate([both(slice(8, 16), k) for k in range(PIECE // 8)], axis=0)
    place_face(face, wide_ref)
    ninth = both(slice(24, 32), 0)
    for k in range(8):
        wide_ref[BODY:, tile(k)] = both(slice(16, 24), k)
        row = (k % GROUP) * BLOCKS + BLOCKS - 1
        wide_ref[row : row + 1, tile(4 + k // GROUP)] = ninth[k : k + 1]
    wide_ref[BLOCKS - 1 : BLOCKS, tile(6)] = atoms[:1]
    out_ref[...] = wide_ref[...].astype(BF16)


def beside(place_ref, groups):
    z = place_ref[1]
    return z, jnp.maximum(z - 1, 0), jnp.minimum(z + 1, groups - 1)


def choose(place_ref, coupling_ref, got_ref, pick_ref, factor_ref):
    groups = got_ref.shape[0]
    z, below, above = beside(place_ref, groups)
    lane = iota((8, LANES), 1)
    named = lambda group: jnp.broadcast_to(
        got_ref[group, :16, tile(6)].astype(F32)[BLOCKS - 1 : BLOCKS], (8, LANES)
    )
    shift = lambda x, by: pltpu.roll(x, by, 1) if by else x
    per = LANES // BODY
    tiles = []
    for start in range(0, groups, per):
        x = jnp.full((8, LANES), -1.0, F32)
        for k in range(min(per, groups - start)):
            x = jnp.where(lane // BODY == k, shift(named(start + k), k * BODY), x)
        tiles.append(x)
    mine = jnp.where(lane < BODY, named(z), -1.0)
    mine = jnp.where(lane // BLOCKS == GROUP, shift(named(below), BLOCKS), mine)
    mine = jnp.where(lane // BLOCKS == GROUP + 1, shift(named(above), BODY + BLOCKS), mine)
    mine = jnp.where(mine < 0, -2.0, mine)
    column = jnp.transpose(jnp.concatenate([mine] * (LANES // 8), axis=0))[:PIECE]
    for k, x in enumerate(tiles):
        match = column == jnp.concatenate([x] * (PIECE // 8), axis=0)
        pick_ref[:, tile(k)] = jnp.where(match, 1.0, 0.0).astype(BF16)
    count = coupling_ref.shape[0]
    atom = iota((PIECE, LANES), 1).astype(F32)
    owner = jnp.where(column == atom, 1.0, 0.0)[:, :count]
    expand = jnp.where(iota((NPROJ, WIDE), 1) // PIECE == iota((NPROJ, WIDE), 0), 1.0, 0.0)
    factor_ref[...] = exact(exact(owner, coupling_ref[...]), expand)


def sum_coefs(got_ref, pick_ref, factor_ref, scaled_ref):
    groups = got_ref.shape[0]
    blocks = jnp.concatenate([got_ref[group, :BODY, :WIDE] for group in range(groups)], axis=0)
    total = dot(pick_ref[:, : groups * BODY], blocks) * factor_ref[...]
    for i in range(NPROJ):
        column = total[:, i * PIECE : (i + 1) * PIECE]
        for k in range(GROUP + 2):
            scaled_ref[k, eight(i), :] = column[eight(k)]
    return [scaled_ref[k].astype(BF16) for k in range(GROUP + 2)]


def add_faces(place_ref, got_ref, near_ref, scaled, local_ref):
    groups = got_ref.shape[0]
    z, below, above = beside(place_ref, groups)
    low = low_lanes(PIECE)
    from_below = read_face(got_ref, below) + dot_tn(scaled[GROUP], near_ref[0])
    from_above = read_face(got_ref, above) + dot_tn(scaled[GROUP + 1], near_ref[1])
    from_below = from_below * (z > 0).astype(F32)
    from_above = from_above * (z < groups - 1).astype(F32)
    cells = [(part, cell * NODES) for part in range(GROUP) for cell in range(2)]
    heads = [local_ref[part, :, a : a + LANES] for part, a in cells]
    tails = [local_ref[part, :, a + NODES - LANES : a + NODES] for part, a in cells]
    for k, (part, a) in enumerate(cells):
        under = tails[k - 1] if k > 0 else from_below
        over = heads[k + 1] if k + 1 < len(cells) else from_above
        local_ref[part, :, a : a + LANES] = heads[k] + jnp.where(
            low, pltpu.roll(under, FACE, 1), 0.0
        )
        local_ref[part, :, a + NODES - LANES : a + NODES] = tails[k] + jnp.where(
            low, 0.0, pltpu.roll(over, FACE, 1)
        )


def fetch_hams(packs, held_ref, sems):
    return run(
        [
            pltpu.make_async_copy(
                packs[k // 2].at[pl.ds((k % 2) * NODES, NODES), :], held_ref.at[k], sems.at[k]
            )
            for k in range(2 * GROUP)
        ]
    )


def add_local(me, v_ref, held_ref, local_ref):
    for r in range(GROUP):
        part = jnp.bitwise_xor(me, r)
        for cell in range(2):
            lanes = slice(cell * NODES, (cell + 1) * NODES)
            local_ref[part, :, lanes] += dot_nt(v_ref[part, :, lanes], held_ref[2 * r + cell])


def write_message(me, new, held_ref, proj_ref, edge_ref, wide_ref, message_ref):
    for r in range(GROUP):
        part = jnp.bitwise_xor(me, r)

        @pl.when(part == 0)
        def _():
            edge_ref[:FACE, :NODES] = held_ref[2 * r, :FACE, :]
            edge_ref[:FACE, NODES:] = jnp.zeros((FACE, NODES), BF16)

        @pl.when(part == GROUP - 1)
        def _():
            edge_ref[FACE:, :NODES] = jnp.zeros((FACE, NODES), BF16)
            edge_ref[FACE:, NODES:] = held_ref[2 * r + 1, NODES - FACE :, :]

    ends = jnp.concatenate([new[0][:, :NODES], new[GROUP - 1][:, NODES:]], axis=1)
    face = dot_nt(ends, edge_ref[...])
    wide_ref[:, SPAN:WIDE] = jnp.zeros((BODY, WIDE - SPAN), F32)
    for part in range(GROUP):
        coef = dot_nt(proj_ref[part], new[part])
        for i in range(NPROJ):
            wide_ref[eight(part), i * PIECE : (i + 1) * PIECE] = coef[eight(i)]
    place_face(face, wide_ref)
    message_ref[...] = wide_ref[...].astype(BF16)


def first_kernel(factors, place_ref, coupling_ref, got_ref, open_hbm, *refs):
    packs, refs = refs[:GROUP], refs[GROUP:]
    next_ref, message_ref, v_ref, proj_ref, near_ref, pick_ref, factor_ref = refs[:7]
    local_ref, held_ref, edge_ref, wide_ref, scaled_ref, raw_ref, sems = refs[7:]
    groups = got_ref.shape[0]
    me = place_ref[0]
    _, below, above = beside(place_ref, groups)
    copies = []
    for r in range(GROUP):
        at = 2 * GROUP + 2 * r
        copies += [
            pltpu.make_async_copy(packs[r].at[pl.ds(PART, 2 * PADDED), :], raw_ref.at[r], sems.at[at]),
            pltpu.make_async_copy(
                open_hbm.at[r, pl.ds(HEAD, PIECE), :], v_ref.at[r], sems.at[at + 1]
            ),
        ]
    run(copies)
    hams = fetch_hams(packs, held_ref, sems)

    place0, place1 = placers()
    for k, group, place in ((0, below, place1), (1, above, place0)):
        rows = got_ref[group].astype(F32)
        raw = [rows[BODY:, tile(j)] for j in range(8)]
        for j in range(8):
            row = (j % GROUP) * BLOCKS + BLOCKS - 1
            raw.append(rows[row : row + 1, tile(4 + j // GROUP)])
        near_ref[k] = dot(place, jnp.concatenate(raw, axis=0).astype(BF16)).astype(BF16)
    choose(place_ref, coupling_ref, got_ref, pick_ref, factor_ref)
    scaled = sum_coefs(got_ref, pick_ref, factor_ref, scaled_ref)

    finish(copies)
    for r in range(GROUP):
        part = jnp.bitwise_xor(me, r)
        for cell, place in ((0, place0), (1, place1)):
            raw = raw_ref[r, cell * PADDED : (cell + 1) * PADDED, :][:ROWS]
            lanes = slice(cell * NODES, (cell + 1) * NODES)
            proj_ref[part, :, lanes] = dot(place, raw).astype(BF16)
    for part in range(GROUP):
        local_ref[part] = dot_tn(scaled[part], proj_ref[part])
    finish(hams)
    add_local(me, v_ref, held_ref, local_ref)
    add_faces(place_ref, got_ref, near_ref, scaled, local_ref)
    gain, _ = factors[0]
    new = []
    for part in range(GROUP):
        new.append(((local_ref[part] - CENTER * v_ref[part].astype(F32)) * gain).astype(BF16))
        next_ref[part] = new[part]
    write_message(me, new, held_ref, proj_ref, edge_ref, wide_ref, message_ref)


def step_kernel(degree, factors, place_ref, got_ref, *refs):
    last = degree == DEGREE - 1
    packs, refs = refs[:GROUP], refs[GROUP:]
    v_ref, old_ref, proj_ref, near_ref, pick_ref, factor_ref = refs[:6]
    refs = refs[6:]
    if last:
        occ_ref, density_ref, *next_refs = refs[: 2 + GROUP]
        refs = refs[2 + GROUP :]
    else:
        next_ref, message_ref = refs[:2]
        refs = refs[2:]
    local_ref, held_ref, edge_ref, wide_ref, scaled_ref, sems = refs
    me = place_ref[0]
    hams = fetch_hams(packs, held_ref, sems)
    scaled = sum_coefs(got_ref, pick_ref, factor_ref, scaled_ref)
    for part in range(GROUP):
        local_ref[part] = dot_tn(scaled[part], proj_ref[part])
    finish(hams)
    add_local(me, v_ref, held_ref, local_ref)
    add_faces(place_ref, got_ref, near_ref, scaled, local_ref)

    gain, back = factors[degree]

    def image(part):
        now = v_ref[part].astype(F32)
        value = (local_ref[part] - CENTER * now) * gain - back * old_ref[part].astype(F32)
        return value.astype(BF16)

    if not last:
        new = [image(part) for part in range(GROUP)]
        for part in range(GROUP):
            next_ref[part] = new[part]
        write_message(me, new, held_ref, proj_ref, edge_ref, wide_ref, message_ref)
        return
    weight = jnp.transpose(jnp.broadcast_to(pick(occ_ref[...], me), (LANES, LANES)))[:PIECE]
    for r in range(GROUP):
        part = jnp.bitwise_xor(me, r)
        new = image(part)
        next_refs[r][...] = new
        values = new.astype(F32)
        for k in range(PART // LANES):
            term = values[:, tile(k)]
            sums = jnp.sum(term * term * weight, axis=0, keepdims=True)
            density_ref[part, 2 * k : 2 * k + 1, :] = sums[:, :FACE]
            density_ref[part, 2 * k + 1 : 2 * k + 2, :] = sums[:, FACE:]


def join_kernel(place_ref, *refs):
    ins, (out_ref, sems) = refs[:GROUP], refs[GROUP:]
    copies = []
    for r in range(GROUP):
        start = pl.multiple_of(jnp.bitwise_xor(place_ref[0], r) * PIECE, 16)
        copies.append(
            pltpu.make_async_copy(ins[r], out_ref.at[pl.ds(start, PIECE), :], sems.at[r])
        )
    run(copies)
    finish(copies)


def vmem():
    return pl.BlockSpec(memory_space=pltpu.VMEM)


def hbm():
    return pl.BlockSpec(memory_space=pltpu.HBM)


def smem():
    return pl.BlockSpec(memory_space=pltpu.SMEM)


def shape(dims, dtype=BF16):
    return jax.ShapeDtypeStruct(dims, dtype)


def shards(interpret, states, cell_ham, projectors, slot_atom, coupling, occupancy):
    width = states.shape[1]
    groups = lax.axis_size("z")
    spread = lax.axis_size("x") * lax.axis_size("yh")
    dma = pltpu.SemaphoreType.DMA
    near = ("yl", "c")
    ring = 2 * lax.axis_size("yh")

    def call(kernel, megabytes=24, **kw):
        params = pltpu.CompilerParams(vmem_limit_bytes=megabytes * 1024 * 1024)
        return pl.pallas_call(kernel, compiler_params=params, interpret=interpret, **kw)

    me = 2 * lax.axis_index("yl") + lax.axis_index("c")
    place = jnp.stack([me, lax.axis_index("z")]).astype(jnp.int32)
    occ = jnp.pad(occupancy.reshape(GROUP, PIECE), ((0, 0), (0, LANES - PIECE)))
    v_t = states.T
    opened = call(
        open_kernel,
        megabytes=60,
        out_shape=shape((GROUP, HEAD + PIECE, PART)),
        in_specs=[smem()] + [hbm()] * 3,
        out_specs=vmem(),
        scratch_shapes=[
            pltpu.VMEM((width, PART), BF16),
            pltpu.VMEM((2, LANES, NODES), BF16),
            pltpu.VMEM((2, ROWS, NODES), BF16),
            pltpu.VMEM((GROUP, HEAD, PART), F32),
            dma((4,)),
        ],
    )(slot_atom, v_t, cell_ham, projectors)
    opened = lax.all_to_all(opened, near, 0, 0)
    pack = call(
        share_kernel,
        megabytes=60,
        out_shape=shape((PACK, NODES)),
        in_specs=[hbm()] * 2,
        out_specs=hbm(),
        scratch_shapes=[
            pltpu.VMEM((2, ROWS, NODES), BF16),
            pltpu.VMEM((2 * PADDED, NODES), BF16),
            dma((4,)),
        ],
    )(cell_ham, projectors)
    message = call(
        pack_kernel,
        out_shape=shape((BODY + 8, PART)),
        in_specs=[vmem()],
        out_specs=vmem(),
        scratch_shapes=[pltpu.VMEM((BODY + 8, PART), F32)],
    )(opened)
    spot = lambda y, core: ((y % 2) * 2 + core) * (ring // 2) + y // 2

    def across(flip):
        return [
            (spot(y, c), spot((y + 1 - 2 * c) % ring, c ^ flip)) for y in range(ring) for c in (0, 1)
        ]

    beside_core = lax.ppermute(pack, "c", [(0, 1), (1, 0)])
    late, message = lax.optimization_barrier((pack, message))
    axes = ("yl", "c", "yh")
    packs = [
        pack,
        beside_core,
        lax.ppermute(late, axes, across(0)),
        lax.ppermute(late, axes, across(1)),
    ]

    factors = chebyshev_factors()
    state_shape = shape((GROUP, PIECE, PART))
    message_shape = shape((BODY, PART))
    scratch = [
        pltpu.VMEM((GROUP, PIECE, PART), F32),
        pltpu.VMEM((2 * GROUP, NODES, NODES), BF16),
        pltpu.VMEM((LANES, PART), BF16),
        pltpu.VMEM((BODY, PART), F32),
        pltpu.VMEM((GROUP + 2, PROJ, PIECE), F32),
    ]
    got = lax.all_gather(message, "z")
    v, message, old, *kept = call(
        functools.partial(first_kernel, factors),
        out_shape=[
            state_shape,
            message_shape,
            state_shape,
            shape((GROUP, PROJ, PART)),
            shape((2, PROJ, LANES)),
            shape((PIECE, -(-groups * BODY // LANES) * LANES)),
            shape((PIECE, WIDE), F32),
        ],
        in_specs=[smem()] + [vmem()] * 2 + [hbm()] * (GROUP + 1),
        out_specs=[vmem()] * 7,
        scratch_shapes=scratch
        + [pltpu.VMEM((GROUP, 2 * PADDED, NODES), BF16), dma((4 * GROUP,))],
    )(place, coupling, got, opened, *packs)
    for degree in range(1, DEGREE):
        got = lax.all_gather(message, "z")
        last = degree == DEGREE - 1
        outs = [state_shape, message_shape]
        if last:
            outs = [shape((GROUP, PART // FACE, FACE), F32)] + [shape((PIECE, PART))] * GROUP
        ends = [occ] if last else []
        result = call(
            functools.partial(step_kernel, degree, factors),
            out_shape=outs,
            in_specs=[smem(), vmem()] + [hbm()] * GROUP + [vmem()] * (6 + len(ends)),
            out_specs=[vmem()] * len(outs),
            scratch_shapes=scratch + [dma((2 * GROUP,))],
        )(place, got, *packs, v, old, *kept, *ends)
        old, v, message = v, result[0], result[1]

    density, *pieces = result
    pieces = [pieces[0]] + [
        lax.ppermute(pieces[r], near, [(k, k ^ r) for k in range(GROUP)]) for r in (1, 2, 3)
    ]
    filtered = call(
        join_kernel,
        out_shape=shape((width, PART)),
        in_specs=[smem()] + [hbm()] * GROUP,
        out_specs=hbm(),
        scratch_shapes=[dma((GROUP,))],
    )(place, *pieces)
    parts = GROUP * spread
    terms = lax.all_to_all(
        density.reshape(parts, GROUP * PART // parts), near + ("x", "yh"), 0, 0, tiled=True
    )
    density = jnp.sum(terms, axis=0) / (width * spread)
    return filtered.T, density


def build(mesh, interpret=False):
    part = ("z", "yl", "c")
    group = ("x", "yh")
    return jax.shard_map(
        functools.partial(shards, interpret),
        mesh=mesh,
        in_specs=(
            P(part, group),
            P(part, None, None),
            P(part, None, None),
            P(part, None),
            P(),
            P(group),
        ),
        out_specs=(P(part, group), P(part + group)),
        check_vma=False,
    )


def solution(mesh):
    count, groups = mesh.shape["mesh"], mesh.shape["state"]
    devices = mesh.devices.reshape(count // GROUP, 2, 2, groups // 4, 4)
    return build(Mesh(devices, ("z", "yl", "c", "x", "yh")))
```

```python
import functools

import jax
import jax.numpy as jnp
from jax import lax
from jax.experimental import pallas as pl
from jax.experimental.pallas import tpu as pltpu
from jax.sharding import Mesh, PartitionSpec as P

FACE = 64
DEGREE = 4
LANES = 128
NODES = 512
NPROJ = 18
SLOTS = 4
ROWS = SLOTS * NPROJ
GROUP = 4
PART = 2 * NODES
PIECE = 48
BLOCKS = 8
PROJ = NPROJ * BLOCKS
SPAN = NPROJ * PIECE
WIDE = 7 * LANES
BODY = GROUP * BLOCKS
PADDED = 80
PACK = PART + 2 * PADDED
HEAD = 32
CENTER = 0.5
HALF_WIDTH = 1.5
LOW_EDGE = -1.2

BF16 = jnp.bfloat16
F32 = jnp.float32
NT = (((1,), (1,)), ((), ()))
TN = (((0,), (0,)), ((), ()))


def chebyshev_factors():
    sigma = HALF_WIDTH / (LOW_EDGE - CENTER)
    gamma = 2.0 / sigma
    factors = [(sigma / HALF_WIDTH, 0.0)]
    for _ in range(1, DEGREE):
        sigma_new = 1.0 / (gamma - sigma)
        factors.append((2.0 * sigma_new / HALF_WIDTH, sigma * sigma_new))
        sigma = sigma_new
    return factors


def iota(shape, dim):
    return lax.broadcasted_iota(jnp.int32, shape, dim)


def dot(a, b):
    return jnp.dot(a, b, preferred_element_type=F32)


def dot_nt(a, b):
    return lax.dot_general(a, b, NT, preferred_element_type=F32)


def dot_tn(a, b):
    return lax.dot_general(a, b, TN, preferred_element_type=F32)


def exact(a, b):
    return jnp.dot(a, b, precision=lax.Precision.HIGHEST, preferred_element_type=F32)


def placers():
    row = iota((PROJ, ROWS), 0)
    col = iota((PROJ, ROWS), 1)
    which = row // BLOCKS
    block = row % BLOCKS
    first = (block < SLOTS) & (col == block * NPROJ + which)
    slot = block - SLOTS + 1
    second = ((block == 0) & (col == which)) | (
        (block >= SLOTS) & (block < 2 * SLOTS - 1) & (col == slot * NPROJ + which)
    )
    return first.astype(F32).astype(BF16), second.astype(F32).astype(BF16)


def low_lanes(rows):
    return iota((rows, LANES), 1) < FACE


def pick(rows, at):
    return jnp.sum(jnp.where(iota(rows.shape, 0) == at, rows, 0.0), axis=0, keepdims=True)


def run(copies):
    for copy in copies:
        copy.start()
    return copies


def finish(copies):
    for copy in copies:
        copy.wait()


def tile(k):
    return slice(k * LANES, (k + 1) * LANES)


def eight(k):
    return slice(k * 8, (k + 1) * 8)


def open_kernel(atom_ref, v_hbm, ham_hbm, proj_hbm, out_ref, v_ref, ham_ref, proj_ref, wide_ref, sems):
    copies = run(
        [
            pltpu.make_async_copy(v_hbm, v_ref, sems.at[0]),
            pltpu.make_async_copy(proj_hbm, proj_ref, sems.at[1]),
            pltpu.make_async_copy(ham_hbm.at[0, :LANES, :], ham_ref.at[0], sems.at[2]),
            pltpu.make_async_copy(ham_hbm.at[1, NODES - LANES :, :], ham_ref.at[1], sems.at[3]),
        ]
    )
    place0, place1 = placers()
    wide_ref[...] = jnp.zeros(wide_ref.shape, F32)
    lane = iota((8, LANES), 1)
    atoms = jnp.full((8, LANES), -1, jnp.int32)
    for block in range(2 * SLOTS - 1):
        cell, slot = (0, block) if block < SLOTS else (1, block - SLOTS + 1)
        atoms = jnp.where(lane == block, atom_ref[cell, slot], atoms)
    atoms = atoms.astype(F32)
    finish(copies)
    width = v_ref.shape[0]
    p0 = dot(place0, proj_ref[0]).astype(BF16)
    p1 = dot(place1, proj_ref[1]).astype(BF16)
    v0 = v_ref[:, :NODES]
    v1 = v_ref[:, NODES:]
    coef = dot_nt(p0, v0) + dot_nt(p1, v1)
    face = jnp.where(low_lanes(width), dot_nt(v0, ham_ref[0]), dot_nt(v1, ham_ref[1]))
    edge = jnp.where(
        low_lanes(ROWS),
        proj_ref[0, :, :LANES].astype(F32),
        proj_ref[1, :, NODES - LANES :].astype(F32),
    )
    for to in range(GROUP):
        for i in range(NPROJ):
            wide_ref[to, :8, i * PIECE : (i + 1) * PIECE] = coef[
                eight(i), to * PIECE : (to + 1) * PIECE
            ]
        for k in range(PIECE // 8):
            wide_ref[to, 8:16, tile(k)] = face[eight(to * (PIECE // 8) + k)]
        wide_ref[to, 8:16, tile(6)] = atoms
        for k in range(8):
            wide_ref[to, 16:24, tile(k)] = edge[eight(k)]
        wide_ref[to, 24:32, :LANES] = edge[eight(8)]
        out_ref[to, :HEAD, :] = wide_ref[to].astype(BF16)
        out_ref[to, HEAD:, :] = v_ref[to * PIECE : (to + 1) * PIECE, :]


def share_kernel(ham_hbm, proj_hbm, out_ref, proj_ref, sems):
    copies = [
        pltpu.make_async_copy(ham_hbm.at[k], out_ref.at[pl.ds(k * NODES, NODES), :], sems.at[k])
        for k in range(2)
    ]
    copies = run([pltpu.make_async_copy(proj_hbm, proj_ref, sems.at[2])] + copies)
    copies[0].wait()
    pad = jnp.zeros((PADDED - ROWS, NODES), BF16)
    for k in range(2):
        start = PART + k * PADDED
        out_ref[start : start + PADDED, :] = jnp.concatenate([proj_ref[k], pad], axis=0)
    finish(copies[1:])


def place_face(face, wide_ref):
    wide_ref[:BODY, WIDE:] = face[:BODY]
    for k in range(PIECE - BODY):
        row = (k % GROUP) * BLOCKS + BLOCKS - 1
        wide_ref[row : row + 1, tile(k // GROUP)] = face[BODY + k : BODY + k + 1]


def read_face(got_ref, group):
    body = got_ref[group, :BODY, :].astype(F32)
    rows = [body[:, WIDE:]]
    for k in range(PIECE - BODY):
        row = (k % GROUP) * BLOCKS + BLOCKS - 1
        rows.append(body[row : row + 1, tile(k // GROUP)])
    return jnp.concatenate(rows, axis=0)


def pack_kernel(in_ref, out_ref, wide_ref):
    last = GROUP - 1
    low = low_lanes(8)
    wide_ref[...] = jnp.zeros(wide_ref.shape, F32)
    pieces = [in_ref[part, :HEAD, :].astype(F32) for part in range(GROUP)]
    both = lambda rows, k: jnp.where(low, pieces[0][rows, tile(k)], pieces[last][rows, tile(k)])
    lane = iota((8, LANES), 1)
    atoms = jnp.full((8, LANES), -1.0, F32)
    for part in range(GROUP):
        wide_ref[eight(part), :WIDE] = pieces[part][:8, :WIDE]
        own = pieces[part][8:16, tile(6)]
        if part:
            own = pltpu.roll(own, part * BLOCKS, 1)
        atoms = jnp.where(lane // BLOCKS == part, own, atoms)
    face = jnp.concatenate([both(slice(8, 16), k) for k in range(PIECE // 8)], axis=0)
    place_face(face, wide_ref)
    ninth = both(slice(24, 32), 0)
    for k in range(8):
        wide_ref[BODY:, tile(k)] = both(slice(16, 24), k)
        row = (k % GROUP) * BLOCKS + BLOCKS - 1
        wide_ref[row : row + 1, tile(4 + k // GROUP)] = ninth[k : k + 1]
    wide_ref[BLOCKS - 1 : BLOCKS, tile(6)] = atoms[:1]
    out_ref[...] = wide_ref[...].astype(BF16)


def beside(place_ref, groups):
    z = place_ref[1]
    return z, jnp.maximum(z - 1, 0), jnp.minimum(z + 1, groups - 1)


def choose(place_ref, coupling_ref, got_ref, pick_ref, factor_ref):
    groups = got_ref.shape[0]
    z, below, above = beside(place_ref, groups)
    lane = iota((8, LANES), 1)
    named = lambda group: jnp.broadcast_to(
        got_ref[group, :16, tile(6)].astype(F32)[BLOCKS - 1 : BLOCKS], (8, LANES)
    )
    shift = lambda x, by: pltpu.roll(x, by, 1) if by else x
    per = LANES // BODY
    tiles = []
    for start in range(0, groups, per):
        x = jnp.full((8, LANES), -1.0, F32)
        for k in range(min(per, groups - start)):
            x = jnp.where(lane // BODY == k, shift(named(start + k), k * BODY), x)
        tiles.append(x)
    mine = jnp.where(lane < BODY, named(z), -1.0)
    mine = jnp.where(lane // BLOCKS == GROUP, shift(named(below), BLOCKS), mine)
    mine = jnp.where(lane // BLOCKS == GROUP + 1, shift(named(above), BODY + BLOCKS), mine)
    mine = jnp.where(mine < 0, -2.0, mine)
    column = jnp.transpose(jnp.concatenate([mine] * (LANES // 8), axis=0))[:PIECE]
    for k, x in enumerate(tiles):
        match = column == jnp.concatenate([x] * (PIECE // 8), axis=0)
        pick_ref[:, tile(k)] = jnp.where(match, 1.0, 0.0).astype(BF16)
    count = coupling_ref.shape[0]
    atom = iota((PIECE, LANES), 1).astype(F32)
    owner = jnp.where(column == atom, 1.0, 0.0)[:, :count]
    expand = jnp.where(iota((NPROJ, WIDE), 1) // PIECE == iota((NPROJ, WIDE), 0), 1.0, 0.0)
    factor_ref[...] = exact(exact(owner, coupling_ref[...]), expand)


def sum_coefs(got_ref, pick_ref, factor_ref, scaled_ref):
    groups = got_ref.shape[0]
    blocks = jnp.concatenate([got_ref[group, :BODY, :WIDE] for group in range(groups)], axis=0)
    total = dot(pick_ref[:, : groups * BODY], blocks) * factor_ref[...]
    for i in range(NPROJ):
        column = total[:, i * PIECE : (i + 1) * PIECE]
        for k in range(GROUP + 2):
            scaled_ref[k, eight(i), :] = column[eight(k)]
    return [scaled_ref[k].astype(BF16) for k in range(GROUP + 2)]


def add_faces(place_ref, got_ref, near_ref, scaled, local_ref):
    groups = got_ref.shape[0]
    z, below, above = beside(place_ref, groups)
    low = low_lanes(PIECE)
    from_below = read_face(got_ref, below) + dot_tn(scaled[GROUP], near_ref[0])
    from_above = read_face(got_ref, above) + dot_tn(scaled[GROUP + 1], near_ref[1])
    from_below = from_below * (z > 0).astype(F32)
    from_above = from_above * (z < groups - 1).astype(F32)
    cells = [(part, cell * NODES) for part in range(GROUP) for cell in range(2)]
    heads = [local_ref[part, :, a : a + LANES] for part, a in cells]
    tails = [local_ref[part, :, a + NODES - LANES : a + NODES] for part, a in cells]
    for k, (part, a) in enumerate(cells):
        under = tails[k - 1] if k > 0 else from_below
        over = heads[k + 1] if k + 1 < len(cells) else from_above
        local_ref[part, :, a : a + LANES] = heads[k] + jnp.where(
            low, pltpu.roll(under, FACE, 1), 0.0
        )
        local_ref[part, :, a + NODES - LANES : a + NODES] = tails[k] + jnp.where(
            low, 0.0, pltpu.roll(over, FACE, 1)
        )


def fetch_hams(packs, held_ref, sems):
    return run(
        [
            pltpu.make_async_copy(
                packs[k // 2].at[pl.ds((k % 2) * NODES, NODES), :], held_ref.at[k], sems.at[k]
            )
            for k in range(2 * GROUP)
        ]
    )


def add_local(me, v_ref, held_ref, local_ref):
    for r in range(GROUP):
        part = jnp.bitwise_xor(me, r)
        for cell in range(2):
            lanes = slice(cell * NODES, (cell + 1) * NODES)
            local_ref[part, :, lanes] += dot_nt(v_ref[part, :, lanes], held_ref[2 * r + cell])


def write_message(me, new, held_ref, proj_ref, edge_ref, wide_ref, message_ref):
    for r in range(GROUP):
        part = jnp.bitwise_xor(me, r)

        @pl.when(part == 0)
        def _():
            edge_ref[:FACE, :NODES] = held_ref[2 * r, :FACE, :]
            edge_ref[:FACE, NODES:] = jnp.zeros((FACE, NODES), BF16)

        @pl.when(part == GROUP - 1)
        def _():
            edge_ref[FACE:, :NODES] = jnp.zeros((FACE, NODES), BF16)
            edge_ref[FACE:, NODES:] = held_ref[2 * r + 1, NODES - FACE :, :]

    ends = jnp.concatenate([new[0][:, :NODES], new[GROUP - 1][:, NODES:]], axis=1)
    face = dot_nt(ends, edge_ref[...])
    wide_ref[:, SPAN:WIDE] = jnp.zeros((BODY, WIDE - SPAN), F32)
    for part in range(GROUP):
        coef = dot_nt(proj_ref[part], new[part])
        for i in range(NPROJ):
            wide_ref[eight(part), i * PIECE : (i + 1) * PIECE] = coef[eight(i)]
    place_face(face, wide_ref)
    message_ref[...] = wide_ref[...].astype(BF16)


def first_kernel(factors, place_ref, coupling_ref, got_ref, open_hbm, *refs):
    packs, refs = refs[:GROUP], refs[GROUP:]
    next_ref, message_ref, v_ref, proj_ref, near_ref, pick_ref, factor_ref = refs[:7]
    local_ref, held_ref, edge_ref, wide_ref, scaled_ref, raw_ref, sems = refs[7:]
    groups = got_ref.shape[0]
    me = place_ref[0]
    _, below, above = beside(place_ref, groups)
    copies = []
    for r in range(GROUP):
        at = 2 * GROUP + 2 * r
        copies += [
            pltpu.make_async_copy(packs[r].at[pl.ds(PART, 2 * PADDED), :], raw_ref.at[r], sems.at[at]),
            pltpu.make_async_copy(
                open_hbm.at[r, pl.ds(HEAD, PIECE), :], v_ref.at[r], sems.at[at + 1]
            ),
        ]
    run(copies)
    hams = fetch_hams(packs, held_ref, sems)

    place0, place1 = placers()
    for k, group, place in ((0, below, place1), (1, above, place0)):
        rows = got_ref[group].astype(F32)
        raw = [rows[BODY:, tile(j)] for j in range(8)]
        for j in range(8):
            row = (j % GROUP) * BLOCKS + BLOCKS - 1
            raw.append(rows[row : row + 1, tile(4 + j // GROUP)])
        near_ref[k] = dot(place, jnp.concatenate(raw, axis=0).astype(BF16)).astype(BF16)
    choose(place_ref, coupling_ref, got_ref, pick_ref, factor_ref)
    scaled = sum_coefs(got_ref, pick_ref, factor_ref, scaled_ref)

    finish(copies)
    for r in range(GROUP):
        part = jnp.bitwise_xor(me, r)
        for cell, place in ((0, place0), (1, place1)):
            raw = raw_ref[r, cell * PADDED : (cell + 1) * PADDED, :][:ROWS]
            lanes = slice(cell * NODES, (cell + 1) * NODES)
            proj_ref[part, :, lanes] = dot(place, raw).astype(BF16)
    for part in range(GROUP):
        local_ref[part] = dot_tn(scaled[part], proj_ref[part])
    finish(hams)
    add_local(me, v_ref, held_ref, local_ref)
    add_faces(place_ref, got_ref, near_ref, scaled, local_ref)
    gain, _ = factors[0]
    new = []
    for part in range(GROUP):
        new.append(((local_ref[part] - CENTER * v_ref[part].astype(F32)) * gain).astype(BF16))
        next_ref[part] = new[part]
    write_message(me, new, held_ref, proj_ref, edge_ref, wide_ref, message_ref)


def step_kernel(degree, factors, place_ref, got_ref, *refs):
    last = degree == DEGREE - 1
    packs, refs = refs[:GROUP], refs[GROUP:]
    v_ref, old_ref, proj_ref, near_ref, pick_ref, factor_ref = refs[:6]
    refs = refs[6:]
    if last:
        occ_ref, density_ref, *next_refs = refs[: 2 + GROUP]
        refs = refs[2 + GROUP :]
    else:
        next_ref, message_ref = refs[:2]
        refs = refs[2:]
    local_ref, held_ref, edge_ref, wide_ref, scaled_ref, sems = refs
    me = place_ref[0]
    hams = fetch_hams(packs, held_ref, sems)
    scaled = sum_coefs(got_ref, pick_ref, factor_ref, scaled_ref)
    for part in range(GROUP):
        local_ref[part] = dot_tn(scaled[part], proj_ref[part])
    finish(hams)
    add_local(me, v_ref, held_ref, local_ref)
    add_faces(place_ref, got_ref, near_ref, scaled, local_ref)

    gain, back = factors[degree]

    def image(part):
        now = v_ref[part].astype(F32)
        value = (local_ref[part] - CENTER * now) * gain - back * old_ref[part].astype(F32)
        return value.astype(BF16)

    if not last:
        new = [image(part) for part in range(GROUP)]
        for part in range(GROUP):
            next_ref[part] = new[part]
        write_message(me, new, held_ref, proj_ref, edge_ref, wide_ref, message_ref)
        return
    weight = jnp.transpose(jnp.broadcast_to(pick(occ_ref[...], me), (LANES, LANES)))[:PIECE]
    for r in range(GROUP):
        part = jnp.bitwise_xor(me, r)
        new = image(part)
        next_refs[r][...] = new
        values = new.astype(F32)
        for k in range(PART // LANES):
            term = values[:, tile(k)]
            sums = jnp.sum(term * term * weight, axis=0, keepdims=True)
            density_ref[part, 2 * k : 2 * k + 1, :] = sums[:, :FACE]
            density_ref[part, 2 * k + 1 : 2 * k + 2, :] = sums[:, FACE:]


def join_kernel(place_ref, *refs):
    ins, (out_ref, sems) = refs[:GROUP], refs[GROUP:]
    copies = []
    for r in range(GROUP):
        start = pl.multiple_of(jnp.bitwise_xor(place_ref[0], r) * PIECE, 16)
        copies.append(
            pltpu.make_async_copy(ins[r], out_ref.at[pl.ds(start, PIECE), :], sems.at[r])
        )
    run(copies)
    finish(copies)


def vmem():
    return pl.BlockSpec(memory_space=pltpu.VMEM)


def hbm():
    return pl.BlockSpec(memory_space=pltpu.HBM)


def smem():
    return pl.BlockSpec(memory_space=pltpu.SMEM)


def shape(dims, dtype=BF16):
    return jax.ShapeDtypeStruct(dims, dtype)


def shards(interpret, states, cell_ham, projectors, slot_atom, coupling, occupancy):
    width = states.shape[1]
    groups = lax.axis_size("z")
    spread = lax.axis_size("x") * lax.axis_size("yh")
    dma = pltpu.SemaphoreType.DMA
    near = ("yl", "c")
    ring = 2 * lax.axis_size("yh")

    def call(kernel, megabytes=24, **kw):
        params = pltpu.CompilerParams(vmem_limit_bytes=megabytes * 1024 * 1024)
        return pl.pallas_call(kernel, compiler_params=params, interpret=interpret, **kw)

    me = 2 * lax.axis_index("yl") + lax.axis_index("c")
    place = jnp.stack([me, lax.axis_index("z")]).astype(jnp.int32)
    occ = jnp.pad(occupancy.reshape(GROUP, PIECE), ((0, 0), (0, LANES - PIECE)))
    v_t = states.T
    opened = call(
        open_kernel,
        megabytes=60,
        out_shape=shape((GROUP, HEAD + PIECE, PART)),
        in_specs=[smem()] + [hbm()] * 3,
        out_specs=vmem(),
        scratch_shapes=[
            pltpu.VMEM((width, PART), BF16),
            pltpu.VMEM((2, LANES, NODES), BF16),
            pltpu.VMEM((2, ROWS, NODES), BF16),
            pltpu.VMEM((GROUP, HEAD, PART), F32),
            dma((4,)),
        ],
    )(slot_atom, v_t, cell_ham, projectors)
    opened = lax.all_to_all(opened, near, 0, 0)
    pack = call(
        share_kernel,
        megabytes=60,
        out_shape=shape((PACK, NODES)),
        in_specs=[hbm()] * 2,
        out_specs=vmem(),
        scratch_shapes=[pltpu.VMEM((2, ROWS, NODES), BF16), dma((3,))],
    )(cell_ham, projectors)
    message = call(
        pack_kernel,
        out_shape=shape((BODY + 8, PART)),
        in_specs=[vmem()],
        out_specs=vmem(),
        scratch_shapes=[pltpu.VMEM((BODY + 8, PART), F32)],
    )(opened)
    spot = lambda y, core: ((y % 2) * 2 + core) * (ring // 2) + y // 2

    def across(flip):
        return [
            (spot(y, c), spot((y + 1 - 2 * c) % ring, c ^ flip)) for y in range(ring) for c in (0, 1)
        ]

    beside_core = lax.ppermute(pack, "c", [(0, 1), (1, 0)])
    late, message = lax.optimization_barrier((pack, message))
    axes = ("yl", "c", "yh")
    packs = [
        pack,
        beside_core,
        lax.ppermute(late, axes, across(0)),
        lax.ppermute(late, axes, across(1)),
    ]

    factors = chebyshev_factors()
    state_shape = shape((GROUP, PIECE, PART))
    message_shape = shape((BODY, PART))
    scratch = [
        pltpu.VMEM((GROUP, PIECE, PART), F32),
        pltpu.VMEM((2 * GROUP, NODES, NODES), BF16),
        pltpu.VMEM((LANES, PART), BF16),
        pltpu.VMEM((BODY, PART), F32),
        pltpu.VMEM((GROUP + 2, PROJ, PIECE), F32),
    ]
    got = lax.all_gather(message, "z")
    v, message, old, *kept = call(
        functools.partial(first_kernel, factors),
        out_shape=[
            state_shape,
            message_shape,
            state_shape,
            shape((GROUP, PROJ, PART)),
            shape((2, PROJ, LANES)),
            shape((PIECE, -(-groups * BODY // LANES) * LANES)),
            shape((PIECE, WIDE), F32),
        ],
        in_specs=[smem()] + [vmem()] * 2 + [hbm()] * (GROUP + 1),
        out_specs=[vmem()] * 7,
        scratch_shapes=scratch
        + [pltpu.VMEM((GROUP, 2 * PADDED, NODES), BF16), dma((4 * GROUP,))],
    )(place, coupling, got, opened, *packs)
    for degree in range(1, DEGREE):
        got = lax.all_gather(message, "z")
        last = degree == DEGREE - 1
        outs = [state_shape, message_shape]
        if last:
            outs = [shape((GROUP, PART // FACE, FACE), F32)] + [shape((PIECE, PART))] * GROUP
        ends = [occ] if last else []
        result = call(
            functools.partial(step_kernel, degree, factors),
            out_shape=outs,
            in_specs=[smem(), vmem()] + [hbm()] * GROUP + [vmem()] * (6 + len(ends)),
            out_specs=[vmem()] * len(outs),
            scratch_shapes=scratch + [dma((2 * GROUP,))],
        )(place, got, *packs, v, old, *kept, *ends)
        old, v, message = v, result[0], result[1]

    density, *pieces = result
    pieces = [pieces[0]] + [
        lax.ppermute(pieces[r], near, [(k, k ^ r) for k in range(GROUP)]) for r in (1, 2, 3)
    ]
    filtered = call(
        join_kernel,
        out_shape=shape((width, PART)),
        in_specs=[smem()] + [hbm()] * GROUP,
        out_specs=hbm(),
        scratch_shapes=[dma((GROUP,))],
    )(place, *pieces)
    parts = GROUP * spread
    terms = lax.all_to_all(
        density.reshape(parts, GROUP * PART // parts), near + ("x", "yh"), 0, 0, tiled=True
    )
    density = jnp.sum(terms, axis=0) / (width * spread)
    return filtered.T, density


def build(mesh, interpret=False):
    part = ("z", "yl", "c")
    group = ("x", "yh")
    return jax.shard_map(
        functools.partial(shards, interpret),
        mesh=mesh,
        in_specs=(
            P(part, group),
            P(part, None, None),
            P(part, None, None),
            P(part, None),
            P(),
            P(group),
        ),
        out_specs=(P(part, group), P(part + group)),
        check_vma=False,
    )


def solution(mesh):
    count, groups = mesh.shape["mesh"], mesh.shape["state"]
    devices = mesh.devices.reshape(count // GROUP, 2, 2, groups // 4, 4)
    return build(Mesh(devices, ("z", "yl", "c", "x", "yh")))
```

```python
import functools

import jax
import jax.numpy as jnp
from jax import lax
from jax.experimental import pallas as pl
from jax.experimental.pallas import tpu as pltpu
from jax.sharding import Mesh, PartitionSpec as P

FACE = 64
DEGREE = 4
LANES = 128
NODES = 512
NPROJ = 18
SLOTS = 4
ROWS = SLOTS * NPROJ
GROUP = 4
PART = 2 * NODES
PIECE = 48
BLOCKS = 8
PROJ = NPROJ * BLOCKS
SPAN = NPROJ * PIECE
WIDE = 7 * LANES
BODY = GROUP * BLOCKS
PADDED = 80
PACK = PART + 2 * PADDED
HEAD = 32
CENTER = 0.5
HALF_WIDTH = 1.5
LOW_EDGE = -1.2

BF16 = jnp.bfloat16
F32 = jnp.float32
NT = (((1,), (1,)), ((), ()))
TN = (((0,), (0,)), ((), ()))


def chebyshev_factors():
    sigma = HALF_WIDTH / (LOW_EDGE - CENTER)
    gamma = 2.0 / sigma
    factors = [(sigma / HALF_WIDTH, 0.0)]
    for _ in range(1, DEGREE):
        sigma_new = 1.0 / (gamma - sigma)
        factors.append((2.0 * sigma_new / HALF_WIDTH, sigma * sigma_new))
        sigma = sigma_new
    return factors


def iota(shape, dim):
    return lax.broadcasted_iota(jnp.int32, shape, dim)


def dot(a, b):
    return jnp.dot(a, b, preferred_element_type=F32)


def dot_nt(a, b):
    return lax.dot_general(a, b, NT, preferred_element_type=F32)


def dot_tn(a, b):
    return lax.dot_general(a, b, TN, preferred_element_type=F32)


def exact(a, b):
    return jnp.dot(a, b, precision=lax.Precision.HIGHEST, preferred_element_type=F32)


def placers():
    row = iota((PROJ, ROWS), 0)
    col = iota((PROJ, ROWS), 1)
    which = row // BLOCKS
    block = row % BLOCKS
    first = (block < SLOTS) & (col == block * NPROJ + which)
    slot = block - SLOTS + 1
    second = ((block == 0) & (col == which)) | (
        (block >= SLOTS) & (block < 2 * SLOTS - 1) & (col == slot * NPROJ + which)
    )
    return first.astype(F32).astype(BF16), second.astype(F32).astype(BF16)


def low_lanes(rows):
    return iota((rows, LANES), 1) < FACE


def pick(rows, at):
    return jnp.sum(jnp.where(iota(rows.shape, 0) == at, rows, 0.0), axis=0, keepdims=True)


def run(copies):
    for copy in copies:
        copy.start()
    return copies


def finish(copies):
    for copy in copies:
        copy.wait()


def tile(k):
    return slice(k * LANES, (k + 1) * LANES)


def eight(k):
    return slice(k * 8, (k + 1) * 8)


def open_kernel(atom_ref, v_hbm, ham_hbm, proj_hbm, out_ref, v_ref, ham_ref, proj_ref, wide_ref, sems):
    copies = run(
        [
            pltpu.make_async_copy(v_hbm, v_ref, sems.at[0]),
            pltpu.make_async_copy(proj_hbm, proj_ref, sems.at[1]),
            pltpu.make_async_copy(ham_hbm.at[0, :LANES, :], ham_ref.at[0], sems.at[2]),
            pltpu.make_async_copy(ham_hbm.at[1, NODES - LANES :, :], ham_ref.at[1], sems.at[3]),
        ]
    )
    place0, place1 = placers()
    wide_ref[...] = jnp.zeros(wide_ref.shape, F32)
    lane = iota((8, LANES), 1)
    atoms = jnp.full((8, LANES), -1, jnp.int32)
    for block in range(2 * SLOTS - 1):
        cell, slot = (0, block) if block < SLOTS else (1, block - SLOTS + 1)
        atoms = jnp.where(lane == block, atom_ref[cell, slot], atoms)
    atoms = atoms.astype(F32)
    finish(copies)
    width = v_ref.shape[0]
    p0 = dot(place0, proj_ref[0]).astype(BF16)
    p1 = dot(place1, proj_ref[1]).astype(BF16)
    v0 = v_ref[:, :NODES]
    v1 = v_ref[:, NODES:]
    coef = dot_nt(p0, v0) + dot_nt(p1, v1)
    face = jnp.where(low_lanes(width), dot_nt(v0, ham_ref[0]), dot_nt(v1, ham_ref[1]))
    edge = jnp.where(
        low_lanes(ROWS),
        proj_ref[0, :, :LANES].astype(F32),
        proj_ref[1, :, NODES - LANES :].astype(F32),
    )
    for to in range(GROUP):
        for i in range(NPROJ):
            wide_ref[to, :8, i * PIECE : (i + 1) * PIECE] = coef[
                eight(i), to * PIECE : (to + 1) * PIECE
            ]
        for k in range(PIECE // 8):
            wide_ref[to, 8:16, tile(k)] = face[eight(to * (PIECE // 8) + k)]
        wide_ref[to, 8:16, tile(6)] = atoms
        for k in range(8):
            wide_ref[to, 16:24, tile(k)] = edge[eight(k)]
        wide_ref[to, 24:32, :LANES] = edge[eight(8)]
        out_ref[to, :HEAD, :] = wide_ref[to].astype(BF16)
        out_ref[to, HEAD:, :] = v_ref[to * PIECE : (to + 1) * PIECE, :]


def share_kernel(ham_hbm, proj_hbm, out_ref, proj_ref, sems):
    copies = [
        pltpu.make_async_copy(ham_hbm.at[k], out_ref.at[pl.ds(k * NODES, NODES), :], sems.at[k])
        for k in range(2)
    ]
    copies = run([pltpu.make_async_copy(proj_hbm, proj_ref, sems.at[2])] + copies)
    copies[0].wait()
    pad = jnp.zeros((PADDED - ROWS, NODES), BF16)
    for k in range(2):
        start = PART + k * PADDED
        out_ref[start : start + PADDED, :] = jnp.concatenate([proj_ref[k], pad], axis=0)
    finish(copies[1:])


def place_face(face, wide_ref):
    wide_ref[:BODY, WIDE:] = face[:BODY]
    for k in range(PIECE - BODY):
        row = (k % GROUP) * BLOCKS + BLOCKS - 1
        wide_ref[row : row + 1, tile(k // GROUP)] = face[BODY + k : BODY + k + 1]


def read_face(got_ref, group):
    body = got_ref[group, :BODY, :].astype(F32)
    rows = [body[:, WIDE:]]
    for k in range(PIECE - BODY):
        row = (k % GROUP) * BLOCKS + BLOCKS - 1
        rows.append(body[row : row + 1, tile(k // GROUP)])
    return jnp.concatenate(rows, axis=0)


def pack_kernel(in_ref, out_ref, wide_ref):
    last = GROUP - 1
    low = low_lanes(8)
    wide_ref[...] = jnp.zeros(wide_ref.shape, F32)
    pieces = [in_ref[part, :HEAD, :].astype(F32) for part in range(GROUP)]
    both = lambda rows, k: jnp.where(low, pieces[0][rows, tile(k)], pieces[last][rows, tile(k)])
    lane = iota((8, LANES), 1)
    atoms = jnp.full((8, LANES), -1.0, F32)
    for part in range(GROUP):
        wide_ref[eight(part), :WIDE] = pieces[part][:8, :WIDE]
        own = pieces[part][8:16, tile(6)]
        if part:
            own = pltpu.roll(own, part * BLOCKS, 1)
        atoms = jnp.where(lane // BLOCKS == part, own, atoms)
    face = jnp.concatenate([both(slice(8, 16), k) for k in range(PIECE // 8)], axis=0)
    place_face(face, wide_ref)
    ninth = both(slice(24, 32), 0)
    for k in range(8):
        wide_ref[BODY:, tile(k)] = both(slice(16, 24), k)
        row = (k % GROUP) * BLOCKS + BLOCKS - 1
        wide_ref[row : row + 1, tile(4 + k // GROUP)] = ninth[k : k + 1]
    wide_ref[BLOCKS - 1 : BLOCKS, tile(6)] = atoms[:1]
    out_ref[...] = wide_ref[...].astype(BF16)


def beside(place_ref, groups):
    z = place_ref[1]
    return z, jnp.maximum(z - 1, 0), jnp.minimum(z + 1, groups - 1)


def choose(place_ref, coupling_ref, got_ref, pick_ref, factor_ref):
    groups = got_ref.shape[0]
    z, below, above = beside(place_ref, groups)
    lane = iota((8, LANES), 1)
    named = lambda group: jnp.broadcast_to(
        got_ref[group, :16, tile(6)].astype(F32)[BLOCKS - 1 : BLOCKS], (8, LANES)
    )
    shift = lambda x, by: pltpu.roll(x, by, 1) if by else x
    per = LANES // BODY
    tiles = []
    for start in range(0, groups, per):
        x = jnp.full((8, LANES), -1.0, F32)
        for k in range(min(per, groups - start)):
            x = jnp.where(lane // BODY == k, shift(named(start + k), k * BODY), x)
        tiles.append(x)
    mine = jnp.where(lane < BODY, named(z), -1.0)
    mine = jnp.where(lane // BLOCKS == GROUP, shift(named(below), BLOCKS), mine)
    mine = jnp.where(lane // BLOCKS == GROUP + 1, shift(named(above), BODY + BLOCKS), mine)
    mine = jnp.where(mine < 0, -2.0, mine)
    column = jnp.transpose(jnp.concatenate([mine] * (LANES // 8), axis=0))[:PIECE]
    for k, x in enumerate(tiles):
        match = column == jnp.concatenate([x] * (PIECE // 8), axis=0)
        pick_ref[:, tile(k)] = jnp.where(match, 1.0, 0.0).astype(BF16)
    count = coupling_ref.shape[0]
    atom = iota((PIECE, LANES), 1).astype(F32)
    owner = jnp.where(column == atom, 1.0, 0.0)[:, :count]
    expand = jnp.where(iota((NPROJ, WIDE), 1) // PIECE == iota((NPROJ, WIDE), 0), 1.0, 0.0)
    factor_ref[...] = exact(exact(owner, coupling_ref[...]), expand)


def sum_coefs(got_ref, pick_ref, factor_ref, scaled_ref):
    groups = got_ref.shape[0]
    blocks = jnp.concatenate([got_ref[group, :BODY, :WIDE] for group in range(groups)], axis=0)
    total = dot(pick_ref[:, : groups * BODY], blocks) * factor_ref[...]
    for i in range(NPROJ):
        column = total[:, i * PIECE : (i + 1) * PIECE]
        for k in range(GROUP + 2):
            scaled_ref[k, eight(i), :] = column[eight(k)]
    return [scaled_ref[k].astype(BF16) for k in range(GROUP + 2)]


def add_faces(place_ref, got_ref, near_ref, scaled, local_ref):
    groups = got_ref.shape[0]
    z, below, above = beside(place_ref, groups)
    low = low_lanes(PIECE)
    from_below = read_face(got_ref, below) + dot_tn(scaled[GROUP], near_ref[0])
    from_above = read_face(got_ref, above) + dot_tn(scaled[GROUP + 1], near_ref[1])
    from_below = from_below * (z > 0).astype(F32)
    from_above = from_above * (z < groups - 1).astype(F32)
    cells = [(part, cell * NODES) for part in range(GROUP) for cell in range(2)]
    heads = [local_ref[part, :, a : a + LANES] for part, a in cells]
    tails = [local_ref[part, :, a + NODES - LANES : a + NODES] for part, a in cells]
    for k, (part, a) in enumerate(cells):
        under = tails[k - 1] if k > 0 else from_below
        over = heads[k + 1] if k + 1 < len(cells) else from_above
        local_ref[part, :, a : a + LANES] = heads[k] + jnp.where(
            low, pltpu.roll(under, FACE, 1), 0.0
        )
        local_ref[part, :, a + NODES - LANES : a + NODES] = tails[k] + jnp.where(
            low, 0.0, pltpu.roll(over, FACE, 1)
        )


def fetch_hams(packs, held_ref, sems):
    return run(
        [
            pltpu.make_async_copy(
                packs[k // 2].at[pl.ds((k % 2) * NODES, NODES), :], held_ref.at[k], sems.at[k]
            )
            for k in range(2 * GROUP)
        ]
    )


def add_local(me, v_ref, held_ref, local_ref):
    for r in range(GROUP):
        part = jnp.bitwise_xor(me, r)
        for cell in range(2):
            lanes = slice(cell * NODES, (cell + 1) * NODES)
            local_ref[part, :, lanes] += dot_nt(v_ref[part, :, lanes], held_ref[2 * r + cell])


def write_message(me, new, held_ref, proj_ref, edge_ref, wide_ref, message_ref):
    for r in range(GROUP):
        part = jnp.bitwise_xor(me, r)

        @pl.when(part == 0)
        def _():
            edge_ref[:FACE, :NODES] = held_ref[2 * r, :FACE, :]
            edge_ref[:FACE, NODES:] = jnp.zeros((FACE, NODES), BF16)

        @pl.when(part == GROUP - 1)
        def _():
            edge_ref[FACE:, :NODES] = jnp.zeros((FACE, NODES), BF16)
            edge_ref[FACE:, NODES:] = held_ref[2 * r + 1, NODES - FACE :, :]

    ends = jnp.concatenate([new[0][:, :NODES], new[GROUP - 1][:, NODES:]], axis=1)
    face = dot_nt(ends, edge_ref[...])
    wide_ref[:, SPAN:WIDE] = jnp.zeros((BODY, WIDE - SPAN), F32)
    for part in range(GROUP):
        coef = dot_nt(proj_ref[part], new[part])
        for i in range(NPROJ):
            wide_ref[eight(part), i * PIECE : (i + 1) * PIECE] = coef[eight(i)]
    place_face(face, wide_ref)
    message_ref[...] = wide_ref[...].astype(BF16)


def first_kernel(factors, place_ref, coupling_ref, got_ref, open_hbm, *refs):
    packs, refs = refs[:GROUP], refs[GROUP:]
    next_ref, message_ref, v_ref, held_ref, proj_ref, near_ref, pick_ref, factor_ref = refs[:8]
    local_ref, edge_ref, wide_ref, scaled_ref, raw_ref, sems = refs[8:]
    groups = got_ref.shape[0]
    me = place_ref[0]
    _, below, above = beside(place_ref, groups)
    copies = []
    for r in range(GROUP):
        at = 2 * GROUP + 2 * r
        copies += [
            pltpu.make_async_copy(packs[r].at[pl.ds(PART, 2 * PADDED), :], raw_ref.at[r], sems.at[at]),
            pltpu.make_async_copy(
                open_hbm.at[r, pl.ds(HEAD, PIECE), :], v_ref.at[r], sems.at[at + 1]
            ),
        ]
    run(copies)
    hams = fetch_hams(packs, held_ref, sems)

    place0, place1 = placers()
    for k, group, place in ((0, below, place1), (1, above, place0)):
        rows = got_ref[group].astype(F32)
        raw = [rows[BODY:, tile(j)] for j in range(8)]
        for j in range(8):
            row = (j % GROUP) * BLOCKS + BLOCKS - 1
            raw.append(rows[row : row + 1, tile(4 + j // GROUP)])
        near_ref[k] = dot(place, jnp.concatenate(raw, axis=0).astype(BF16)).astype(BF16)
    choose(place_ref, coupling_ref, got_ref, pick_ref, factor_ref)
    scaled = sum_coefs(got_ref, pick_ref, factor_ref, scaled_ref)

    finish(copies)
    for r in range(GROUP):
        part = jnp.bitwise_xor(me, r)
        for cell, place in ((0, place0), (1, place1)):
            raw = raw_ref[r, cell * PADDED : (cell + 1) * PADDED, :][:ROWS]
            lanes = slice(cell * NODES, (cell + 1) * NODES)
            proj_ref[part, :, lanes] = dot(place, raw).astype(BF16)
    for part in range(GROUP):
        local_ref[part] = dot_tn(scaled[part], proj_ref[part])
    finish(hams)
    add_local(me, v_ref, held_ref, local_ref)
    add_faces(place_ref, got_ref, near_ref, scaled, local_ref)
    gain, _ = factors[0]
    new = []
    for part in range(GROUP):
        new.append(((local_ref[part] - CENTER * v_ref[part].astype(F32)) * gain).astype(BF16))
        next_ref[part] = new[part]
    write_message(me, new, held_ref, proj_ref, edge_ref, wide_ref, message_ref)


def step_kernel(degree, factors, place_ref, got_ref, *refs):
    last = degree == DEGREE - 1
    v_ref, old_ref, held_ref, proj_ref, near_ref, pick_ref, factor_ref = refs[:7]
    refs = refs[7:]
    if last:
        occ_ref, density_ref, *next_refs = refs[: 2 + GROUP]
        refs = refs[2 + GROUP :]
    else:
        next_ref, message_ref = refs[:2]
        refs = refs[2:]
    local_ref, edge_ref, wide_ref, scaled_ref = refs
    me = place_ref[0]
    scaled = sum_coefs(got_ref, pick_ref, factor_ref, scaled_ref)
    for part in range(GROUP):
        local_ref[part] = dot_tn(scaled[part], proj_ref[part])
    add_local(me, v_ref, held_ref, local_ref)
    add_faces(place_ref, got_ref, near_ref, scaled, local_ref)

    gain, back = factors[degree]

    def image(part):
        now = v_ref[part].astype(F32)
        value = (local_ref[part] - CENTER * now) * gain - back * old_ref[part].astype(F32)
        return value.astype(BF16)

    if not last:
        new = [image(part) for part in range(GROUP)]
        for part in range(GROUP):
            next_ref[part] = new[part]
        write_message(me, new, held_ref, proj_ref, edge_ref, wide_ref, message_ref)
        return
    weight = jnp.transpose(jnp.broadcast_to(pick(occ_ref[...], me), (LANES, LANES)))[:PIECE]
    for r in range(GROUP):
        part = jnp.bitwise_xor(me, r)
        new = image(part)
        next_refs[r][...] = new
        values = new.astype(F32)
        for k in range(PART // LANES):
            term = values[:, tile(k)]
            sums = jnp.sum(term * term * weight, axis=0, keepdims=True)
            density_ref[part, 2 * k : 2 * k + 1, :] = sums[:, :FACE]
            density_ref[part, 2 * k + 1 : 2 * k + 2, :] = sums[:, FACE:]


def join_kernel(place_ref, *refs):
    ins, (out_ref, sems) = refs[:GROUP], refs[GROUP:]
    copies = []
    for r in range(GROUP):
        start = pl.multiple_of(jnp.bitwise_xor(place_ref[0], r) * PIECE, 16)
        copies.append(
            pltpu.make_async_copy(ins[r], out_ref.at[pl.ds(start, PIECE), :], sems.at[r])
        )
    run(copies)
    finish(copies)


def vmem():
    return pl.BlockSpec(memory_space=pltpu.VMEM)


def hbm():
    return pl.BlockSpec(memory_space=pltpu.HBM)


def smem():
    return pl.BlockSpec(memory_space=pltpu.SMEM)


def shape(dims, dtype=BF16):
    return jax.ShapeDtypeStruct(dims, dtype)


def shards(interpret, states, cell_ham, projectors, slot_atom, coupling, occupancy):
    width = states.shape[1]
    groups = lax.axis_size("z")
    spread = lax.axis_size("x") * lax.axis_size("yh")
    dma = pltpu.SemaphoreType.DMA
    near = ("yl", "c")
    ring = 2 * lax.axis_size("yh")

    def call(kernel, megabytes=24, **kw):
        params = pltpu.CompilerParams(vmem_limit_bytes=megabytes * 1024 * 1024)
        return pl.pallas_call(kernel, compiler_params=params, interpret=interpret, **kw)

    me = 2 * lax.axis_index("yl") + lax.axis_index("c")
    place = jnp.stack([me, lax.axis_index("z")]).astype(jnp.int32)
    occ = jnp.pad(occupancy.reshape(GROUP, PIECE), ((0, 0), (0, LANES - PIECE)))
    v_t = states.T
    opened = call(
        open_kernel,
        megabytes=60,
        out_shape=shape((GROUP, HEAD + PIECE, PART)),
        in_specs=[smem()] + [hbm()] * 3,
        out_specs=vmem(),
        scratch_shapes=[
            pltpu.VMEM((width, PART), BF16),
            pltpu.VMEM((2, LANES, NODES), BF16),
            pltpu.VMEM((2, ROWS, NODES), BF16),
            pltpu.VMEM((GROUP, HEAD, PART), F32),
            dma((4,)),
        ],
    )(slot_atom, v_t, cell_ham, projectors)
    opened = lax.all_to_all(opened, near, 0, 0)
    pack = call(
        share_kernel,
        megabytes=60,
        out_shape=shape((PACK, NODES)),
        in_specs=[hbm()] * 2,
        out_specs=vmem(),
        scratch_shapes=[pltpu.VMEM((2, ROWS, NODES), BF16), dma((3,))],
    )(cell_ham, projectors)
    message = call(
        pack_kernel,
        out_shape=shape((BODY + 8, PART)),
        in_specs=[vmem()],
        out_specs=vmem(),
        scratch_shapes=[pltpu.VMEM((BODY + 8, PART), F32)],
    )(opened)
    spot = lambda y, core: ((y % 2) * 2 + core) * (ring // 2) + y // 2

    def across(flip):
        return [
            (spot(y, c), spot((y + 1 - 2 * c) % ring, c ^ flip)) for y in range(ring) for c in (0, 1)
        ]

    beside_core = lax.ppermute(pack, "c", [(0, 1), (1, 0)])
    axes = ("yl", "c", "yh")
    packs = [
        pack,
        beside_core,
        lax.ppermute(pack, axes, across(0)),
        lax.ppermute(pack, axes, across(1)),
    ]

    factors = chebyshev_factors()
    state_shape = shape((GROUP, PIECE, PART))
    message_shape = shape((BODY, PART))
    scratch = [
        pltpu.VMEM((GROUP, PIECE, PART), F32),
        pltpu.VMEM((LANES, PART), BF16),
        pltpu.VMEM((BODY, PART), F32),
        pltpu.VMEM((GROUP + 2, PROJ, PIECE), F32),
    ]
    got = lax.all_gather(message, "z")
    v, message, old, *kept = call(
        functools.partial(first_kernel, factors),
        out_shape=[
            state_shape,
            message_shape,
            state_shape,
            shape((2 * GROUP, NODES, NODES)),
            shape((GROUP, PROJ, PART)),
            shape((2, PROJ, LANES)),
            shape((PIECE, -(-groups * BODY // LANES) * LANES)),
            shape((PIECE, WIDE), F32),
        ],
        in_specs=[smem()] + [vmem()] * 2 + [hbm()] * (GROUP + 1),
        out_specs=[vmem()] * 8,
        scratch_shapes=scratch
        + [pltpu.VMEM((GROUP, 2 * PADDED, NODES), BF16), dma((4 * GROUP,))],
    )(place, coupling, got, opened, *packs)
    for degree in range(1, DEGREE):
        got = lax.all_gather(message, "z")
        last = degree == DEGREE - 1
        outs = [state_shape, message_shape]
        if last:
            outs = [shape((GROUP, PART // FACE, FACE), F32)] + [shape((PIECE, PART))] * GROUP
        ends = [occ] if last else []
        result = call(
            functools.partial(step_kernel, degree, factors),
            out_shape=outs,
            in_specs=[smem()] + [vmem()] * (8 + len(ends)),
            out_specs=[vmem()] * len(outs),
            scratch_shapes=scratch,
        )(place, got, v, old, *kept, *ends)
        old, v, message = v, result[0], result[1]

    density, *pieces = result
    pieces = [pieces[0]] + [
        lax.ppermute(pieces[r], near, [(k, k ^ r) for k in range(GROUP)]) for r in (1, 2, 3)
    ]
    filtered = call(
        join_kernel,
        out_shape=shape((width, PART)),
        in_specs=[smem()] + [hbm()] * GROUP,
        out_specs=hbm(),
        scratch_shapes=[dma((GROUP,))],
    )(place, *pieces)
    parts = GROUP * spread
    terms = lax.all_to_all(
        density.reshape(parts, GROUP * PART // parts), near + ("x", "yh"), 0, 0, tiled=True
    )
    density = jnp.sum(terms, axis=0) / (width * spread)
    return filtered.T, density


def build(mesh, interpret=False):
    part = ("z", "yl", "c")
    group = ("x", "yh")
    return jax.shard_map(
        functools.partial(shards, interpret),
        mesh=mesh,
        in_specs=(
            P(part, group),
            P(part, None, None),
            P(part, None, None),
            P(part, None),
            P(),
            P(group),
        ),
        out_specs=(P(part, group), P(part + group)),
        check_vma=False,
    )


def solution(mesh):
    count, groups = mesh.shape["mesh"], mesh.shape["state"]
    devices = mesh.devices.reshape(count // GROUP, 2, 2, groups // 4, 4)
    return build(Mesh(devices, ("z", "yl", "c", "x", "yh")))
```

```python
import functools

import jax
import jax.numpy as jnp
from jax import lax
from jax.experimental import pallas as pl
from jax.experimental.pallas import tpu as pltpu
from jax.sharding import Mesh, PartitionSpec as P

FACE = 64
DEGREE = 4
LANES = 128
NODES = 512
NPROJ = 18
SLOTS = 4
ROWS = SLOTS * NPROJ
GROUP = 4
PART = 2 * NODES
PIECE = 48
BLOCKS = 8
PROJ = NPROJ * BLOCKS
SPAN = NPROJ * PIECE
WIDE = 7 * LANES
BODY = GROUP * BLOCKS
PADDED = 80
PACK = PART + 2 * PADDED
HEAD = 32
CENTER = 0.5
HALF_WIDTH = 1.5
LOW_EDGE = -1.2

BF16 = jnp.bfloat16
F32 = jnp.float32
NT = (((1,), (1,)), ((), ()))
TN = (((0,), (0,)), ((), ()))


def chebyshev_factors():
    sigma = HALF_WIDTH / (LOW_EDGE - CENTER)
    gamma = 2.0 / sigma
    factors = [(sigma / HALF_WIDTH, 0.0)]
    for _ in range(1, DEGREE):
        sigma_new = 1.0 / (gamma - sigma)
        factors.append((2.0 * sigma_new / HALF_WIDTH, sigma * sigma_new))
        sigma = sigma_new
    return factors


def iota(shape, dim):
    return lax.broadcasted_iota(jnp.int32, shape, dim)


def dot(a, b):
    return jnp.dot(a, b, preferred_element_type=F32)


def dot_nt(a, b):
    return lax.dot_general(a, b, NT, preferred_element_type=F32)


def dot_tn(a, b):
    return lax.dot_general(a, b, TN, preferred_element_type=F32)


def exact(a, b):
    return jnp.dot(a, b, precision=lax.Precision.HIGHEST, preferred_element_type=F32)


def placers():
    row = iota((PROJ, ROWS), 0)
    col = iota((PROJ, ROWS), 1)
    which = row // BLOCKS
    block = row % BLOCKS
    first = (block < SLOTS) & (col == block * NPROJ + which)
    slot = block - SLOTS + 1
    second = ((block == 0) & (col == which)) | (
        (block >= SLOTS) & (block < 2 * SLOTS - 1) & (col == slot * NPROJ + which)
    )
    return first.astype(F32).astype(BF16), second.astype(F32).astype(BF16)


def low_lanes(rows):
    return iota((rows, LANES), 1) < FACE


def pick(rows, at):
    return jnp.sum(jnp.where(iota(rows.shape, 0) == at, rows, 0.0), axis=0, keepdims=True)


def run(copies):
    for copy in copies:
        copy.start()
    return copies


def finish(copies):
    for copy in copies:
        copy.wait()


def tile(k):
    return slice(k * LANES, (k + 1) * LANES)


def eight(k):
    return slice(k * 8, (k + 1) * 8)


def open_kernel(
    atom_ref, v_hbm, ham_hbm, proj_hbm, out_ref, pack_ref, v_ref, ham_ref, proj_ref, wide_ref, sems
):
    proj_in, v_in, *edges = run(
        [
            pltpu.make_async_copy(proj_hbm, proj_ref, sems.at[0]),
            pltpu.make_async_copy(v_hbm, v_ref, sems.at[1]),
            pltpu.make_async_copy(ham_hbm.at[0, :LANES, :], ham_ref.at[0], sems.at[2]),
            pltpu.make_async_copy(ham_hbm.at[1, NODES - LANES :, :], ham_ref.at[1], sems.at[3]),
        ]
    )
    hams = run(
        [
            pltpu.make_async_copy(
                ham_hbm.at[k], pack_ref.at[pl.ds(k * NODES, NODES), :], sems.at[4 + k]
            )
            for k in range(2)
        ]
    )
    place0, place1 = placers()
    wide_ref[...] = jnp.zeros(wide_ref.shape, F32)
    lane = iota((8, LANES), 1)
    atoms = jnp.full((8, LANES), -1, jnp.int32)
    for block in range(2 * SLOTS - 1):
        cell, slot = (0, block) if block < SLOTS else (1, block - SLOTS + 1)
        atoms = jnp.where(lane == block, atom_ref[cell, slot], atoms)
    atoms = atoms.astype(F32)
    width = v_ref.shape[0]
    proj_in.wait()
    pad = jnp.zeros((PADDED - ROWS, NODES), BF16)
    for k in range(2):
        start = PART + k * PADDED
        pack_ref[start : start + PADDED, :] = jnp.concatenate([proj_ref[k], pad], axis=0)
    p0 = dot(place0, proj_ref[0]).astype(BF16)
    p1 = dot(place1, proj_ref[1]).astype(BF16)
    v_in.wait()
    v0 = v_ref[:, :NODES]
    v1 = v_ref[:, NODES:]
    coef = dot_nt(p0, v0) + dot_nt(p1, v1)
    finish(edges)
    face = jnp.where(low_lanes(width), dot_nt(v0, ham_ref[0]), dot_nt(v1, ham_ref[1]))
    edge = jnp.where(
        low_lanes(ROWS),
        proj_ref[0, :, :LANES].astype(F32),
        proj_ref[1, :, NODES - LANES :].astype(F32),
    )
    for to in range(GROUP):
        for i in range(NPROJ):
            wide_ref[to, :8, i * PIECE : (i + 1) * PIECE] = coef[
                eight(i), to * PIECE : (to + 1) * PIECE
            ]
        for k in range(PIECE // 8):
            wide_ref[to, 8:16, tile(k)] = face[eight(to * (PIECE // 8) + k)]
        wide_ref[to, 8:16, tile(6)] = atoms
        for k in range(8):
            wide_ref[to, 16:24, tile(k)] = edge[eight(k)]
        wide_ref[to, 24:32, :LANES] = edge[eight(8)]
        out_ref[to, :HEAD, :] = wide_ref[to].astype(BF16)
        out_ref[to, HEAD:, :] = v_ref[to * PIECE : (to + 1) * PIECE, :]
    finish(hams)


def place_face(face, wide_ref):
    wide_ref[:BODY, WIDE:] = face[:BODY]
    for k in range(PIECE - BODY):
        row = (k % GROUP) * BLOCKS + BLOCKS - 1
        wide_ref[row : row + 1, tile(k // GROUP)] = face[BODY + k : BODY + k + 1]


def read_face(got_ref, group):
    body = got_ref[group, :BODY, :].astype(F32)
    rows = [body[:, WIDE:]]
    for k in range(PIECE - BODY):
        row = (k % GROUP) * BLOCKS + BLOCKS - 1
        rows.append(body[row : row + 1, tile(k // GROUP)])
    return jnp.concatenate(rows, axis=0)


def pack_kernel(in_ref, out_ref, wide_ref):
    last = GROUP - 1
    low = low_lanes(8)
    wide_ref[...] = jnp.zeros(wide_ref.shape, F32)
    pieces = [in_ref[part, :HEAD, :].astype(F32) for part in range(GROUP)]
    both = lambda rows, k: jnp.where(low, pieces[0][rows, tile(k)], pieces[last][rows, tile(k)])
    lane = iota((8, LANES), 1)
    atoms = jnp.full((8, LANES), -1.0, F32)
    for part in range(GROUP):
        wide_ref[eight(part), :WIDE] = pieces[part][:8, :WIDE]
        own = pieces[part][8:16, tile(6)]
        if part:
            own = pltpu.roll(own, part * BLOCKS, 1)
        atoms = jnp.where(lane // BLOCKS == part, own, atoms)
    face = jnp.concatenate([both(slice(8, 16), k) for k in range(PIECE // 8)], axis=0)
    place_face(face, wide_ref)
    ninth = both(slice(24, 32), 0)
    for k in range(8):
        wide_ref[BODY:, tile(k)] = both(slice(16, 24), k)
        row = (k % GROUP) * BLOCKS + BLOCKS - 1
        wide_ref[row : row + 1, tile(4 + k // GROUP)] = ninth[k : k + 1]
    wide_ref[BLOCKS - 1 : BLOCKS, tile(6)] = atoms[:1]
    out_ref[...] = wide_ref[...].astype(BF16)


def beside(place_ref, groups):
    z = place_ref[1]
    return z, jnp.maximum(z - 1, 0), jnp.minimum(z + 1, groups - 1)


def choose(place_ref, coupling_ref, got_ref, pick_ref, factor_ref):
    groups = got_ref.shape[0]
    z, below, above = beside(place_ref, groups)
    lane = iota((8, LANES), 1)
    named = lambda group: jnp.broadcast_to(
        got_ref[group, :16, tile(6)].astype(F32)[BLOCKS - 1 : BLOCKS], (8, LANES)
    )
    shift = lambda x, by: pltpu.roll(x, by, 1) if by else x
    per = LANES // BODY
    tiles = []
    for start in range(0, groups, per):
        x = jnp.full((8, LANES), -1.0, F32)
        for k in range(min(per, groups - start)):
            x = jnp.where(lane // BODY == k, shift(named(start + k), k * BODY), x)
        tiles.append(x)
    mine = jnp.where(lane < BODY, named(z), -1.0)
    mine = jnp.where(lane // BLOCKS == GROUP, shift(named(below), BLOCKS), mine)
    mine = jnp.where(lane // BLOCKS == GROUP + 1, shift(named(above), BODY + BLOCKS), mine)
    mine = jnp.where(mine < 0, -2.0, mine)
    column = jnp.transpose(jnp.concatenate([mine] * (LANES // 8), axis=0))[:PIECE]
    for k, x in enumerate(tiles):
        match = column == jnp.concatenate([x] * (PIECE // 8), axis=0)
        pick_ref[:, tile(k)] = jnp.where(match, 1.0, 0.0).astype(BF16)
    count = coupling_ref.shape[0]
    atom = iota((PIECE, LANES), 1).astype(F32)
    owner = jnp.where(column == atom, 1.0, 0.0)[:, :count]
    expand = jnp.where(iota((NPROJ, WIDE), 1) // PIECE == iota((NPROJ, WIDE), 0), 1.0, 0.0)
    factor_ref[...] = exact(exact(owner, coupling_ref[...]), expand)


def sum_coefs(got_ref, pick_ref, factor_ref, scaled_ref):
    groups = got_ref.shape[0]
    blocks = jnp.concatenate([got_ref[group, :BODY, :WIDE] for group in range(groups)], axis=0)
    total = dot(pick_ref[:, : groups * BODY], blocks) * factor_ref[...]
    for i in range(NPROJ):
        column = total[:, i * PIECE : (i + 1) * PIECE]
        for k in range(GROUP + 2):
            scaled_ref[k, eight(i), :] = column[eight(k)]
    return [scaled_ref[k].astype(BF16) for k in range(GROUP + 2)]


def add_faces(place_ref, got_ref, near_ref, scaled, local_ref):
    groups = got_ref.shape[0]
    z, below, above = beside(place_ref, groups)
    low = low_lanes(PIECE)
    from_below = read_face(got_ref, below) + dot_tn(scaled[GROUP], near_ref[0])
    from_above = read_face(got_ref, above) + dot_tn(scaled[GROUP + 1], near_ref[1])
    from_below = from_below * (z > 0).astype(F32)
    from_above = from_above * (z < groups - 1).astype(F32)
    cells = [(part, cell * NODES) for part in range(GROUP) for cell in range(2)]
    heads = [local_ref[part, :, a : a + LANES] for part, a in cells]
    tails = [local_ref[part, :, a + NODES - LANES : a + NODES] for part, a in cells]
    for k, (part, a) in enumerate(cells):
        under = tails[k - 1] if k > 0 else from_below
        over = heads[k + 1] if k + 1 < len(cells) else from_above
        local_ref[part, :, a : a + LANES] = heads[k] + jnp.where(
            low, pltpu.roll(under, FACE, 1), 0.0
        )
        local_ref[part, :, a + NODES - LANES : a + NODES] = tails[k] + jnp.where(
            low, 0.0, pltpu.roll(over, FACE, 1)
        )


def fetch_hams(packs, held_ref, sems):
    return run(
        [
            pltpu.make_async_copy(
                packs[k // 2].at[pl.ds((k % 2) * NODES, NODES), :], held_ref.at[k], sems.at[k]
            )
            for k in range(2 * GROUP)
        ]
    )


def add_local(me, v_ref, held_ref, local_ref):
    for r in range(GROUP):
        part = jnp.bitwise_xor(me, r)
        for cell in range(2):
            lanes = slice(cell * NODES, (cell + 1) * NODES)
            local_ref[part, :, lanes] += dot_nt(v_ref[part, :, lanes], held_ref[2 * r + cell])


def write_message(me, new, held_ref, proj_ref, edge_ref, wide_ref, message_ref):
    for r in range(GROUP):
        part = jnp.bitwise_xor(me, r)

        @pl.when(part == 0)
        def _():
            edge_ref[:FACE, :NODES] = held_ref[2 * r, :FACE, :]
            edge_ref[:FACE, NODES:] = jnp.zeros((FACE, NODES), BF16)

        @pl.when(part == GROUP - 1)
        def _():
            edge_ref[FACE:, :NODES] = jnp.zeros((FACE, NODES), BF16)
            edge_ref[FACE:, NODES:] = held_ref[2 * r + 1, NODES - FACE :, :]

    ends = jnp.concatenate([new[0][:, :NODES], new[GROUP - 1][:, NODES:]], axis=1)
    face = dot_nt(ends, edge_ref[...])
    wide_ref[:, SPAN:WIDE] = jnp.zeros((BODY, WIDE - SPAN), F32)
    for part in range(GROUP):
        coef = dot_nt(proj_ref[part], new[part])
        for i in range(NPROJ):
            wide_ref[eight(part), i * PIECE : (i + 1) * PIECE] = coef[eight(i)]
    place_face(face, wide_ref)
    message_ref[...] = wide_ref[...].astype(BF16)


def first_kernel(factors, place_ref, coupling_ref, got_ref, open_hbm, *refs):
    packs, refs = refs[:GROUP], refs[GROUP:]
    next_ref, message_ref, v_ref, held_ref, proj_ref, near_ref, pick_ref, factor_ref = refs[:8]
    local_ref, edge_ref, wide_ref, scaled_ref, raw_ref, sems = refs[8:]
    groups = got_ref.shape[0]
    me = place_ref[0]
    _, below, above = beside(place_ref, groups)
    copies = []
    for r in range(GROUP):
        at = 2 * GROUP + 2 * r
        copies += [
            pltpu.make_async_copy(packs[r].at[pl.ds(PART, 2 * PADDED), :], raw_ref.at[r], sems.at[at]),
            pltpu.make_async_copy(
                open_hbm.at[r, pl.ds(HEAD, PIECE), :], v_ref.at[r], sems.at[at + 1]
            ),
        ]
    run(copies)
    hams = fetch_hams(packs, held_ref, sems)

    place0, place1 = placers()
    for k, group, place in ((0, below, place1), (1, above, place0)):
        rows = got_ref[group].astype(F32)
        raw = [rows[BODY:, tile(j)] for j in range(8)]
        for j in range(8):
            row = (j % GROUP) * BLOCKS + BLOCKS - 1
            raw.append(rows[row : row + 1, tile(4 + j // GROUP)])
        near_ref[k] = dot(place, jnp.concatenate(raw, axis=0).astype(BF16)).astype(BF16)
    choose(place_ref, coupling_ref, got_ref, pick_ref, factor_ref)
    scaled = sum_coefs(got_ref, pick_ref, factor_ref, scaled_ref)

    finish(copies)
    for r in range(GROUP):
        part = jnp.bitwise_xor(me, r)
        for cell, place in ((0, place0), (1, place1)):
            raw = raw_ref[r, cell * PADDED : (cell + 1) * PADDED, :][:ROWS]
            lanes = slice(cell * NODES, (cell + 1) * NODES)
            proj_ref[part, :, lanes] = dot(place, raw).astype(BF16)
    for part in range(GROUP):
        local_ref[part] = dot_tn(scaled[part], proj_ref[part])
    finish(hams)
    add_local(me, v_ref, held_ref, local_ref)
    add_faces(place_ref, got_ref, near_ref, scaled, local_ref)
    gain, _ = factors[0]
    new = []
    for part in range(GROUP):
        new.append(((local_ref[part] - CENTER * v_ref[part].astype(F32)) * gain).astype(BF16))
        next_ref[part] = new[part]
    write_message(me, new, held_ref, proj_ref, edge_ref, wide_ref, message_ref)


def step_kernel(degree, factors, place_ref, got_ref, *refs):
    last = degree == DEGREE - 1
    v_ref, old_ref, held_ref, proj_ref, near_ref, pick_ref, factor_ref = refs[:7]
    refs = refs[7:]
    if last:
        occ_ref, density_ref, *next_refs = refs[: 2 + GROUP]
        refs = refs[2 + GROUP :]
    else:
        next_ref, message_ref = refs[:2]
        refs = refs[2:]
    local_ref, edge_ref, wide_ref, scaled_ref = refs
    me = place_ref[0]
    scaled = sum_coefs(got_ref, pick_ref, factor_ref, scaled_ref)
    for part in range(GROUP):
        local_ref[part] = dot_tn(scaled[part], proj_ref[part])
    add_local(me, v_ref, held_ref, local_ref)
    add_faces(place_ref, got_ref, near_ref, scaled, local_ref)

    gain, back = factors[degree]

    def image(part):
        now = v_ref[part].astype(F32)
        value = (local_ref[part] - CENTER * now) * gain - back * old_ref[part].astype(F32)
        return value.astype(BF16)

    if not last:
        new = [image(part) for part in range(GROUP)]
        for part in range(GROUP):
            next_ref[part] = new[part]
        write_message(me, new, held_ref, proj_ref, edge_ref, wide_ref, message_ref)
        return
    weight = jnp.transpose(jnp.broadcast_to(pick(occ_ref[...], me), (LANES, LANES)))[:PIECE]
    for r in range(GROUP):
        part = jnp.bitwise_xor(me, r)
        new = image(part)
        next_refs[r][...] = new
        values = new.astype(F32)
        for k in range(PART // LANES):
            term = values[:, tile(k)]
            sums = jnp.sum(term * term * weight, axis=0, keepdims=True)
            density_ref[part, 2 * k : 2 * k + 1, :] = sums[:, :FACE]
            density_ref[part, 2 * k + 1 : 2 * k + 2, :] = sums[:, FACE:]


def join_kernel(place_ref, *refs):
    ins, (out_ref, sems) = refs[:GROUP], refs[GROUP:]
    copies = []
    for r in range(GROUP):
        start = pl.multiple_of(jnp.bitwise_xor(place_ref[0], r) * PIECE, 16)
        copies.append(
            pltpu.make_async_copy(ins[r], out_ref.at[pl.ds(start, PIECE), :], sems.at[r])
        )
    run(copies)
    finish(copies)


def vmem():
    return pl.BlockSpec(memory_space=pltpu.VMEM)


def hbm():
    return pl.BlockSpec(memory_space=pltpu.HBM)


def smem():
    return pl.BlockSpec(memory_space=pltpu.SMEM)


def shape(dims, dtype=BF16):
    return jax.ShapeDtypeStruct(dims, dtype)


def shards(interpret, states, cell_ham, projectors, slot_atom, coupling, occupancy):
    width = states.shape[1]
    groups = lax.axis_size("z")
    spread = lax.axis_size("x") * lax.axis_size("yh")
    dma = pltpu.SemaphoreType.DMA
    near = ("yl", "c")
    ring = 2 * lax.axis_size("yh")

    def call(kernel, megabytes=24, **kw):
        params = pltpu.CompilerParams(vmem_limit_bytes=megabytes * 1024 * 1024)
        return pl.pallas_call(kernel, compiler_params=params, interpret=interpret, **kw)

    me = 2 * lax.axis_index("yl") + lax.axis_index("c")
    place = jnp.stack([me, lax.axis_index("z")]).astype(jnp.int32)
    occ = jnp.pad(occupancy.reshape(GROUP, PIECE), ((0, 0), (0, LANES - PIECE)))
    v_t = states.T
    opened, pack = call(
        open_kernel,
        megabytes=60,
        out_shape=[shape((GROUP, HEAD + PIECE, PART)), shape((PACK, NODES))],
        in_specs=[smem()] + [hbm()] * 3,
        out_specs=[vmem()] * 2,
        scratch_shapes=[
            pltpu.VMEM((width, PART), BF16),
            pltpu.VMEM((2, LANES, NODES), BF16),
            pltpu.VMEM((2, ROWS, NODES), BF16),
            pltpu.VMEM((GROUP, HEAD, PART), F32),
            dma((6,)),
        ],
    )(slot_atom, v_t, cell_ham, projectors)
    opened = lax.all_to_all(opened, near, 0, 0)
    message = call(
        pack_kernel,
        out_shape=shape((BODY + 8, PART)),
        in_specs=[vmem()],
        out_specs=vmem(),
        scratch_shapes=[pltpu.VMEM((BODY + 8, PART), F32)],
    )(opened)
    spot = lambda y, core: ((y % 2) * 2 + core) * (ring // 2) + y // 2

    def across(flip):
        return [
            (spot(y, c), spot((y + 1 - 2 * c) % ring, c ^ flip)) for y in range(ring) for c in (0, 1)
        ]

    beside_core = lax.ppermute(pack, "c", [(0, 1), (1, 0)])
    axes = ("yl", "c", "yh")
    packs = [
        pack,
        beside_core,
        lax.ppermute(pack, axes, across(0)),
        lax.ppermute(pack, axes, across(1)),
    ]

    factors = chebyshev_factors()
    state_shape = shape((GROUP, PIECE, PART))
    message_shape = shape((BODY, PART))
    scratch = [
        pltpu.VMEM((GROUP, PIECE, PART), F32),
        pltpu.VMEM((LANES, PART), BF16),
        pltpu.VMEM((BODY, PART), F32),
        pltpu.VMEM((GROUP + 2, PROJ, PIECE), F32),
    ]
    got = lax.all_gather(message, "z")
    v, message, old, *kept = call(
        functools.partial(first_kernel, factors),
        out_shape=[
            state_shape,
            message_shape,
            state_shape,
            shape((2 * GROUP, NODES, NODES)),
            shape((GROUP, PROJ, PART)),
            shape((2, PROJ, LANES)),
            shape((PIECE, -(-groups * BODY // LANES) * LANES)),
            shape((PIECE, WIDE), F32),
        ],
        in_specs=[smem()] + [vmem()] * 2 + [hbm()] * (GROUP + 1),
        out_specs=[vmem()] * 8,
        scratch_shapes=scratch
        + [pltpu.VMEM((GROUP, 2 * PADDED, NODES), BF16), dma((4 * GROUP,))],
    )(place, coupling, got, opened, *packs)
    for degree in range(1, DEGREE):
        got = lax.all_gather(message, "z")
        last = degree == DEGREE - 1
        outs = [state_shape, message_shape]
        if last:
            outs = [shape((GROUP, PART // FACE, FACE), F32)] + [shape((PIECE, PART))] * GROUP
        ends = [occ] if last else []
        result = call(
            functools.partial(step_kernel, degree, factors),
            out_shape=outs,
            in_specs=[smem()] + [vmem()] * (8 + len(ends)),
            out_specs=[vmem()] * len(outs),
            scratch_shapes=scratch,
        )(place, got, v, old, *kept, *ends)
        old, v, message = v, result[0], result[1]

    density, *pieces = result
    for r in (3, 2, 1):
        pieces[r] = lax.ppermute(pieces[r], near, [(k, k ^ r) for k in range(GROUP)])
    filtered = call(
        join_kernel,
        out_shape=shape((width, PART)),
        in_specs=[smem()] + [hbm()] * GROUP,
        out_specs=hbm(),
        scratch_shapes=[dma((GROUP,))],
    )(place, *pieces)
    parts = GROUP * spread
    terms = lax.all_to_all(
        density.reshape(parts, GROUP * PART // parts), near + ("x", "yh"), 0, 0, tiled=True
    )
    density = jnp.sum(terms, axis=0) / (width * spread)
    return filtered.T, density


def build(mesh, interpret=False):
    part = ("z", "yl", "c")
    group = ("x", "yh")
    return jax.shard_map(
        functools.partial(shards, interpret),
        mesh=mesh,
        in_specs=(
            P(part, group),
            P(part, None, None),
            P(part, None, None),
            P(part, None),
            P(),
            P(group),
        ),
        out_specs=(P(part, group), P(part + group)),
        check_vma=False,
    )


def solution(mesh):
    count, groups = mesh.shape["mesh"], mesh.shape["state"]
    devices = mesh.devices.reshape(count // GROUP, 2, 2, groups // 4, 4)
    return build(Mesh(devices, ("z", "yl", "c", "x", "yh")))
```

```python
import functools

import jax
import jax.numpy as jnp
from jax import lax
from jax.experimental import pallas as pl
from jax.experimental.pallas import tpu as pltpu
from jax.sharding import Mesh, PartitionSpec as P

FACE = 64
DEGREE = 4
LANES = 128
NODES = 512
NPROJ = 18
SLOTS = 4
ROWS = SLOTS * NPROJ
GROUP = 4
PART = 2 * NODES
PIECE = 48
BLOCKS = 8
PROJ = NPROJ * BLOCKS
SPAN = NPROJ * PIECE
WIDE = 7 * LANES
BODY = GROUP * BLOCKS
PADDED = 80
PACK = PART + 2 * PADDED
HEAD = 32
CENTER = 0.5
HALF_WIDTH = 1.5
LOW_EDGE = -1.2

BF16 = jnp.bfloat16
F32 = jnp.float32
NT = (((1,), (1,)), ((), ()))
TN = (((0,), (0,)), ((), ()))


def chebyshev_factors():
    sigma = HALF_WIDTH / (LOW_EDGE - CENTER)
    gamma = 2.0 / sigma
    factors = [(sigma / HALF_WIDTH, 0.0)]
    for _ in range(1, DEGREE):
        sigma_new = 1.0 / (gamma - sigma)
        factors.append((2.0 * sigma_new / HALF_WIDTH, sigma * sigma_new))
        sigma = sigma_new
    return factors


def iota(shape, dim):
    return lax.broadcasted_iota(jnp.int32, shape, dim)


def dot(a, b):
    return jnp.dot(a, b, preferred_element_type=F32)


def dot_nt(a, b):
    return lax.dot_general(a, b, NT, preferred_element_type=F32)


def dot_tn(a, b):
    return lax.dot_general(a, b, TN, preferred_element_type=F32)


def exact(a, b):
    return jnp.dot(a, b, precision=lax.Precision.HIGHEST, preferred_element_type=F32)


def placers():
    row = iota((PROJ, ROWS), 0)
    col = iota((PROJ, ROWS), 1)
    which = row // BLOCKS
    block = row % BLOCKS
    first = (block < SLOTS) & (col == block * NPROJ + which)
    slot = block - SLOTS + 1
    second = ((block == 0) & (col == which)) | (
        (block >= SLOTS) & (block < 2 * SLOTS - 1) & (col == slot * NPROJ + which)
    )
    return first.astype(F32).astype(BF16), second.astype(F32).astype(BF16)


def low_lanes(rows):
    return iota((rows, LANES), 1) < FACE


def pick(rows, at):
    return jnp.sum(jnp.where(iota(rows.shape, 0) == at, rows, 0.0), axis=0, keepdims=True)


def run(copies):
    for copy in copies:
        copy.start()
    return copies


def finish(copies):
    for copy in copies:
        copy.wait()


def tile(k):
    return slice(k * LANES, (k + 1) * LANES)


def eight(k):
    return slice(k * 8, (k + 1) * 8)


def open_kernel(
    atom_ref, v_hbm, ham_hbm, proj_hbm, out_ref, pack_ref, v_ref, ham_ref, proj_ref, wide_ref, sems
):
    proj_in, v_in, *edges = run(
        [
            pltpu.make_async_copy(proj_hbm, proj_ref, sems.at[0]),
            pltpu.make_async_copy(v_hbm, v_ref, sems.at[1]),
            pltpu.make_async_copy(ham_hbm.at[0, :LANES, :], ham_ref.at[0], sems.at[2]),
            pltpu.make_async_copy(ham_hbm.at[1, NODES - LANES :, :], ham_ref.at[1], sems.at[3]),
        ]
    )
    hams = run(
        [
            pltpu.make_async_copy(
                ham_hbm.at[k], pack_ref.at[pl.ds(k * NODES, NODES), :], sems.at[4 + k]
            )
            for k in range(2)
        ]
    )
    place0, place1 = placers()
    wide_ref[...] = jnp.zeros(wide_ref.shape, F32)
    lane = iota((8, LANES), 1)
    atoms = jnp.full((8, LANES), -1, jnp.int32)
    for block in range(2 * SLOTS - 1):
        cell, slot = (0, block) if block < SLOTS else (1, block - SLOTS + 1)
        atoms = jnp.where(lane == block, atom_ref[cell, slot], atoms)
    atoms = atoms.astype(F32)
    width = v_ref.shape[0]
    proj_in.wait()
    pad = jnp.zeros((PADDED - ROWS, NODES), BF16)
    for k in range(2):
        start = PART + k * PADDED
        pack_ref[start : start + PADDED, :] = jnp.concatenate([proj_ref[k], pad], axis=0)
    p0 = dot(place0, proj_ref[0]).astype(BF16)
    p1 = dot(place1, proj_ref[1]).astype(BF16)
    v_in.wait()
    v0 = v_ref[:, :NODES]
    v1 = v_ref[:, NODES:]
    coef = dot_nt(p0, v0) + dot_nt(p1, v1)
    finish(edges)
    face = jnp.where(low_lanes(width), dot_nt(v0, ham_ref[0]), dot_nt(v1, ham_ref[1]))
    edge = jnp.where(
        low_lanes(ROWS),
        proj_ref[0, :, :LANES].astype(F32),
        proj_ref[1, :, NODES - LANES :].astype(F32),
    )
    for to in range(GROUP):
        for i in range(NPROJ):
            wide_ref[to, :8, i * PIECE : (i + 1) * PIECE] = coef[
                eight(i), to * PIECE : (to + 1) * PIECE
            ]
        for k in range(PIECE // 8):
            wide_ref[to, 8:16, tile(k)] = face[eight(to * (PIECE // 8) + k)]
        wide_ref[to, 8:16, tile(6)] = atoms
        for k in range(8):
            wide_ref[to, 16:24, tile(k)] = edge[eight(k)]
        wide_ref[to, 24:32, :LANES] = edge[eight(8)]
        out_ref[to, :HEAD, :] = wide_ref[to].astype(BF16)
        out_ref[to, HEAD:, :] = v_ref[to * PIECE : (to + 1) * PIECE, :]
    finish(hams)


def place_face(face, wide_ref):
    wide_ref[:BODY, WIDE:] = face[:BODY]
    for k in range(PIECE - BODY):
        row = (k % GROUP) * BLOCKS + BLOCKS - 1
        wide_ref[row : row + 1, tile(k // GROUP)] = face[BODY + k : BODY + k + 1]


def read_face(got_ref, group):
    body = got_ref[group, :BODY, :].astype(F32)
    rows = [body[:, WIDE:]]
    for k in range(PIECE - BODY):
        row = (k % GROUP) * BLOCKS + BLOCKS - 1
        rows.append(body[row : row + 1, tile(k // GROUP)])
    return jnp.concatenate(rows, axis=0)


def pack_kernel(in_ref, out_ref, wide_ref):
    last = GROUP - 1
    low = low_lanes(8)
    wide_ref[...] = jnp.zeros(wide_ref.shape, F32)
    pieces = [in_ref[part, :HEAD, :].astype(F32) for part in range(GROUP)]
    both = lambda rows, k: jnp.where(low, pieces[0][rows, tile(k)], pieces[last][rows, tile(k)])
    lane = iota((8, LANES), 1)
    atoms = jnp.full((8, LANES), -1.0, F32)
    for part in range(GROUP):
        wide_ref[eight(part), :WIDE] = pieces[part][:8, :WIDE]
        own = pieces[part][8:16, tile(6)]
        if part:
            own = pltpu.roll(own, part * BLOCKS, 1)
        atoms = jnp.where(lane // BLOCKS == part, own, atoms)
    face = jnp.concatenate([both(slice(8, 16), k) for k in range(PIECE // 8)], axis=0)
    place_face(face, wide_ref)
    ninth = both(slice(24, 32), 0)
    for k in range(8):
        wide_ref[BODY:, tile(k)] = both(slice(16, 24), k)
        row = (k % GROUP) * BLOCKS + BLOCKS - 1
        wide_ref[row : row + 1, tile(4 + k // GROUP)] = ninth[k : k + 1]
    wide_ref[BLOCKS - 1 : BLOCKS, tile(6)] = atoms[:1]
    out_ref[...] = wide_ref[...].astype(BF16)


def beside(place_ref, groups):
    z = place_ref[1]
    return z, jnp.maximum(z - 1, 0), jnp.minimum(z + 1, groups - 1)


def choose(place_ref, coupling_ref, got_ref, pick_ref, factor_ref):
    groups = got_ref.shape[0]
    z, below, above = beside(place_ref, groups)
    lane = iota((8, LANES), 1)
    named = lambda group: jnp.broadcast_to(
        got_ref[group, :16, tile(6)].astype(F32)[BLOCKS - 1 : BLOCKS], (8, LANES)
    )
    shift = lambda x, by: pltpu.roll(x, by, 1) if by else x
    per = LANES // BODY
    tiles = []
    for start in range(0, groups, per):
        x = jnp.full((8, LANES), -1.0, F32)
        for k in range(min(per, groups - start)):
            x = jnp.where(lane // BODY == k, shift(named(start + k), k * BODY), x)
        tiles.append(x)
    mine = jnp.where(lane < BODY, named(z), -1.0)
    mine = jnp.where(lane // BLOCKS == GROUP, shift(named(below), BLOCKS), mine)
    mine = jnp.where(lane // BLOCKS == GROUP + 1, shift(named(above), BODY + BLOCKS), mine)
    mine = jnp.where(mine < 0, -2.0, mine)
    column = jnp.transpose(jnp.concatenate([mine] * (LANES // 8), axis=0))[:PIECE]
    for k, x in enumerate(tiles):
        match = column == jnp.concatenate([x] * (PIECE // 8), axis=0)
        pick_ref[:, tile(k)] = jnp.where(match, 1.0, 0.0).astype(BF16)
    count = coupling_ref.shape[0]
    atom = iota((PIECE, LANES), 1).astype(F32)
    owner = jnp.where(column == atom, 1.0, 0.0)[:, :count]
    expand = jnp.where(iota((NPROJ, WIDE), 1) // PIECE == iota((NPROJ, WIDE), 0), 1.0, 0.0)
    factor_ref[...] = exact(exact(owner, coupling_ref[...]), expand)


def sum_coefs(got_ref, pick_ref, factor_ref, scaled_ref):
    groups = got_ref.shape[0]
    blocks = jnp.concatenate([got_ref[group, :BODY, :WIDE] for group in range(groups)], axis=0)
    total = dot(pick_ref[:, : groups * BODY], blocks) * factor_ref[...]
    for i in range(NPROJ):
        column = total[:, i * PIECE : (i + 1) * PIECE]
        for k in range(GROUP + 2):
            scaled_ref[k, eight(i), :] = column[eight(k)]
    return [scaled_ref[k].astype(BF16) for k in range(GROUP + 2)]


def add_faces(place_ref, got_ref, near_ref, scaled, local_ref):
    groups = got_ref.shape[0]
    z, below, above = beside(place_ref, groups)
    low = low_lanes(PIECE)
    from_below = read_face(got_ref, below) + dot_tn(scaled[GROUP], near_ref[0])
    from_above = read_face(got_ref, above) + dot_tn(scaled[GROUP + 1], near_ref[1])
    from_below = from_below * (z > 0).astype(F32)
    from_above = from_above * (z < groups - 1).astype(F32)
    cells = [(part, cell * NODES) for part in range(GROUP) for cell in range(2)]
    heads = [local_ref[part, :, a : a + LANES] for part, a in cells]
    tails = [local_ref[part, :, a + NODES - LANES : a + NODES] for part, a in cells]
    for k, (part, a) in enumerate(cells):
        under = tails[k - 1] if k > 0 else from_below
        over = heads[k + 1] if k + 1 < len(cells) else from_above
        local_ref[part, :, a : a + LANES] = heads[k] + jnp.where(
            low, pltpu.roll(under, FACE, 1), 0.0
        )
        local_ref[part, :, a + NODES - LANES : a + NODES] = tails[k] + jnp.where(
            low, 0.0, pltpu.roll(over, FACE, 1)
        )


def fetch_hams(packs, held_ref, sems):
    return run(
        [
            pltpu.make_async_copy(
                packs[k // 2].at[pl.ds((k % 2) * NODES, NODES), :], held_ref.at[k], sems.at[k]
            )
            for k in range(2 * GROUP)
        ]
    )


def add_local(me, v_ref, held_ref, local_ref):
    for r in range(GROUP):
        part = jnp.bitwise_xor(me, r)
        for cell in range(2):
            lanes = slice(cell * NODES, (cell + 1) * NODES)
            local_ref[part, :, lanes] += dot_nt(v_ref[part, :, lanes], held_ref[2 * r + cell])


def write_message(me, new, held_ref, proj_ref, edge_ref, wide_ref, message_ref):
    for r in range(GROUP):
        part = jnp.bitwise_xor(me, r)

        @pl.when(part == 0)
        def _():
            edge_ref[:FACE, :NODES] = held_ref[2 * r, :FACE, :]
            edge_ref[:FACE, NODES:] = jnp.zeros((FACE, NODES), BF16)

        @pl.when(part == GROUP - 1)
        def _():
            edge_ref[FACE:, :NODES] = jnp.zeros((FACE, NODES), BF16)
            edge_ref[FACE:, NODES:] = held_ref[2 * r + 1, NODES - FACE :, :]

    ends = jnp.concatenate([new[0][:, :NODES], new[GROUP - 1][:, NODES:]], axis=1)
    face = dot_nt(ends, edge_ref[...])
    wide_ref[:, SPAN:WIDE] = jnp.zeros((BODY, WIDE - SPAN), F32)
    for part in range(GROUP):
        coef = dot_nt(proj_ref[part], new[part])
        for i in range(NPROJ):
            wide_ref[eight(part), i * PIECE : (i + 1) * PIECE] = coef[eight(i)]
    place_face(face, wide_ref)
    message_ref[...] = wide_ref[...].astype(BF16)


def first_kernel(factors, place_ref, coupling_ref, got_ref, open_hbm, *refs):
    packs, refs = refs[:GROUP], refs[GROUP:]
    next_ref, message_ref, v_ref, held_ref, proj_ref, near_ref, pick_ref, factor_ref = refs[:8]
    local_ref, edge_ref, wide_ref, scaled_ref, raw_ref, sems = refs[8:]
    groups = got_ref.shape[0]
    me = place_ref[0]
    _, below, above = beside(place_ref, groups)
    copies = []
    for r in range(GROUP):
        at = 2 * GROUP + 2 * r
        copies += [
            pltpu.make_async_copy(packs[r].at[pl.ds(PART, 2 * PADDED), :], raw_ref.at[r], sems.at[at]),
            pltpu.make_async_copy(
                open_hbm.at[r, pl.ds(HEAD, PIECE), :], v_ref.at[r], sems.at[at + 1]
            ),
        ]
    run(copies)
    hams = fetch_hams(packs, held_ref, sems)

    place0, place1 = placers()
    for k, group, place in ((0, below, place1), (1, above, place0)):
        rows = got_ref[group].astype(F32)
        raw = [rows[BODY:, tile(j)] for j in range(8)]
        for j in range(8):
            row = (j % GROUP) * BLOCKS + BLOCKS - 1
            raw.append(rows[row : row + 1, tile(4 + j // GROUP)])
        near_ref[k] = dot(place, jnp.concatenate(raw, axis=0).astype(BF16)).astype(BF16)
    choose(place_ref, coupling_ref, got_ref, pick_ref, factor_ref)
    scaled = sum_coefs(got_ref, pick_ref, factor_ref, scaled_ref)

    finish(copies)
    for r in range(GROUP):
        part = jnp.bitwise_xor(me, r)
        for cell, place in ((0, place0), (1, place1)):
            raw = raw_ref[r, cell * PADDED : (cell + 1) * PADDED, :][:ROWS]
            lanes = slice(cell * NODES, (cell + 1) * NODES)
            proj_ref[part, :, lanes] = dot(place, raw).astype(BF16)
    for part in range(GROUP):
        local_ref[part] = dot_tn(scaled[part], proj_ref[part])
    finish(hams)
    add_local(me, v_ref, held_ref, local_ref)
    add_faces(place_ref, got_ref, near_ref, scaled, local_ref)
    gain, _ = factors[0]
    new = []
    for part in range(GROUP):
        new.append(((local_ref[part] - CENTER * v_ref[part].astype(F32)) * gain).astype(BF16))
        next_ref[part] = new[part]
    write_message(me, new, held_ref, proj_ref, edge_ref, wide_ref, message_ref)


def step_kernel(degree, factors, place_ref, got_ref, *refs):
    last = degree == DEGREE - 1
    v_ref, old_ref, held_ref, proj_ref, near_ref, pick_ref, factor_ref = refs[:7]
    refs = refs[7:]
    if last:
        occ_ref, density_ref, *next_refs = refs[: 2 + GROUP]
        refs = refs[2 + GROUP :]
    else:
        next_ref, message_ref = refs[:2]
        refs = refs[2:]
    local_ref, edge_ref, wide_ref, scaled_ref = refs
    me = place_ref[0]
    scaled = sum_coefs(got_ref, pick_ref, factor_ref, scaled_ref)
    for part in range(GROUP):
        local_ref[part] = dot_tn(scaled[part], proj_ref[part])
    add_local(me, v_ref, held_ref, local_ref)
    add_faces(place_ref, got_ref, near_ref, scaled, local_ref)

    gain, back = factors[degree]

    def image(part):
        now = v_ref[part].astype(F32)
        value = (local_ref[part] - CENTER * now) * gain - back * old_ref[part].astype(F32)
        return value.astype(BF16)

    if not last:
        new = [image(part) for part in range(GROUP)]
        for part in range(GROUP):
            next_ref[part] = new[part]
        write_message(me, new, held_ref, proj_ref, edge_ref, wide_ref, message_ref)
        return
    weight = jnp.transpose(jnp.broadcast_to(pick(occ_ref[...], me), (LANES, LANES)))[:PIECE]
    for r in range(GROUP):
        part = jnp.bitwise_xor(me, r)
        new = image(part)
        next_refs[r][...] = new
        values = new.astype(F32)
        for k in range(PART // LANES):
            term = values[:, tile(k)]
            sums = jnp.sum(term * term * weight, axis=0, keepdims=True)
            density_ref[part, 2 * k : 2 * k + 1, :] = sums[:, :FACE]
            density_ref[part, 2 * k + 1 : 2 * k + 2, :] = sums[:, FACE:]


def join_kernel(place_ref, *refs):
    ins, (out_ref, sems) = refs[:GROUP], refs[GROUP:]
    copies = []
    for r in range(GROUP):
        start = pl.multiple_of(jnp.bitwise_xor(place_ref[0], r) * PIECE, 16)
        copies.append(
            pltpu.make_async_copy(ins[GROUP - 1 - r], out_ref.at[pl.ds(start, PIECE), :], sems.at[r])
        )
    run(copies)
    finish(copies)


def vmem():
    return pl.BlockSpec(memory_space=pltpu.VMEM)


def hbm():
    return pl.BlockSpec(memory_space=pltpu.HBM)


def smem():
    return pl.BlockSpec(memory_space=pltpu.SMEM)


def shape(dims, dtype=BF16):
    return jax.ShapeDtypeStruct(dims, dtype)


def shards(interpret, states, cell_ham, projectors, slot_atom, coupling, occupancy):
    width = states.shape[1]
    groups = lax.axis_size("z")
    spread = lax.axis_size("x") * lax.axis_size("yh")
    dma = pltpu.SemaphoreType.DMA
    near = ("yl", "c")
    ring = 2 * lax.axis_size("yh")

    def call(kernel, megabytes=24, **kw):
        params = pltpu.CompilerParams(vmem_limit_bytes=megabytes * 1024 * 1024)
        return pl.pallas_call(kernel, compiler_params=params, interpret=interpret, **kw)

    me = 2 * lax.axis_index("yl") + lax.axis_index("c")
    place = jnp.stack([me, lax.axis_index("z")]).astype(jnp.int32)
    occ = jnp.pad(occupancy.reshape(GROUP, PIECE), ((0, 0), (0, LANES - PIECE)))
    v_t = states.T
    opened, pack = call(
        open_kernel,
        megabytes=60,
        out_shape=[shape((GROUP, HEAD + PIECE, PART)), shape((PACK, NODES))],
        in_specs=[smem()] + [hbm()] * 3,
        out_specs=[vmem()] * 2,
        scratch_shapes=[
            pltpu.VMEM((width, PART), BF16),
            pltpu.VMEM((2, LANES, NODES), BF16),
            pltpu.VMEM((2, ROWS, NODES), BF16),
            pltpu.VMEM((GROUP, HEAD, PART), F32),
            dma((6,)),
        ],
    )(slot_atom, v_t, cell_ham, projectors)
    opened = lax.all_to_all(opened, near, 0, 0)
    message = call(
        pack_kernel,
        out_shape=shape((BODY + 8, PART)),
        in_specs=[vmem()],
        out_specs=vmem(),
        scratch_shapes=[pltpu.VMEM((BODY + 8, PART), F32)],
    )(opened)
    spot = lambda y, core: ((y % 2) * 2 + core) * (ring // 2) + y // 2

    def across(flip):
        return [
            (spot(y, c), spot((y + 1 - 2 * c) % ring, c ^ flip)) for y in range(ring) for c in (0, 1)
        ]

    beside_core = lax.ppermute(pack, "c", [(0, 1), (1, 0)])
    axes = ("yl", "c", "yh")
    packs = [
        pack,
        beside_core,
        lax.ppermute(pack, axes, across(0)),
        lax.ppermute(pack, axes, across(1)),
    ]

    factors = chebyshev_factors()
    state_shape = shape((GROUP, PIECE, PART))
    message_shape = shape((BODY, PART))
    scratch = [
        pltpu.VMEM((GROUP, PIECE, PART), F32),
        pltpu.VMEM((LANES, PART), BF16),
        pltpu.VMEM((BODY, PART), F32),
        pltpu.VMEM((GROUP + 2, PROJ, PIECE), F32),
    ]
    got = lax.all_gather(message, "z")
    v, message, old, *kept = call(
        functools.partial(first_kernel, factors),
        out_shape=[
            state_shape,
            message_shape,
            state_shape,
            shape((2 * GROUP, NODES, NODES)),
            shape((GROUP, PROJ, PART)),
            shape((2, PROJ, LANES)),
            shape((PIECE, -(-groups * BODY // LANES) * LANES)),
            shape((PIECE, WIDE), F32),
        ],
        in_specs=[smem()] + [vmem()] * 2 + [hbm()] * (GROUP + 1),
        out_specs=[vmem()] * 8,
        scratch_shapes=scratch
        + [pltpu.VMEM((GROUP, 2 * PADDED, NODES), BF16), dma((4 * GROUP,))],
    )(place, coupling, got, opened, *packs)
    for degree in range(1, DEGREE):
        got = lax.all_gather(message, "z")
        last = degree == DEGREE - 1
        outs = [state_shape, message_shape]
        if last:
            outs = [shape((GROUP, PART // FACE, FACE), F32)] + [shape((PIECE, PART))] * GROUP
        ends = [occ] if last else []
        result = call(
            functools.partial(step_kernel, degree, factors),
            out_shape=outs,
            in_specs=[smem()] + [vmem()] * (8 + len(ends)),
            out_specs=[vmem()] * len(outs),
            scratch_shapes=scratch,
        )(place, got, v, old, *kept, *ends)
        old, v, message = v, result[0], result[1]

    density, *pieces = result
    for r in (3, 2, 1):
        pieces[r] = lax.ppermute(pieces[r], near, [(k, k ^ r) for k in range(GROUP)])
    filtered = call(
        join_kernel,
        out_shape=shape((width, PART)),
        in_specs=[smem()] + [hbm()] * GROUP,
        out_specs=hbm(),
        scratch_shapes=[dma((GROUP,))],
    )(place, *pieces[::-1])
    parts = GROUP * spread
    terms = lax.all_to_all(
        density.reshape(parts, GROUP * PART // parts), near + ("x", "yh"), 0, 0, tiled=True
    )
    density = jnp.sum(terms, axis=0) / (width * spread)
    return filtered.T, density


def build(mesh, interpret=False):
    part = ("z", "yl", "c")
    group = ("x", "yh")
    return jax.shard_map(
        functools.partial(shards, interpret),
        mesh=mesh,
        in_specs=(
            P(part, group),
            P(part, None, None),
            P(part, None, None),
            P(part, None),
            P(),
            P(group),
        ),
        out_specs=(P(part, group), P(part + group)),
        check_vma=False,
    )


def solution(mesh):
    count, groups = mesh.shape["mesh"], mesh.shape["state"]
    devices = mesh.devices.reshape(count // GROUP, 2, 2, groups // 4, 4)
    return build(Mesh(devices, ("z", "yl", "c", "x", "yh")))
```

```python
import functools

import jax
import jax.numpy as jnp
from jax import lax
from jax.experimental import pallas as pl
from jax.experimental.pallas import tpu as pltpu
from jax.sharding import Mesh, PartitionSpec as P

FACE = 64
DEGREE = 4
LANES = 128
NODES = 512
NPROJ = 18
SLOTS = 4
ROWS = SLOTS * NPROJ
GROUP = 4
PART = 2 * NODES
PIECE = 48
BLOCKS = 8
PROJ = NPROJ * BLOCKS
SPAN = NPROJ * PIECE
WIDE = 7 * LANES
BODY = GROUP * BLOCKS
PADDED = 80
PACK = PART + 2 * PADDED
HEAD = 32
CENTER = 0.5
HALF_WIDTH = 1.5
LOW_EDGE = -1.2

BF16 = jnp.bfloat16
F32 = jnp.float32
NT = (((1,), (1,)), ((), ()))
TN = (((0,), (0,)), ((), ()))


def chebyshev_factors():
    sigma = HALF_WIDTH / (LOW_EDGE - CENTER)
    gamma = 2.0 / sigma
    factors = [(sigma / HALF_WIDTH, 0.0)]
    for _ in range(1, DEGREE):
        sigma_new = 1.0 / (gamma - sigma)
        factors.append((2.0 * sigma_new / HALF_WIDTH, sigma * sigma_new))
        sigma = sigma_new
    return factors


def iota(shape, dim):
    return lax.broadcasted_iota(jnp.int32, shape, dim)


def dot(a, b):
    return jnp.dot(a, b, preferred_element_type=F32)


def dot_nt(a, b):
    return lax.dot_general(a, b, NT, preferred_element_type=F32)


def dot_tn(a, b):
    return lax.dot_general(a, b, TN, preferred_element_type=F32)


def exact(a, b):
    return jnp.dot(a, b, precision=lax.Precision.HIGHEST, preferred_element_type=F32)


def placers():
    row = iota((PROJ, ROWS), 0)
    col = iota((PROJ, ROWS), 1)
    which = row // BLOCKS
    block = row % BLOCKS
    first = (block < SLOTS) & (col == block * NPROJ + which)
    slot = block - SLOTS + 1
    second = ((block == 0) & (col == which)) | (
        (block >= SLOTS) & (block < 2 * SLOTS - 1) & (col == slot * NPROJ + which)
    )
    return first.astype(F32).astype(BF16), second.astype(F32).astype(BF16)


def low_lanes(rows):
    return iota((rows, LANES), 1) < FACE


def pick(rows, at):
    return jnp.sum(jnp.where(iota(rows.shape, 0) == at, rows, 0.0), axis=0, keepdims=True)


def run(copies):
    for copy in copies:
        copy.start()
    return copies


def finish(copies):
    for copy in copies:
        copy.wait()


def tile(k):
    return slice(k * LANES, (k + 1) * LANES)


def eight(k):
    return slice(k * 8, (k + 1) * 8)


def open_kernel(
    atom_ref, v_hbm, ham_hbm, proj_hbm, out_ref, pack_ref, v_ref, ham_ref, proj_ref, wide_ref, sems
):
    proj_in, v_in, *edges = run(
        [
            pltpu.make_async_copy(proj_hbm, proj_ref, sems.at[0]),
            pltpu.make_async_copy(v_hbm, v_ref, sems.at[1]),
            pltpu.make_async_copy(ham_hbm.at[0, :LANES, :], ham_ref.at[0], sems.at[2]),
            pltpu.make_async_copy(ham_hbm.at[1, NODES - LANES :, :], ham_ref.at[1], sems.at[3]),
        ]
    )
    hams = run(
        [
            pltpu.make_async_copy(
                ham_hbm.at[k], pack_ref.at[pl.ds(k * NODES, NODES), :], sems.at[4 + k]
            )
            for k in range(2)
        ]
    )
    place0, place1 = placers()
    wide_ref[...] = jnp.zeros(wide_ref.shape, F32)
    lane = iota((8, LANES), 1)
    atoms = jnp.full((8, LANES), -1, jnp.int32)
    for block in range(2 * SLOTS - 1):
        cell, slot = (0, block) if block < SLOTS else (1, block - SLOTS + 1)
        atoms = jnp.where(lane == block, atom_ref[cell, slot], atoms)
    atoms = atoms.astype(F32)
    width = v_ref.shape[0]
    proj_in.wait()
    pad = jnp.zeros((PADDED - ROWS, NODES), BF16)
    for k in range(2):
        start = PART + k * PADDED
        pack_ref[start : start + PADDED, :] = jnp.concatenate([proj_ref[k], pad], axis=0)
    p0 = dot(place0, proj_ref[0]).astype(BF16)
    p1 = dot(place1, proj_ref[1]).astype(BF16)
    v_in.wait()
    v0 = v_ref[:, :NODES]
    v1 = v_ref[:, NODES:]
    coef = dot_nt(p0, v0) + dot_nt(p1, v1)
    finish(edges)
    face = jnp.where(low_lanes(width), dot_nt(v0, ham_ref[0]), dot_nt(v1, ham_ref[1]))
    edge = jnp.where(
        low_lanes(ROWS),
        proj_ref[0, :, :LANES].astype(F32),
        proj_ref[1, :, NODES - LANES :].astype(F32),
    )
    for to in range(GROUP):
        for i in range(NPROJ):
            wide_ref[to, :8, i * PIECE : (i + 1) * PIECE] = coef[
                eight(i), to * PIECE : (to + 1) * PIECE
            ]
        for k in range(PIECE // 8):
            wide_ref[to, 8:16, tile(k)] = face[eight(to * (PIECE // 8) + k)]
        wide_ref[to, 8:16, tile(6)] = atoms
        for k in range(8):
            wide_ref[to, 16:24, tile(k)] = edge[eight(k)]
        wide_ref[to, 24:32, :LANES] = edge[eight(8)]
        out_ref[to, :HEAD, :] = wide_ref[to].astype(BF16)
        out_ref[to, HEAD:, :] = v_ref[to * PIECE : (to + 1) * PIECE, :]
    finish(hams)


def read(got_ref, group, rows, lane, width):
    start = group * PART + lane
    if not isinstance(group, int):
        start = pl.multiple_of(start, LANES)
    return got_ref[:rows, pl.ds(start, width)]


def place_face(face, wide_ref):
    wide_ref[:BODY, WIDE:] = face[:BODY]
    for k in range(PIECE - BODY):
        row = (k % GROUP) * BLOCKS + BLOCKS - 1
        wide_ref[row : row + 1, tile(k // GROUP)] = face[BODY + k : BODY + k + 1]


def read_face(got_ref, group):
    body = read(got_ref, group, BODY, 0, PART).astype(F32)
    rows = [body[:, WIDE:]]
    for k in range(PIECE - BODY):
        row = (k % GROUP) * BLOCKS + BLOCKS - 1
        rows.append(body[row : row + 1, tile(k // GROUP)])
    return jnp.concatenate(rows, axis=0)


def pack_kernel(in_ref, out_ref, wide_ref):
    last = GROUP - 1
    low = low_lanes(8)
    wide_ref[...] = jnp.zeros(wide_ref.shape, F32)
    pieces = [in_ref[part, :HEAD, :].astype(F32) for part in range(GROUP)]
    both = lambda rows, k: jnp.where(low, pieces[0][rows, tile(k)], pieces[last][rows, tile(k)])
    lane = iota((8, LANES), 1)
    atoms = jnp.full((8, LANES), -1.0, F32)
    for part in range(GROUP):
        wide_ref[eight(part), :WIDE] = pieces[part][:8, :WIDE]
        own = pieces[part][8:16, tile(6)]
        if part:
            own = pltpu.roll(own, part * BLOCKS, 1)
        atoms = jnp.where(lane // BLOCKS == part, own, atoms)
    face = jnp.concatenate([both(slice(8, 16), k) for k in range(PIECE // 8)], axis=0)
    place_face(face, wide_ref)
    ninth = both(slice(24, 32), 0)
    for k in range(8):
        wide_ref[BODY:, tile(k)] = both(slice(16, 24), k)
        row = (k % GROUP) * BLOCKS + BLOCKS - 1
        wide_ref[row : row + 1, tile(4 + k // GROUP)] = ninth[k : k + 1]
    wide_ref[BLOCKS - 1 : BLOCKS, tile(6)] = atoms[:1]
    out_ref[...] = wide_ref[...].astype(BF16)


def beside(place_ref, groups):
    z = place_ref[1]
    return z, jnp.maximum(z - 1, 0), jnp.minimum(z + 1, groups - 1)


def choose(place_ref, coupling_ref, got_ref, pick_ref, factor_ref):
    groups = got_ref.shape[1] // PART
    z, below, above = beside(place_ref, groups)
    lane = iota((8, LANES), 1)
    named = lambda group: jnp.broadcast_to(
        read(got_ref, group, 16, 6 * LANES, LANES).astype(F32)[BLOCKS - 1 : BLOCKS], (8, LANES)
    )
    shift = lambda x, by: pltpu.roll(x, by, 1) if by else x
    per = LANES // BODY
    tiles = []
    for start in range(0, groups, per):
        x = jnp.full((8, LANES), -1.0, F32)
        for k in range(min(per, groups - start)):
            x = jnp.where(lane // BODY == k, shift(named(start + k), k * BODY), x)
        tiles.append(x)
    mine = jnp.where(lane < BODY, named(z), -1.0)
    mine = jnp.where(lane // BLOCKS == GROUP, shift(named(below), BLOCKS), mine)
    mine = jnp.where(lane // BLOCKS == GROUP + 1, shift(named(above), BODY + BLOCKS), mine)
    mine = jnp.where(mine < 0, -2.0, mine)
    column = jnp.transpose(jnp.concatenate([mine] * (LANES // 8), axis=0))[:PIECE]
    for k, x in enumerate(tiles):
        match = column == jnp.concatenate([x] * (PIECE // 8), axis=0)
        pick_ref[:, tile(k)] = jnp.where(match, 1.0, 0.0).astype(BF16)
    count = coupling_ref.shape[0]
    atom = iota((PIECE, LANES), 1).astype(F32)
    owner = jnp.where(column == atom, 1.0, 0.0)[:, :count]
    expand = jnp.where(iota((NPROJ, WIDE), 1) // PIECE == iota((NPROJ, WIDE), 0), 1.0, 0.0)
    factor_ref[...] = exact(exact(owner, coupling_ref[...]), expand)


def sum_coefs(got_ref, pick_ref, factor_ref, scaled_ref):
    groups = got_ref.shape[1] // PART
    blocks = jnp.concatenate([read(got_ref, g, BODY, 0, WIDE) for g in range(groups)], axis=0)
    total = dot(pick_ref[:, : groups * BODY], blocks) * factor_ref[...]
    for i in range(NPROJ):
        column = total[:, i * PIECE : (i + 1) * PIECE]
        for k in range(GROUP + 2):
            scaled_ref[k, eight(i), :] = column[eight(k)]
    return [scaled_ref[k].astype(BF16) for k in range(GROUP + 2)]


def add_faces(place_ref, got_ref, near_ref, scaled, local_ref):
    groups = got_ref.shape[1] // PART
    z, below, above = beside(place_ref, groups)
    low = low_lanes(PIECE)
    from_below = read_face(got_ref, below) + dot_tn(scaled[GROUP], near_ref[0])
    from_above = read_face(got_ref, above) + dot_tn(scaled[GROUP + 1], near_ref[1])
    from_below = from_below * (z > 0).astype(F32)
    from_above = from_above * (z < groups - 1).astype(F32)
    cells = [(part, cell * NODES) for part in range(GROUP) for cell in range(2)]
    heads = [local_ref[part, :, a : a + LANES] for part, a in cells]
    tails = [local_ref[part, :, a + NODES - LANES : a + NODES] for part, a in cells]
    for k, (part, a) in enumerate(cells):
        under = tails[k - 1] if k > 0 else from_below
        over = heads[k + 1] if k + 1 < len(cells) else from_above
        local_ref[part, :, a : a + LANES] = heads[k] + jnp.where(
            low, pltpu.roll(under, FACE, 1), 0.0
        )
        local_ref[part, :, a + NODES - LANES : a + NODES] = tails[k] + jnp.where(
            low, 0.0, pltpu.roll(over, FACE, 1)
        )


def fetch_hams(packs, held_ref, sems):
    return run(
        [
            pltpu.make_async_copy(
                packs[k // 2].at[pl.ds((k % 2) * NODES, NODES), :], held_ref.at[k], sems.at[k]
            )
            for k in range(2 * GROUP)
        ]
    )


def add_local(me, v_ref, held_ref, local_ref):
    for r in range(GROUP):
        part = jnp.bitwise_xor(me, r)
        for cell in range(2):
            lanes = slice(cell * NODES, (cell + 1) * NODES)
            local_ref[part, :, lanes] += dot_nt(v_ref[part, :, lanes], held_ref[2 * r + cell])


def write_message(me, new, held_ref, proj_ref, edge_ref, wide_ref, message_ref):
    for r in range(GROUP):
        part = jnp.bitwise_xor(me, r)

        @pl.when(part == 0)
        def _():
            edge_ref[:FACE, :NODES] = held_ref[2 * r, :FACE, :]
            edge_ref[:FACE, NODES:] = jnp.zeros((FACE, NODES), BF16)

        @pl.when(part == GROUP - 1)
        def _():
            edge_ref[FACE:, :NODES] = jnp.zeros((FACE, NODES), BF16)
            edge_ref[FACE:, NODES:] = held_ref[2 * r + 1, NODES - FACE :, :]

    ends = jnp.concatenate([new[0][:, :NODES], new[GROUP - 1][:, NODES:]], axis=1)
    face = dot_nt(ends, edge_ref[...])
    wide_ref[:, SPAN:WIDE] = jnp.zeros((BODY, WIDE - SPAN), F32)
    for part in range(GROUP):
        coef = dot_nt(proj_ref[part], new[part])
        for i in range(NPROJ):
            wide_ref[eight(part), i * PIECE : (i + 1) * PIECE] = coef[eight(i)]
    place_face(face, wide_ref)
    message_ref[...] = wide_ref[...].astype(BF16)


def first_kernel(factors, place_ref, coupling_ref, got_ref, open_hbm, *refs):
    packs, refs = refs[:GROUP], refs[GROUP:]
    next_ref, message_ref, v_ref, held_ref, proj_ref, near_ref, pick_ref, factor_ref = refs[:8]
    local_ref, edge_ref, wide_ref, scaled_ref, raw_ref, sems = refs[8:]
    groups = got_ref.shape[1] // PART
    me = place_ref[0]
    _, below, above = beside(place_ref, groups)
    copies = []
    for r in range(GROUP):
        at = 2 * GROUP + 2 * r
        copies += [
            pltpu.make_async_copy(packs[r].at[pl.ds(PART, 2 * PADDED), :], raw_ref.at[r], sems.at[at]),
            pltpu.make_async_copy(
                open_hbm.at[r, pl.ds(HEAD, PIECE), :], v_ref.at[r], sems.at[at + 1]
            ),
        ]
    run(copies)
    hams = fetch_hams(packs, held_ref, sems)

    place0, place1 = placers()
    for k, group, place in ((0, below, place1), (1, above, place0)):
        rows = read(got_ref, group, BODY + 8, 0, PART).astype(F32)
        raw = [rows[BODY:, tile(j)] for j in range(8)]
        for j in range(8):
            row = (j % GROUP) * BLOCKS + BLOCKS - 1
            raw.append(rows[row : row + 1, tile(4 + j // GROUP)])
        near_ref[k] = dot(place, jnp.concatenate(raw, axis=0).astype(BF16)).astype(BF16)
    choose(place_ref, coupling_ref, got_ref, pick_ref, factor_ref)
    scaled = sum_coefs(got_ref, pick_ref, factor_ref, scaled_ref)

    finish(copies)
    for r in range(GROUP):
        part = jnp.bitwise_xor(me, r)
        for cell, place in ((0, place0), (1, place1)):
            raw = raw_ref[r, cell * PADDED : (cell + 1) * PADDED, :][:ROWS]
            lanes = slice(cell * NODES, (cell + 1) * NODES)
            proj_ref[part, :, lanes] = dot(place, raw).astype(BF16)
    for part in range(GROUP):
        local_ref[part] = dot_tn(scaled[part], proj_ref[part])
    finish(hams)
    add_local(me, v_ref, held_ref, local_ref)
    add_faces(place_ref, got_ref, near_ref, scaled, local_ref)
    gain, _ = factors[0]
    new = []
    for part in range(GROUP):
        new.append(((local_ref[part] - CENTER * v_ref[part].astype(F32)) * gain).astype(BF16))
        next_ref[part] = new[part]
    write_message(me, new, held_ref, proj_ref, edge_ref, wide_ref, message_ref)


def step_kernel(degree, factors, place_ref, got_ref, *refs):
    last = degree == DEGREE - 1
    v_ref, old_ref, held_ref, proj_ref, near_ref, pick_ref, factor_ref = refs[:7]
    refs = refs[7:]
    if last:
        occ_ref, density_ref, *next_refs = refs[: 2 + GROUP]
        refs = refs[2 + GROUP :]
    else:
        next_ref, message_ref = refs[:2]
        refs = refs[2:]
    local_ref, edge_ref, wide_ref, scaled_ref = refs
    me = place_ref[0]
    scaled = sum_coefs(got_ref, pick_ref, factor_ref, scaled_ref)
    for part in range(GROUP):
        local_ref[part] = dot_tn(scaled[part], proj_ref[part])
    add_local(me, v_ref, held_ref, local_ref)
    add_faces(place_ref, got_ref, near_ref, scaled, local_ref)

    gain, back = factors[degree]

    def image(part):
        now = v_ref[part].astype(F32)
        value = (local_ref[part] - CENTER * now) * gain - back * old_ref[part].astype(F32)
        return value.astype(BF16)

    if not last:
        new = [image(part) for part in range(GROUP)]
        for part in range(GROUP):
            next_ref[part] = new[part]
        write_message(me, new, held_ref, proj_ref, edge_ref, wide_ref, message_ref)
        return
    weight = jnp.transpose(jnp.broadcast_to(pick(occ_ref[...], me), (LANES, LANES)))[:PIECE]
    for r in range(GROUP):
        part = jnp.bitwise_xor(me, r)
        new = image(part)
        next_refs[r][...] = new
        values = new.astype(F32)
        for k in range(PART // LANES):
            term = values[:, tile(k)]
            sums = jnp.sum(term * term * weight, axis=0, keepdims=True)
            density_ref[part, 2 * k : 2 * k + 1, :] = sums[:, :FACE]
            density_ref[part, 2 * k + 1 : 2 * k + 2, :] = sums[:, FACE:]


def join_kernel(place_ref, *refs):
    ins, (out_ref, sems) = refs[:GROUP], refs[GROUP:]
    copies = []
    for r in range(GROUP):
        start = pl.multiple_of(jnp.bitwise_xor(place_ref[0], r) * PIECE, 16)
        copies.append(
            pltpu.make_async_copy(ins[GROUP - 1 - r], out_ref.at[pl.ds(start, PIECE), :], sems.at[r])
        )
    run(copies)
    finish(copies)


def vmem():
    return pl.BlockSpec(memory_space=pltpu.VMEM)


def hbm():
    return pl.BlockSpec(memory_space=pltpu.HBM)


def smem():
    return pl.BlockSpec(memory_space=pltpu.SMEM)


def shape(dims, dtype=BF16):
    return jax.ShapeDtypeStruct(dims, dtype)


def shards(interpret, states, cell_ham, projectors, slot_atom, coupling, occupancy):
    width = states.shape[1]
    groups = lax.axis_size("z")
    spread = lax.axis_size("x") * lax.axis_size("yh")
    dma = pltpu.SemaphoreType.DMA
    near = ("yl", "c")
    ring = 2 * lax.axis_size("yh")

    def call(kernel, megabytes=24, **kw):
        params = pltpu.CompilerParams(vmem_limit_bytes=megabytes * 1024 * 1024)
        return pl.pallas_call(kernel, compiler_params=params, interpret=interpret, **kw)

    me = 2 * lax.axis_index("yl") + lax.axis_index("c")
    place = jnp.stack([me, lax.axis_index("z")]).astype(jnp.int32)
    occ = jnp.pad(occupancy.reshape(GROUP, PIECE), ((0, 0), (0, LANES - PIECE)))
    v_t = states.T
    opened, pack = call(
        open_kernel,
        megabytes=60,
        out_shape=[shape((GROUP, HEAD + PIECE, PART)), shape((PACK, NODES))],
        in_specs=[smem()] + [hbm()] * 3,
        out_specs=[vmem()] * 2,
        scratch_shapes=[
            pltpu.VMEM((width, PART), BF16),
            pltpu.VMEM((2, LANES, NODES), BF16),
            pltpu.VMEM((2, ROWS, NODES), BF16),
            pltpu.VMEM((GROUP, HEAD, PART), F32),
            dma((6,)),
        ],
    )(slot_atom, v_t, cell_ham, projectors)
    opened = lax.all_to_all(opened, near, 0, 0)
    message = call(
        pack_kernel,
        out_shape=shape((BODY + 8, PART)),
        in_specs=[vmem()],
        out_specs=vmem(),
        scratch_shapes=[pltpu.VMEM((BODY + 8, PART), F32)],
    )(opened)
    spot = lambda y, core: ((y % 2) * 2 + core) * (ring // 2) + y // 2

    def across(flip):
        return [
            (spot(y, c), spot((y + 1 - 2 * c) % ring, c ^ flip)) for y in range(ring) for c in (0, 1)
        ]

    beside_core = lax.ppermute(pack, "c", [(0, 1), (1, 0)])
    axes = ("yl", "c", "yh")
    packs = [
        pack,
        beside_core,
        lax.ppermute(pack, axes, across(0)),
        lax.ppermute(pack, axes, across(1)),
    ]

    factors = chebyshev_factors()
    state_shape = shape((GROUP, PIECE, PART))
    message_shape = shape((BODY, PART))
    scratch = [
        pltpu.VMEM((GROUP, PIECE, PART), F32),
        pltpu.VMEM((LANES, PART), BF16),
        pltpu.VMEM((BODY, PART), F32),
        pltpu.VMEM((GROUP + 2, PROJ, PIECE), F32),
    ]
    got = lax.all_gather(message, "z", axis=1, tiled=True)
    v, message, old, *kept = call(
        functools.partial(first_kernel, factors),
        out_shape=[
            state_shape,
            message_shape,
            state_shape,
            shape((2 * GROUP, NODES, NODES)),
            shape((GROUP, PROJ, PART)),
            shape((2, PROJ, LANES)),
            shape((PIECE, -(-groups * BODY // LANES) * LANES)),
            shape((PIECE, WIDE), F32),
        ],
        in_specs=[smem()] + [vmem()] * 2 + [hbm()] * (GROUP + 1),
        out_specs=[vmem()] * 8,
        scratch_shapes=scratch
        + [pltpu.VMEM((GROUP, 2 * PADDED, NODES), BF16), dma((4 * GROUP,))],
    )(place, coupling, got, opened, *packs)
    for degree in range(1, DEGREE):
        got = lax.all_gather(message, "z", axis=1, tiled=True)
        last = degree == DEGREE - 1
        outs = [state_shape, message_shape]
        if last:
            outs = [shape((GROUP, PART // FACE, FACE), F32)] + [shape((PIECE, PART))] * GROUP
        ends = [occ] if last else []
        result = call(
            functools.partial(step_kernel, degree, factors),
            out_shape=outs,
            in_specs=[smem()] + [vmem()] * (8 + len(ends)),
            out_specs=[vmem()] * len(outs),
            scratch_shapes=scratch,
        )(place, got, v, old, *kept, *ends)
        old, v, message = v, result[0], result[1]

    density, *pieces = result
    for r in (3, 2, 1):
        pieces[r] = lax.ppermute(pieces[r], near, [(k, k ^ r) for k in range(GROUP)])
    filtered = call(
        join_kernel,
        out_shape=shape((width, PART)),
        in_specs=[smem()] + [hbm()] * GROUP,
        out_specs=hbm(),
        scratch_shapes=[dma((GROUP,))],
    )(place, *pieces[::-1])
    parts = GROUP * spread
    terms = lax.all_to_all(
        density.reshape(parts, GROUP * PART // parts), near + ("x", "yh"), 0, 0, tiled=True
    )
    density = jnp.sum(terms, axis=0) / (width * spread)
    return filtered.T, density


def build(mesh, interpret=False):
    part = ("z", "yl", "c")
    group = ("x", "yh")
    return jax.shard_map(
        functools.partial(shards, interpret),
        mesh=mesh,
        in_specs=(
            P(part, group),
            P(part, None, None),
            P(part, None, None),
            P(part, None),
            P(),
            P(group),
        ),
        out_specs=(P(part, group), P(part + group)),
        check_vma=False,
    )


def solution(mesh):
    count, groups = mesh.shape["mesh"], mesh.shape["state"]
    devices = mesh.devices.reshape(count // GROUP, 2, 2, groups // 4, 4)
    return build(Mesh(devices, ("z", "yl", "c", "x", "yh")))
```

```python
import functools

import jax
import jax.numpy as jnp
from jax import lax
from jax.experimental import pallas as pl
from jax.experimental.pallas import tpu as pltpu
from jax.sharding import Mesh, PartitionSpec as P

FACE = 64
DEGREE = 4
LANES = 128
NODES = 512
NPROJ = 18
SLOTS = 4
ROWS = SLOTS * NPROJ
GROUP = 4
PART = 2 * NODES
PIECE = 48
BLOCKS = 8
PROJ = NPROJ * BLOCKS
SPAN = NPROJ * PIECE
WIDE = 7 * LANES
BODY = GROUP * BLOCKS
PADDED = 80
PACK = PART + 2 * PADDED
HEAD = 32
CENTER = 0.5
HALF_WIDTH = 1.5
LOW_EDGE = -1.2

BF16 = jnp.bfloat16
F32 = jnp.float32
NT = (((1,), (1,)), ((), ()))
TN = (((0,), (0,)), ((), ()))


def chebyshev_factors():
    sigma = HALF_WIDTH / (LOW_EDGE - CENTER)
    gamma = 2.0 / sigma
    factors = [(sigma / HALF_WIDTH, 0.0)]
    for _ in range(1, DEGREE):
        sigma_new = 1.0 / (gamma - sigma)
        factors.append((2.0 * sigma_new / HALF_WIDTH, sigma * sigma_new))
        sigma = sigma_new
    return factors


def iota(shape, dim):
    return lax.broadcasted_iota(jnp.int32, shape, dim)


def dot(a, b):
    return jnp.dot(a, b, preferred_element_type=F32)


def dot_nt(a, b):
    return lax.dot_general(a, b, NT, preferred_element_type=F32)


def dot_tn(a, b):
    return lax.dot_general(a, b, TN, preferred_element_type=F32)


def exact(a, b):
    return jnp.dot(a, b, precision=lax.Precision.HIGHEST, preferred_element_type=F32)


def placers():
    row = iota((PROJ, ROWS), 0)
    col = iota((PROJ, ROWS), 1)
    which = row // BLOCKS
    block = row % BLOCKS
    first = (block < SLOTS) & (col == block * NPROJ + which)
    slot = block - SLOTS + 1
    second = ((block == 0) & (col == which)) | (
        (block >= SLOTS) & (block < 2 * SLOTS - 1) & (col == slot * NPROJ + which)
    )
    return first.astype(F32).astype(BF16), second.astype(F32).astype(BF16)


def low_lanes(rows):
    return iota((rows, LANES), 1) < FACE


def pick(rows, at):
    return jnp.sum(jnp.where(iota(rows.shape, 0) == at, rows, 0.0), axis=0, keepdims=True)


def run(copies):
    for copy in copies:
        copy.start()
    return copies


def finish(copies):
    for copy in copies:
        copy.wait()


def tile(k):
    return slice(k * LANES, (k + 1) * LANES)


def eight(k):
    return slice(k * 8, (k + 1) * 8)


def open_kernel(
    atom_ref, v_hbm, ham_hbm, proj_hbm, out_ref, pack_ref, v_ref, ham_ref, proj_ref, wide_ref, sems
):
    proj_in, v_in, *edges = run(
        [
            pltpu.make_async_copy(proj_hbm, proj_ref, sems.at[0]),
            pltpu.make_async_copy(v_hbm, v_ref, sems.at[1]),
            pltpu.make_async_copy(ham_hbm.at[0, :LANES, :], ham_ref.at[0], sems.at[2]),
            pltpu.make_async_copy(ham_hbm.at[1, NODES - LANES :, :], ham_ref.at[1], sems.at[3]),
        ]
    )
    hams = run(
        [
            pltpu.make_async_copy(
                ham_hbm.at[k], pack_ref.at[pl.ds(k * NODES, NODES), :], sems.at[4 + k]
            )
            for k in range(2)
        ]
    )
    place0, place1 = placers()
    wide_ref[...] = jnp.zeros(wide_ref.shape, F32)
    lane = iota((8, LANES), 1)
    atoms = jnp.full((8, LANES), -1, jnp.int32)
    for block in range(2 * SLOTS - 1):
        cell, slot = (0, block) if block < SLOTS else (1, block - SLOTS + 1)
        atoms = jnp.where(lane == block, atom_ref[cell, slot], atoms)
    atoms = atoms.astype(F32)
    width = v_ref.shape[0]
    proj_in.wait()
    pad = jnp.zeros((PADDED - ROWS, NODES), BF16)
    for k in range(2):
        start = PART + k * PADDED
        pack_ref[start : start + PADDED, :] = jnp.concatenate([proj_ref[k], pad], axis=0)
    p0 = dot(place0, proj_ref[0]).astype(BF16)
    p1 = dot(place1, proj_ref[1]).astype(BF16)
    v_in.wait()
    v0 = v_ref[:, :NODES]
    v1 = v_ref[:, NODES:]
    coef = dot_nt(p0, v0) + dot_nt(p1, v1)
    finish(edges)
    face = jnp.where(low_lanes(width), dot_nt(v0, ham_ref[0]), dot_nt(v1, ham_ref[1]))
    edge = jnp.where(
        low_lanes(ROWS),
        proj_ref[0, :, :LANES].astype(F32),
        proj_ref[1, :, NODES - LANES :].astype(F32),
    )
    for to in range(GROUP):
        for i in range(NPROJ):
            wide_ref[to, :8, i * PIECE : (i + 1) * PIECE] = coef[
                eight(i), to * PIECE : (to + 1) * PIECE
            ]
        for k in range(PIECE // 8):
            wide_ref[to, 8:16, tile(k)] = face[eight(to * (PIECE // 8) + k)]
        wide_ref[to, 8:16, tile(6)] = atoms
        for k in range(8):
            wide_ref[to, 16:24, tile(k)] = edge[eight(k)]
        wide_ref[to, 24:32, :LANES] = edge[eight(8)]
        out_ref[to, :HEAD, :] = wide_ref[to].astype(BF16)
        out_ref[to, HEAD:, :] = v_ref[to * PIECE : (to + 1) * PIECE, :]
    finish(hams)


def read(got_ref, group, rows, lane, width):
    start = group * PART + lane
    if not isinstance(group, int):
        start = pl.multiple_of(start, LANES)
    return got_ref[:rows, pl.ds(start, width)]


def place_face(face, wide_ref):
    wide_ref[:BODY, WIDE:] = face[:BODY]
    for k in range(PIECE - BODY):
        row = (k % GROUP) * BLOCKS + BLOCKS - 1
        wide_ref[row : row + 1, tile(k // GROUP)] = face[BODY + k : BODY + k + 1]


def read_face(got_ref, group):
    body = read(got_ref, group, BODY, 0, PART).astype(F32)
    rows = [body[:, WIDE:]]
    for k in range(PIECE - BODY):
        row = (k % GROUP) * BLOCKS + BLOCKS - 1
        rows.append(body[row : row + 1, tile(k // GROUP)])
    return jnp.concatenate(rows, axis=0)


def pack_kernel(in_ref, out_ref, wide_ref):
    last = GROUP - 1
    low = low_lanes(8)
    wide_ref[...] = jnp.zeros(wide_ref.shape, F32)
    pieces = [in_ref[part, :HEAD, :].astype(F32) for part in range(GROUP)]
    both = lambda rows, k: jnp.where(low, pieces[0][rows, tile(k)], pieces[last][rows, tile(k)])
    lane = iota((8, LANES), 1)
    atoms = jnp.full((8, LANES), -1.0, F32)
    for part in range(GROUP):
        wide_ref[eight(part), :WIDE] = pieces[part][:8, :WIDE]
        own = pieces[part][8:16, tile(6)]
        if part:
            own = pltpu.roll(own, part * BLOCKS, 1)
        atoms = jnp.where(lane // BLOCKS == part, own, atoms)
    face = jnp.concatenate([both(slice(8, 16), k) for k in range(PIECE // 8)], axis=0)
    place_face(face, wide_ref)
    ninth = both(slice(24, 32), 0)
    for k in range(8):
        wide_ref[BODY:, tile(k)] = both(slice(16, 24), k)
        row = (k % GROUP) * BLOCKS + BLOCKS - 1
        wide_ref[row : row + 1, tile(4 + k // GROUP)] = ninth[k : k + 1]
    wide_ref[BLOCKS - 1 : BLOCKS, tile(6)] = atoms[:1]
    out_ref[...] = wide_ref[...].astype(BF16)


def beside(place_ref, groups):
    z = place_ref[1]
    return z, jnp.maximum(z - 1, 0), jnp.minimum(z + 1, groups - 1)


def choose(place_ref, coupling_ref, got_ref, pick_ref, factor_ref):
    groups = got_ref.shape[1] // PART
    z, below, above = beside(place_ref, groups)
    lane = iota((8, LANES), 1)
    named = lambda group: jnp.broadcast_to(
        read(got_ref, group, 16, 6 * LANES, LANES).astype(F32)[BLOCKS - 1 : BLOCKS], (8, LANES)
    )
    shift = lambda x, by: pltpu.roll(x, by, 1) if by else x
    per = LANES // BODY
    tiles = []
    for start in range(0, groups, per):
        x = jnp.full((8, LANES), -1.0, F32)
        for k in range(min(per, groups - start)):
            x = jnp.where(lane // BODY == k, shift(named(start + k), k * BODY), x)
        tiles.append(x)
    mine = jnp.where(lane < BODY, named(z), -1.0)
    mine = jnp.where(lane // BLOCKS == GROUP, shift(named(below), BLOCKS), mine)
    mine = jnp.where(lane // BLOCKS == GROUP + 1, shift(named(above), BODY + BLOCKS), mine)
    mine = jnp.where(mine < 0, -2.0, mine)
    column = jnp.transpose(jnp.concatenate([mine] * (LANES // 8), axis=0))[:PIECE]
    for k, x in enumerate(tiles):
        match = column == jnp.concatenate([x] * (PIECE // 8), axis=0)
        pick_ref[:, tile(k)] = jnp.where(match, 1.0, 0.0).astype(BF16)
    count = coupling_ref.shape[0]
    atom = iota((PIECE, LANES), 1).astype(F32)
    owner = jnp.where(column == atom, 1.0, 0.0)[:, :count]
    expand = jnp.where(iota((NPROJ, WIDE), 1) // PIECE == iota((NPROJ, WIDE), 0), 1.0, 0.0)
    factor_ref[...] = exact(exact(owner, coupling_ref[...]), expand)


def sum_coefs(got_ref, pick_ref, factor_ref, scaled_ref):
    groups = got_ref.shape[1] // PART
    blocks = jnp.concatenate([read(got_ref, g, BODY, 0, WIDE) for g in range(groups)], axis=0)
    total = dot(pick_ref[:, : groups * BODY], blocks) * factor_ref[...]
    for i in range(NPROJ):
        column = total[:, i * PIECE : (i + 1) * PIECE]
        for k in range(GROUP + 2):
            scaled_ref[k, eight(i), :] = column[eight(k)]
    return [scaled_ref[k].astype(BF16) for k in range(GROUP + 2)]


def add_faces(place_ref, got_ref, near_ref, scaled, local_ref):
    groups = got_ref.shape[1] // PART
    z, below, above = beside(place_ref, groups)
    low = low_lanes(PIECE)
    from_below = read_face(got_ref, below) + dot_tn(scaled[GROUP], near_ref[0])
    from_above = read_face(got_ref, above) + dot_tn(scaled[GROUP + 1], near_ref[1])
    from_below = from_below * (z > 0).astype(F32)
    from_above = from_above * (z < groups - 1).astype(F32)
    cells = [(part, cell * NODES) for part in range(GROUP) for cell in range(2)]
    heads = [local_ref[part, :, a : a + LANES] for part, a in cells]
    tails = [local_ref[part, :, a + NODES - LANES : a + NODES] for part, a in cells]
    for k, (part, a) in enumerate(cells):
        under = tails[k - 1] if k > 0 else from_below
        over = heads[k + 1] if k + 1 < len(cells) else from_above
        local_ref[part, :, a : a + LANES] = heads[k] + jnp.where(
            low, pltpu.roll(under, FACE, 1), 0.0
        )
        local_ref[part, :, a + NODES - LANES : a + NODES] = tails[k] + jnp.where(
            low, 0.0, pltpu.roll(over, FACE, 1)
        )


def fetch_hams(packs, held_ref, sems):
    return run(
        [
            pltpu.make_async_copy(
                packs[k // 2].at[pl.ds((k % 2) * NODES, NODES), :], held_ref.at[k], sems.at[k]
            )
            for k in range(2 * GROUP)
        ]
    )


def add_local(me, v_ref, held_ref, local_ref):
    for r in range(GROUP):
        part = jnp.bitwise_xor(me, r)
        for cell in range(2):
            lanes = slice(cell * NODES, (cell + 1) * NODES)
            local_ref[part, :, lanes] += dot_nt(v_ref[part, :, lanes], held_ref[2 * r + cell])


def write_message(me, new, held_ref, proj_ref, edge_ref, wide_ref, message_ref):
    for r in range(GROUP):
        part = jnp.bitwise_xor(me, r)

        @pl.when(part == 0)
        def _():
            edge_ref[:FACE, :NODES] = held_ref[2 * r, :FACE, :]
            edge_ref[:FACE, NODES:] = jnp.zeros((FACE, NODES), BF16)

        @pl.when(part == GROUP - 1)
        def _():
            edge_ref[FACE:, :NODES] = jnp.zeros((FACE, NODES), BF16)
            edge_ref[FACE:, NODES:] = held_ref[2 * r + 1, NODES - FACE :, :]

    ends = jnp.concatenate([new[0][:, :NODES], new[GROUP - 1][:, NODES:]], axis=1)
    face = dot_nt(ends, edge_ref[...])
    wide_ref[:, SPAN:WIDE] = jnp.zeros((BODY, WIDE - SPAN), F32)
    for part in range(GROUP):
        coef = dot_nt(proj_ref[part], new[part])
        for i in range(NPROJ):
            wide_ref[eight(part), i * PIECE : (i + 1) * PIECE] = coef[eight(i)]
    place_face(face, wide_ref)
    message_ref[...] = wide_ref[...].astype(BF16)


def first_kernel(factors, place_ref, coupling_ref, got_ref, open_hbm, *refs):
    packs, refs = (refs[0], refs[3], refs[1], refs[2]), refs[GROUP:]
    next_ref, message_ref, v_ref, held_ref, proj_ref, near_ref, pick_ref, factor_ref = refs[:8]
    local_ref, edge_ref, wide_ref, scaled_ref, raw_ref, sems = refs[8:]
    groups = got_ref.shape[1] // PART
    me = place_ref[0]
    _, below, above = beside(place_ref, groups)
    copies = []
    for r in range(GROUP):
        at = 2 * GROUP + 2 * r
        copies += [
            pltpu.make_async_copy(packs[r].at[pl.ds(PART, 2 * PADDED), :], raw_ref.at[r], sems.at[at]),
            pltpu.make_async_copy(
                open_hbm.at[r, pl.ds(HEAD, PIECE), :], v_ref.at[r], sems.at[at + 1]
            ),
        ]
    run(copies)
    hams = fetch_hams(packs, held_ref, sems)

    place0, place1 = placers()
    for k, group, place in ((0, below, place1), (1, above, place0)):
        rows = read(got_ref, group, BODY + 8, 0, PART).astype(F32)
        raw = [rows[BODY:, tile(j)] for j in range(8)]
        for j in range(8):
            row = (j % GROUP) * BLOCKS + BLOCKS - 1
            raw.append(rows[row : row + 1, tile(4 + j // GROUP)])
        near_ref[k] = dot(place, jnp.concatenate(raw, axis=0).astype(BF16)).astype(BF16)
    choose(place_ref, coupling_ref, got_ref, pick_ref, factor_ref)
    scaled = sum_coefs(got_ref, pick_ref, factor_ref, scaled_ref)

    finish(copies)
    for r in range(GROUP):
        part = jnp.bitwise_xor(me, r)
        for cell, place in ((0, place0), (1, place1)):
            raw = raw_ref[r, cell * PADDED : (cell + 1) * PADDED, :][:ROWS]
            lanes = slice(cell * NODES, (cell + 1) * NODES)
            proj_ref[part, :, lanes] = dot(place, raw).astype(BF16)
    for part in range(GROUP):
        local_ref[part] = dot_tn(scaled[part], proj_ref[part])
    finish(hams)
    add_local(me, v_ref, held_ref, local_ref)
    add_faces(place_ref, got_ref, near_ref, scaled, local_ref)
    gain, _ = factors[0]
    new = []
    for part in range(GROUP):
        new.append(((local_ref[part] - CENTER * v_ref[part].astype(F32)) * gain).astype(BF16))
        next_ref[part] = new[part]
    write_message(me, new, held_ref, proj_ref, edge_ref, wide_ref, message_ref)


def step_kernel(degree, factors, place_ref, got_ref, *refs):
    last = degree == DEGREE - 1
    v_ref, old_ref, held_ref, proj_ref, near_ref, pick_ref, factor_ref = refs[:7]
    refs = refs[7:]
    if last:
        occ_ref, density_ref, *next_refs = refs[: 2 + GROUP]
        refs = refs[2 + GROUP :]
    else:
        next_ref, message_ref = refs[:2]
        refs = refs[2:]
    local_ref, edge_ref, wide_ref, scaled_ref = refs
    me = place_ref[0]
    scaled = sum_coefs(got_ref, pick_ref, factor_ref, scaled_ref)
    for part in range(GROUP):
        local_ref[part] = dot_tn(scaled[part], proj_ref[part])
    add_local(me, v_ref, held_ref, local_ref)
    add_faces(place_ref, got_ref, near_ref, scaled, local_ref)

    gain, back = factors[degree]

    def image(part):
        now = v_ref[part].astype(F32)
        value = (local_ref[part] - CENTER * now) * gain - back * old_ref[part].astype(F32)
        return value.astype(BF16)

    if not last:
        new = [image(part) for part in range(GROUP)]
        for part in range(GROUP):
            next_ref[part] = new[part]
        write_message(me, new, held_ref, proj_ref, edge_ref, wide_ref, message_ref)
        return
    weight = jnp.transpose(jnp.broadcast_to(pick(occ_ref[...], me), (LANES, LANES)))[:PIECE]
    for r in range(GROUP):
        part = jnp.bitwise_xor(me, r)
        new = image(part)
        next_refs[r][...] = new
        values = new.astype(F32)
        for k in range(PART // LANES):
            term = values[:, tile(k)]
            sums = jnp.sum(term * term * weight, axis=0, keepdims=True)
            density_ref[part, 2 * k : 2 * k + 1, :] = sums[:, :FACE]
            density_ref[part, 2 * k + 1 : 2 * k + 2, :] = sums[:, FACE:]


def join_kernel(place_ref, *refs):
    ins, (out_ref, sems) = refs[:GROUP], refs[GROUP:]
    copies = []
    for r in range(GROUP):
        start = pl.multiple_of(jnp.bitwise_xor(place_ref[0], r) * PIECE, 16)
        copies.append(
            pltpu.make_async_copy(ins[GROUP - 1 - r], out_ref.at[pl.ds(start, PIECE), :], sems.at[r])
        )
    run(copies)
    finish(copies)


def vmem():
    return pl.BlockSpec(memory_space=pltpu.VMEM)


def hbm():
    return pl.BlockSpec(memory_space=pltpu.HBM)


def smem():
    return pl.BlockSpec(memory_space=pltpu.SMEM)


def shape(dims, dtype=BF16):
    return jax.ShapeDtypeStruct(dims, dtype)


def shards(interpret, states, cell_ham, projectors, slot_atom, coupling, occupancy):
    width = states.shape[1]
    groups = lax.axis_size("z")
    spread = lax.axis_size("x") * lax.axis_size("yh")
    dma = pltpu.SemaphoreType.DMA
    near = ("yl", "c")
    ring = 2 * lax.axis_size("yh")

    def call(kernel, megabytes=24, **kw):
        params = pltpu.CompilerParams(vmem_limit_bytes=megabytes * 1024 * 1024)
        return pl.pallas_call(kernel, compiler_params=params, interpret=interpret, **kw)

    me = 2 * lax.axis_index("yl") + lax.axis_index("c")
    place = jnp.stack([me, lax.axis_index("z")]).astype(jnp.int32)
    occ = jnp.pad(occupancy.reshape(GROUP, PIECE), ((0, 0), (0, LANES - PIECE)))
    v_t = states.T
    opened, pack = call(
        open_kernel,
        megabytes=60,
        out_shape=[shape((GROUP, HEAD + PIECE, PART)), shape((PACK, NODES))],
        in_specs=[smem()] + [hbm()] * 3,
        out_specs=[vmem()] * 2,
        scratch_shapes=[
            pltpu.VMEM((width, PART), BF16),
            pltpu.VMEM((2, LANES, NODES), BF16),
            pltpu.VMEM((2, ROWS, NODES), BF16),
            pltpu.VMEM((GROUP, HEAD, PART), F32),
            dma((6,)),
        ],
    )(slot_atom, v_t, cell_ham, projectors)
    opened = lax.all_to_all(opened, near, 0, 0)
    message = call(
        pack_kernel,
        out_shape=shape((BODY + 8, PART)),
        in_specs=[vmem()],
        out_specs=vmem(),
        scratch_shapes=[pltpu.VMEM((BODY + 8, PART), F32)],
    )(opened)
    spot = lambda y, core: ((y % 2) * 2 + core) * (ring // 2) + y // 2

    def across(flip):
        return [
            (spot(y, c), spot((y + 1 - 2 * c) % ring, c ^ flip)) for y in range(ring) for c in (0, 1)
        ]

    axes = ("yl", "c", "yh")
    packs = [
        pack,
        lax.ppermute(pack, axes, across(0)),
        lax.ppermute(pack, axes, across(1)),
        lax.ppermute(pack, "c", [(0, 1), (1, 0)]),
    ]

    factors = chebyshev_factors()
    state_shape = shape((GROUP, PIECE, PART))
    message_shape = shape((BODY, PART))
    scratch = [
        pltpu.VMEM((GROUP, PIECE, PART), F32),
        pltpu.VMEM((LANES, PART), BF16),
        pltpu.VMEM((BODY, PART), F32),
        pltpu.VMEM((GROUP + 2, PROJ, PIECE), F32),
    ]
    got = lax.all_gather(message, "z", axis=1, tiled=True)
    v, message, old, *kept = call(
        functools.partial(first_kernel, factors),
        out_shape=[
            state_shape,
            message_shape,
            state_shape,
            shape((2 * GROUP, NODES, NODES)),
            shape((GROUP, PROJ, PART)),
            shape((2, PROJ, LANES)),
            shape((PIECE, -(-groups * BODY // LANES) * LANES)),
            shape((PIECE, WIDE), F32),
        ],
        in_specs=[smem()] + [vmem()] * 2 + [hbm()] * (GROUP + 1),
        out_specs=[vmem()] * 8,
        scratch_shapes=scratch
        + [pltpu.VMEM((GROUP, 2 * PADDED, NODES), BF16), dma((4 * GROUP,))],
    )(place, coupling, got, opened, *packs)
    for degree in range(1, DEGREE):
        got = lax.all_gather(message, "z", axis=1, tiled=True)
        last = degree == DEGREE - 1
        outs = [state_shape, message_shape]
        if last:
            outs = [shape((GROUP, PART // FACE, FACE), F32)] + [shape((PIECE, PART))] * GROUP
        ends = [occ] if last else []
        result = call(
            functools.partial(step_kernel, degree, factors),
            out_shape=outs,
            in_specs=[smem()] + [vmem()] * (8 + len(ends)),
            out_specs=[vmem()] * len(outs),
            scratch_shapes=scratch,
        )(place, got, v, old, *kept, *ends)
        old, v, message = v, result[0], result[1]

    density, *pieces = result
    for r in (3, 2, 1):
        pieces[r] = lax.ppermute(pieces[r], near, [(k, k ^ r) for k in range(GROUP)])
    filtered = call(
        join_kernel,
        out_shape=shape((width, PART)),
        in_specs=[smem()] + [hbm()] * GROUP,
        out_specs=hbm(),
        scratch_shapes=[dma((GROUP,))],
    )(place, *pieces[::-1])
    parts = GROUP * spread
    terms = lax.all_to_all(
        density.reshape(parts, GROUP * PART // parts), near + ("x", "yh"), 0, 0, tiled=True
    )
    density = jnp.sum(terms, axis=0) / (width * spread)
    return filtered.T, density


def build(mesh, interpret=False):
    part = ("z", "yl", "c")
    group = ("x", "yh")
    return jax.shard_map(
        functools.partial(shards, interpret),
        mesh=mesh,
        in_specs=(
            P(part, group),
            P(part, None, None),
            P(part, None, None),
            P(part, None),
            P(),
            P(group),
        ),
        out_specs=(P(part, group), P(part + group)),
        check_vma=False,
    )


def solution(mesh):
    count, groups = mesh.shape["mesh"], mesh.shape["state"]
    devices = mesh.devices.reshape(count // GROUP, 2, 2, groups // 4, 4)
    return build(Mesh(devices, ("z", "yl", "c", "x", "yh")))
```

```python
import functools

import jax
import jax.numpy as jnp
from jax import lax
from jax.experimental import pallas as pl
from jax.experimental.pallas import tpu as pltpu
from jax.sharding import Mesh, PartitionSpec as P

FACE = 64
DEGREE = 4
LANES = 128
NODES = 512
NPROJ = 18
SLOTS = 4
ROWS = SLOTS * NPROJ
GROUP = 4
PART = 2 * NODES
PIECE = 48
BLOCKS = 8
PROJ = NPROJ * BLOCKS
SPAN = NPROJ * PIECE
WIDE = 7 * LANES
BODY = GROUP * BLOCKS
PADDED = 80
PACK = PART + 2 * PADDED
HEAD = 32
CENTER = 0.5
HALF_WIDTH = 1.5
LOW_EDGE = -1.2

BF16 = jnp.bfloat16
F32 = jnp.float32
NT = (((1,), (1,)), ((), ()))
TN = (((0,), (0,)), ((), ()))


def chebyshev_factors():
    sigma = HALF_WIDTH / (LOW_EDGE - CENTER)
    gamma = 2.0 / sigma
    factors = [(sigma / HALF_WIDTH, 0.0)]
    for _ in range(1, DEGREE):
        sigma_new = 1.0 / (gamma - sigma)
        factors.append((2.0 * sigma_new / HALF_WIDTH, sigma * sigma_new))
        sigma = sigma_new
    return factors


def iota(shape, dim):
    return lax.broadcasted_iota(jnp.int32, shape, dim)


def dot(a, b):
    return jnp.dot(a, b, preferred_element_type=F32)


def dot_nt(a, b):
    return lax.dot_general(a, b, NT, preferred_element_type=F32)


def dot_tn(a, b):
    return lax.dot_general(a, b, TN, preferred_element_type=F32)


def exact(a, b):
    return jnp.dot(a, b, precision=lax.Precision.HIGHEST, preferred_element_type=F32)


def placers():
    row = iota((PROJ, ROWS), 0)
    col = iota((PROJ, ROWS), 1)
    which = row // BLOCKS
    block = row % BLOCKS
    first = (block < SLOTS) & (col == block * NPROJ + which)
    slot = block - SLOTS + 1
    second = ((block == 0) & (col == which)) | (
        (block >= SLOTS) & (block < 2 * SLOTS - 1) & (col == slot * NPROJ + which)
    )
    return first.astype(F32).astype(BF16), second.astype(F32).astype(BF16)


def low_lanes(rows):
    return iota((rows, LANES), 1) < FACE


def pick(rows, at):
    return jnp.sum(jnp.where(iota(rows.shape, 0) == at, rows, 0.0), axis=0, keepdims=True)


def run(copies):
    for copy in copies:
        copy.start()
    return copies


def finish(copies):
    for copy in copies:
        copy.wait()


def tile(k):
    return slice(k * LANES, (k + 1) * LANES)


def eight(k):
    return slice(k * 8, (k + 1) * 8)


def open_kernel(
    atom_ref, v_hbm, ham_hbm, proj_hbm, out_ref, pack_ref, v_ref, ham_ref, proj_ref, wide_ref, sems
):
    proj_in, v_in, *edges = run(
        [
            pltpu.make_async_copy(proj_hbm, proj_ref, sems.at[0]),
            pltpu.make_async_copy(v_hbm, v_ref, sems.at[1]),
            pltpu.make_async_copy(ham_hbm.at[0, :LANES, :], ham_ref.at[0], sems.at[2]),
            pltpu.make_async_copy(ham_hbm.at[1, NODES - LANES :, :], ham_ref.at[1], sems.at[3]),
        ]
    )
    hams = run(
        [
            pltpu.make_async_copy(
                ham_hbm.at[k], pack_ref.at[pl.ds(k * NODES, NODES), :], sems.at[4 + k]
            )
            for k in range(2)
        ]
    )
    place0, place1 = placers()
    wide_ref[...] = jnp.zeros(wide_ref.shape, F32)
    lane = iota((8, LANES), 1)
    atoms = jnp.full((8, LANES), -1, jnp.int32)
    for block in range(2 * SLOTS - 1):
        cell, slot = (0, block) if block < SLOTS else (1, block - SLOTS + 1)
        atoms = jnp.where(lane == block, atom_ref[cell, slot], atoms)
    atoms = atoms.astype(F32)
    width = v_ref.shape[0]
    proj_in.wait()
    pad = jnp.zeros((PADDED - ROWS, NODES), BF16)
    for k in range(2):
        start = PART + k * PADDED
        pack_ref[start : start + PADDED, :] = jnp.concatenate([proj_ref[k], pad], axis=0)
    p0 = dot(place0, proj_ref[0]).astype(BF16)
    p1 = dot(place1, proj_ref[1]).astype(BF16)
    v_in.wait()
    v0 = v_ref[:, :NODES]
    v1 = v_ref[:, NODES:]
    coef = dot_nt(p0, v0) + dot_nt(p1, v1)
    finish(edges)
    face = jnp.where(low_lanes(width), dot_nt(v0, ham_ref[0]), dot_nt(v1, ham_ref[1]))
    edge = jnp.where(
        low_lanes(ROWS),
        proj_ref[0, :, :LANES].astype(F32),
        proj_ref[1, :, NODES - LANES :].astype(F32),
    )
    for to in range(GROUP):
        for i in range(NPROJ):
            wide_ref[to, :8, i * PIECE : (i + 1) * PIECE] = coef[
                eight(i), to * PIECE : (to + 1) * PIECE
            ]
        for k in range(PIECE // 8):
            wide_ref[to, 8:16, tile(k)] = face[eight(to * (PIECE // 8) + k)]
        wide_ref[to, 8:16, tile(6)] = atoms
        for k in range(8):
            wide_ref[to, 16:24, tile(k)] = edge[eight(k)]
        wide_ref[to, 24:32, :LANES] = edge[eight(8)]
        out_ref[to, :HEAD, :] = wide_ref[to].astype(BF16)
        out_ref[to, HEAD:, :] = v_ref[to * PIECE : (to + 1) * PIECE, :]
    finish(hams)


def read(got_ref, group, rows, lane, width):
    start = group * PART + lane
    if not isinstance(group, int):
        start = pl.multiple_of(start, LANES)
    return got_ref[:rows, pl.ds(start, width)]


def place_face(face, wide_ref):
    wide_ref[:BODY, WIDE:] = face[:BODY]
    for k in range(PIECE - BODY):
        row = (k % GROUP) * BLOCKS + BLOCKS - 1
        wide_ref[row : row + 1, tile(k // GROUP)] = face[BODY + k : BODY + k + 1]


def read_face(got_ref, group):
    body = read(got_ref, group, BODY, 0, PART).astype(F32)
    rows = [body[:, WIDE:]]
    for k in range(PIECE - BODY):
        row = (k % GROUP) * BLOCKS + BLOCKS - 1
        rows.append(body[row : row + 1, tile(k // GROUP)])
    return jnp.concatenate(rows, axis=0)


def pack_kernel(in_ref, out_ref, wide_ref):
    last = GROUP - 1
    low = low_lanes(8)
    wide_ref[...] = jnp.zeros(wide_ref.shape, F32)
    pieces = [in_ref[part, :HEAD, :].astype(F32) for part in range(GROUP)]
    both = lambda rows, k: jnp.where(low, pieces[0][rows, tile(k)], pieces[last][rows, tile(k)])
    lane = iota((8, LANES), 1)
    atoms = jnp.full((8, LANES), -1.0, F32)
    for part in range(GROUP):
        wide_ref[eight(part), :WIDE] = pieces[part][:8, :WIDE]
        own = pieces[part][8:16, tile(6)]
        if part:
            own = pltpu.roll(own, part * BLOCKS, 1)
        atoms = jnp.where(lane // BLOCKS == part, own, atoms)
    face = jnp.concatenate([both(slice(8, 16), k) for k in range(PIECE // 8)], axis=0)
    place_face(face, wide_ref)
    ninth = both(slice(24, 32), 0)
    for k in range(8):
        wide_ref[BODY:, tile(k)] = both(slice(16, 24), k)
        row = (k % GROUP) * BLOCKS + BLOCKS - 1
        wide_ref[row : row + 1, tile(4 + k // GROUP)] = ninth[k : k + 1]
    wide_ref[BLOCKS - 1 : BLOCKS, tile(6)] = atoms[:1]
    out_ref[...] = wide_ref[...].astype(BF16)


def beside(place_ref, groups):
    z = place_ref[1]
    return z, jnp.maximum(z - 1, 0), jnp.minimum(z + 1, groups - 1)


def choose(place_ref, coupling_ref, got_ref, pick_ref, factor_ref):
    groups = got_ref.shape[1] // PART
    z, below, above = beside(place_ref, groups)
    lane = iota((8, LANES), 1)
    named = lambda group: jnp.broadcast_to(
        read(got_ref, group, 16, 6 * LANES, LANES).astype(F32)[BLOCKS - 1 : BLOCKS], (8, LANES)
    )
    shift = lambda x, by: pltpu.roll(x, by, 1) if by else x
    per = LANES // BODY
    tiles = []
    for start in range(0, groups, per):
        x = jnp.full((8, LANES), -1.0, F32)
        for k in range(min(per, groups - start)):
            x = jnp.where(lane // BODY == k, shift(named(start + k), k * BODY), x)
        tiles.append(x)
    mine = jnp.where(lane < BODY, named(z), -1.0)
    mine = jnp.where(lane // BLOCKS == GROUP, shift(named(below), BLOCKS), mine)
    mine = jnp.where(lane // BLOCKS == GROUP + 1, shift(named(above), BODY + BLOCKS), mine)
    mine = jnp.where(mine < 0, -2.0, mine)
    column = jnp.transpose(jnp.concatenate([mine] * (LANES // 8), axis=0))[:PIECE]
    for k, x in enumerate(tiles):
        match = column == jnp.concatenate([x] * (PIECE // 8), axis=0)
        pick_ref[:, tile(k)] = jnp.where(match, 1.0, 0.0).astype(BF16)
    count = coupling_ref.shape[0]
    atom = iota((PIECE, LANES), 1).astype(F32)
    owner = jnp.where(column == atom, 1.0, 0.0)[:, :count]
    expand = jnp.where(iota((NPROJ, WIDE), 1) // PIECE == iota((NPROJ, WIDE), 0), 1.0, 0.0)
    factor_ref[...] = exact(exact(owner, coupling_ref[...]), expand)


def sum_coefs(got_ref, pick_ref, factor_ref, scaled_ref):
    groups = got_ref.shape[1] // PART
    blocks = jnp.concatenate([read(got_ref, g, BODY, 0, WIDE) for g in range(groups)], axis=0)
    total = dot(pick_ref[:, : groups * BODY], blocks) * factor_ref[...]
    for i in range(NPROJ):
        column = total[:, i * PIECE : (i + 1) * PIECE]
        for k in range(GROUP + 2):
            scaled_ref[k, eight(i), :] = column[eight(k)]
    return [scaled_ref[k].astype(BF16) for k in range(GROUP + 2)]


def add_faces(place_ref, got_ref, near_ref, scaled, local_ref):
    groups = got_ref.shape[1] // PART
    z, below, above = beside(place_ref, groups)
    low = low_lanes(PIECE)
    from_below = read_face(got_ref, below) + dot_tn(scaled[GROUP], near_ref[0])
    from_above = read_face(got_ref, above) + dot_tn(scaled[GROUP + 1], near_ref[1])
    from_below = from_below * (z > 0).astype(F32)
    from_above = from_above * (z < groups - 1).astype(F32)
    cells = [(part, cell * NODES) for part in range(GROUP) for cell in range(2)]
    heads = [local_ref[part, :, a : a + LANES] for part, a in cells]
    tails = [local_ref[part, :, a + NODES - LANES : a + NODES] for part, a in cells]
    for k, (part, a) in enumerate(cells):
        under = tails[k - 1] if k > 0 else from_below
        over = heads[k + 1] if k + 1 < len(cells) else from_above
        local_ref[part, :, a : a + LANES] = heads[k] + jnp.where(
            low, pltpu.roll(under, FACE, 1), 0.0
        )
        local_ref[part, :, a + NODES - LANES : a + NODES] = tails[k] + jnp.where(
            low, 0.0, pltpu.roll(over, FACE, 1)
        )


def fetch_hams(packs, held_ref, sems):
    return run(
        [
            pltpu.make_async_copy(
                packs[k // 2].at[pl.ds((k % 2) * NODES, NODES), :], held_ref.at[k], sems.at[k]
            )
            for k in range(2 * GROUP)
        ]
    )


def add_local(me, v_ref, held_ref, local_ref, hams=()):
    for r in range(GROUP):
        finish(hams[2 * r : 2 * r + 2])
        part = jnp.bitwise_xor(me, r)
        for cell in range(2):
            lanes = slice(cell * NODES, (cell + 1) * NODES)
            local_ref[part, :, lanes] += dot_nt(v_ref[part, :, lanes], held_ref[2 * r + cell])


def write_message(me, new, held_ref, proj_ref, edge_ref, wide_ref, message_ref):
    for r in range(GROUP):
        part = jnp.bitwise_xor(me, r)

        @pl.when(part == 0)
        def _():
            edge_ref[:FACE, :NODES] = held_ref[2 * r, :FACE, :]
            edge_ref[:FACE, NODES:] = jnp.zeros((FACE, NODES), BF16)

        @pl.when(part == GROUP - 1)
        def _():
            edge_ref[FACE:, :NODES] = jnp.zeros((FACE, NODES), BF16)
            edge_ref[FACE:, NODES:] = held_ref[2 * r + 1, NODES - FACE :, :]

    ends = jnp.concatenate([new[0][:, :NODES], new[GROUP - 1][:, NODES:]], axis=1)
    face = dot_nt(ends, edge_ref[...])
    wide_ref[:, SPAN:WIDE] = jnp.zeros((BODY, WIDE - SPAN), F32)
    for part in range(GROUP):
        coef = dot_nt(proj_ref[part], new[part])
        for i in range(NPROJ):
            wide_ref[eight(part), i * PIECE : (i + 1) * PIECE] = coef[eight(i)]
    place_face(face, wide_ref)
    message_ref[...] = wide_ref[...].astype(BF16)


def first_kernel(factors, place_ref, coupling_ref, got_ref, open_hbm, *refs):
    packs, refs = (refs[0], refs[3], refs[1], refs[2]), refs[GROUP:]
    next_ref, message_ref, v_ref, held_ref, proj_ref, near_ref, pick_ref, factor_ref = refs[:8]
    local_ref, edge_ref, wide_ref, scaled_ref, raw_ref, sems = refs[8:]
    groups = got_ref.shape[1] // PART
    me = place_ref[0]
    _, below, above = beside(place_ref, groups)
    copies = []
    for r in range(GROUP):
        at = 2 * GROUP + 2 * r
        copies += [
            pltpu.make_async_copy(packs[r].at[pl.ds(PART, 2 * PADDED), :], raw_ref.at[r], sems.at[at]),
            pltpu.make_async_copy(
                open_hbm.at[r, pl.ds(HEAD, PIECE), :], v_ref.at[r], sems.at[at + 1]
            ),
        ]
    run(copies)
    hams = fetch_hams(packs, held_ref, sems)

    place0, place1 = placers()
    for k, group, place in ((0, below, place1), (1, above, place0)):
        rows = read(got_ref, group, BODY + 8, 0, PART).astype(F32)
        raw = [rows[BODY:, tile(j)] for j in range(8)]
        for j in range(8):
            row = (j % GROUP) * BLOCKS + BLOCKS - 1
            raw.append(rows[row : row + 1, tile(4 + j // GROUP)])
        near_ref[k] = dot(place, jnp.concatenate(raw, axis=0).astype(BF16)).astype(BF16)
    choose(place_ref, coupling_ref, got_ref, pick_ref, factor_ref)
    scaled = sum_coefs(got_ref, pick_ref, factor_ref, scaled_ref)

    finish(copies)
    for r in range(GROUP):
        part = jnp.bitwise_xor(me, r)
        for cell, place in ((0, place0), (1, place1)):
            raw = raw_ref[r, cell * PADDED : (cell + 1) * PADDED, :][:ROWS]
            lanes = slice(cell * NODES, (cell + 1) * NODES)
            proj_ref[part, :, lanes] = dot(place, raw).astype(BF16)
    for part in range(GROUP):
        local_ref[part] = dot_tn(scaled[part], proj_ref[part])
    add_local(me, v_ref, held_ref, local_ref, hams)
    add_faces(place_ref, got_ref, near_ref, scaled, local_ref)
    gain, _ = factors[0]
    new = []
    for part in range(GROUP):
        new.append(((local_ref[part] - CENTER * v_ref[part].astype(F32)) * gain).astype(BF16))
        next_ref[part] = new[part]
    write_message(me, new, held_ref, proj_ref, edge_ref, wide_ref, message_ref)


def step_kernel(degree, factors, place_ref, got_ref, *refs):
    last = degree == DEGREE - 1
    v_ref, old_ref, held_ref, proj_ref, near_ref, pick_ref, factor_ref = refs[:7]
    refs = refs[7:]
    if last:
        occ_ref, density_ref, *next_refs = refs[: 2 + GROUP]
        refs = refs[2 + GROUP :]
    else:
        next_ref, message_ref = refs[:2]
        refs = refs[2:]
    local_ref, edge_ref, wide_ref, scaled_ref = refs
    me = place_ref[0]
    scaled = sum_coefs(got_ref, pick_ref, factor_ref, scaled_ref)
    for part in range(GROUP):
        local_ref[part] = dot_tn(scaled[part], proj_ref[part])
    add_local(me, v_ref, held_ref, local_ref)
    add_faces(place_ref, got_ref, near_ref, scaled, local_ref)

    gain, back = factors[degree]

    def image(part):
        now = v_ref[part].astype(F32)
        value = (local_ref[part] - CENTER * now) * gain - back * old_ref[part].astype(F32)
        return value.astype(BF16)

    if not last:
        new = [image(part) for part in range(GROUP)]
        for part in range(GROUP):
            next_ref[part] = new[part]
        write_message(me, new, held_ref, proj_ref, edge_ref, wide_ref, message_ref)
        return
    weight = jnp.transpose(jnp.broadcast_to(pick(occ_ref[...], me), (LANES, LANES)))[:PIECE]
    for r in range(GROUP):
        part = jnp.bitwise_xor(me, r)
        new = image(part)
        next_refs[r][...] = new
        values = new.astype(F32)
        for k in range(PART // LANES):
            term = values[:, tile(k)]
            sums = jnp.sum(term * term * weight, axis=0, keepdims=True)
            density_ref[part, 2 * k : 2 * k + 1, :] = sums[:, :FACE]
            density_ref[part, 2 * k + 1 : 2 * k + 2, :] = sums[:, FACE:]


def join_kernel(place_ref, *refs):
    ins, (out_ref, sems) = refs[:GROUP], refs[GROUP:]
    copies = []
    for r in range(GROUP):
        start = pl.multiple_of(jnp.bitwise_xor(place_ref[0], r) * PIECE, 16)
        copies.append(
            pltpu.make_async_copy(ins[GROUP - 1 - r], out_ref.at[pl.ds(start, PIECE), :], sems.at[r])
        )
    run(copies)
    finish(copies)


def vmem():
    return pl.BlockSpec(memory_space=pltpu.VMEM)


def hbm():
    return pl.BlockSpec(memory_space=pltpu.HBM)


def smem():
    return pl.BlockSpec(memory_space=pltpu.SMEM)


def shape(dims, dtype=BF16):
    return jax.ShapeDtypeStruct(dims, dtype)


def shards(interpret, states, cell_ham, projectors, slot_atom, coupling, occupancy):
    width = states.shape[1]
    groups = lax.axis_size("z")
    spread = lax.axis_size("x") * lax.axis_size("yh")
    dma = pltpu.SemaphoreType.DMA
    near = ("yl", "c")
    ring = 2 * lax.axis_size("yh")

    def call(kernel, megabytes=24, **kw):
        params = pltpu.CompilerParams(vmem_limit_bytes=megabytes * 1024 * 1024)
        return pl.pallas_call(kernel, compiler_params=params, interpret=interpret, **kw)

    me = 2 * lax.axis_index("yl") + lax.axis_index("c")
    place = jnp.stack([me, lax.axis_index("z")]).astype(jnp.int32)
    occ = jnp.pad(occupancy.reshape(GROUP, PIECE), ((0, 0), (0, LANES - PIECE)))
    v_t = states.T
    opened, pack = call(
        open_kernel,
        megabytes=60,
        out_shape=[shape((GROUP, HEAD + PIECE, PART)), shape((PACK, NODES))],
        in_specs=[smem()] + [hbm()] * 3,
        out_specs=[vmem()] * 2,
        scratch_shapes=[
            pltpu.VMEM((width, PART), BF16),
            pltpu.VMEM((2, LANES, NODES), BF16),
            pltpu.VMEM((2, ROWS, NODES), BF16),
            pltpu.VMEM((GROUP, HEAD, PART), F32),
            dma((6,)),
        ],
    )(slot_atom, v_t, cell_ham, projectors)
    opened = lax.all_to_all(opened, near, 0, 0)
    message = call(
        pack_kernel,
        out_shape=shape((BODY + 8, PART)),
        in_specs=[vmem()],
        out_specs=vmem(),
        scratch_shapes=[pltpu.VMEM((BODY + 8, PART), F32)],
    )(opened)
    spot = lambda y, core: ((y % 2) * 2 + core) * (ring // 2) + y // 2

    def across(flip):
        return [
            (spot(y, c), spot((y + 1 - 2 * c) % ring, c ^ flip)) for y in range(ring) for c in (0, 1)
        ]

    axes = ("yl", "c", "yh")
    packs = [
        pack,
        lax.ppermute(pack, axes, across(0)),
        lax.ppermute(pack, axes, across(1)),
        lax.ppermute(pack, "c", [(0, 1), (1, 0)]),
    ]

    factors = chebyshev_factors()
    state_shape = shape((GROUP, PIECE, PART))
    message_shape = shape((BODY, PART))
    scratch = [
        pltpu.VMEM((GROUP, PIECE, PART), F32),
        pltpu.VMEM((LANES, PART), BF16),
        pltpu.VMEM((BODY, PART), F32),
        pltpu.VMEM((GROUP + 2, PROJ, PIECE), F32),
    ]
    got = lax.all_gather(message, "z", axis=1, tiled=True)
    v, message, old, *kept = call(
        functools.partial(first_kernel, factors),
        out_shape=[
            state_shape,
            message_shape,
            state_shape,
            shape((2 * GROUP, NODES, NODES)),
            shape((GROUP, PROJ, PART)),
            shape((2, PROJ, LANES)),
            shape((PIECE, -(-groups * BODY // LANES) * LANES)),
            shape((PIECE, WIDE), F32),
        ],
        in_specs=[smem()] + [vmem()] * 2 + [hbm()] * (GROUP + 1),
        out_specs=[vmem()] * 8,
        scratch_shapes=scratch
        + [pltpu.VMEM((GROUP, 2 * PADDED, NODES), BF16), dma((4 * GROUP,))],
    )(place, coupling, got, opened, *packs)
    for degree in range(1, DEGREE):
        got = lax.all_gather(message, "z", axis=1, tiled=True)
        last = degree == DEGREE - 1
        outs = [state_shape, message_shape]
        if last:
            outs = [shape((GROUP, PART // FACE, FACE), F32)] + [shape((PIECE, PART))] * GROUP
        ends = [occ] if last else []
        result = call(
            functools.partial(step_kernel, degree, factors),
            out_shape=outs,
            in_specs=[smem()] + [vmem()] * (8 + len(ends)),
            out_specs=[vmem()] * len(outs),
            scratch_shapes=scratch,
        )(place, got, v, old, *kept, *ends)
        old, v, message = v, result[0], result[1]

    density, *pieces = result
    for r in (3, 2, 1):
        pieces[r] = lax.ppermute(pieces[r], near, [(k, k ^ r) for k in range(GROUP)])
    filtered = call(
        join_kernel,
        out_shape=shape((width, PART)),
        in_specs=[smem()] + [hbm()] * GROUP,
        out_specs=hbm(),
        scratch_shapes=[dma((GROUP,))],
    )(place, *pieces[::-1])
    parts = GROUP * spread
    terms = lax.all_to_all(
        density.reshape(parts, GROUP * PART // parts), near + ("x", "yh"), 0, 0, tiled=True
    )
    density = jnp.sum(terms, axis=0) / (width * spread)
    return filtered.T, density


def build(mesh, interpret=False):
    part = ("z", "yl", "c")
    group = ("x", "yh")
    return jax.shard_map(
        functools.partial(shards, interpret),
        mesh=mesh,
        in_specs=(
            P(part, group),
            P(part, None, None),
            P(part, None, None),
            P(part, None),
            P(),
            P(group),
        ),
        out_specs=(P(part, group), P(part + group)),
        check_vma=False,
    )


def solution(mesh):
    count, groups = mesh.shape["mesh"], mesh.shape["state"]
    devices = mesh.devices.reshape(count // GROUP, 2, 2, groups // 4, 4)
    return build(Mesh(devices, ("z", "yl", "c", "x", "yh")))
```
